32 devices in a mesh: fsdp: 4 (over y, x), dp: 8 (over z, core).
Axes of the slice: x: 2, y: 2, z: 4, core: 2. Of those that a mesh axis runs over, the one named last changes fastest.
Arguments:
- tokens: bfloat16 [10240, 2048], P(('fsdp', 'dp')), may hold values from -6 to 6
- summaries: bfloat16 [32, 50, 2048], P(('fsdp', 'dp')), may hold values from -6 to 6
- presence: int32 [32, 50], P(('fsdp', 'dp')), may hold values 0 or 1
- seg_counts: int32 [8], replicated, may hold values from 1 to 8, 32 in all
- ln1_gain: bfloat16 [2048], P(('fsdp', 'dp')), may hold values from 0.5 to 1.5
- ln1_bias: bfloat16 [2048], P(('fsdp', 'dp')), may hold values from -1.1953125 to 1.1953125
- w_query: bfloat16 [2048, 2048], P(('fsdp', 'dp')), may hold values from -0.125 to 0.125
- query_bias: bfloat16 [2048], P(('fsdp', 'dp')), may hold values from -1.796875 to 1.796875
- w_key: bfloat16 [2048, 2048], P(('fsdp', 'dp')), may hold values from -0.125 to 0.125
- w_value: bfloat16 [2048, 2048], P(('fsdp', 'dp')), may hold values from -0.125 to 0.125
- value_bias: bfloat16 [2048], P(('fsdp', 'dp')), may hold values from -1.796875 to 1.796875
- w_out: bfloat16 [2048, 2048], P(('fsdp', 'dp')), may hold values from -0.375 to 0.375
- out_bias: bfloat16 [2048], P(('fsdp', 'dp')), may hold values from -1.796875 to 1.796875
- ln2_gain: bfloat16 [2048], P(('fsdp', 'dp')), may hold values from 0.5 to 1.5
- ln2_bias: bfloat16 [2048], P(('fsdp', 'dp')), may hold values from -1.1953125 to 1.1953125
- w_up: bfloat16 [2048, 8192], P(('fsdp', 'dp')), may hold values from -0.125 to 0.125
- up_bias: bfloat16 [8192], P(('fsdp', 'dp')), may hold values from -1.796875 to 1.796875
- w_down: bfloat16 [8192, 2048], P(('fsdp', 'dp')), may hold values from -0.0625 to 0.0625
- down_bias: bfloat16 [2048], P(('fsdp', 'dp')), may hold values from -1.796875 to 1.796875
- cotangent: bfloat16 [10240, 2048], P(('fsdp', 'dp')), may hold values from -6 to 6
Outputs:
- output: bfloat16 [10240, 2048], P(('fsdp', 'dp'))
- tokens_grad: float32 [10240, 2048], P(('fsdp', 'dp'))
- summaries_grad: float32 [32, 50, 2048], P(('fsdp', 'dp'))
- ln1_gain_grad: float32 [2048], P(('fsdp', 'dp'))
- ln1_bias_grad: float32 [2048], P(('fsdp', 'dp'))
- w_query_grad: float32 [2048, 2048], P(('fsdp', 'dp'))
- query_bias_grad: float32 [2048], P(('fsdp', 'dp'))
- w_key_grad: float32 [2048, 2048], P(('fsdp', 'dp'))
- w_value_grad: float32 [2048, 2048], P(('fsdp', 'dp'))
- value_bias_grad: float32 [2048], P(('fsdp', 'dp'))
- w_out_grad: float32 [2048, 2048], P(('fsdp', 'dp'))
- out_bias_grad: float32 [2048], P(('fsdp', 'dp'))
- ln2_gain_grad: float32 [2048], P(('fsdp', 'dp'))
- ln2_bias_grad: float32 [2048], P(('fsdp', 'dp'))
- w_up_grad: float32 [2048, 8192], P(('fsdp', 'dp'))
- up_bias_grad: float32 [8192], P(('fsdp', 'dp'))
- w_down_grad: float32 [8192, 2048], P(('fsdp', 'dp'))
- down_bias_grad: float32 [2048], P(('fsdp', 'dp'))
The draws below stay inside these ranges and needn't reach their ends.
Inputs may be any that keep to these rules, and one draw needn't show every extreme that they name: `seg_counts`: the counts add up to 32; some item has exactly 8 segments.
All inputs are finite; a program needn't handle non-finite values. No bound on the sum of `presence` on one device may be relied on, other than what follows from the above.
Results may differ from the reference program's by a relative error of at most 0.013.
Values may be sent and summed in bfloat16 or wider, within the bound.
No kernel may reach another device: no remote copies, remote signals or barrier semaphores. Data moves between devices by JAX's collectives and lax.ppermute only.
A program may use at most 448 MiB of HBM per device.

```python
import math
import jax
import jax.numpy as jnp
import numpy as np
from jax import lax

D = 2048
HEADS = 32
FF = 8192
NSUM = 50
SEG = 320
SLOTS = 32
ITEMS = 8
TOKENS = 10240


def set_ends(entries, own_key, least, high):
    place = [jax.random.randint(jax.random.fold_in(own_key, axis), (), 0, length) for axis, length in enumerate(entries.shape)]
    longest = entries.shape.index(max(entries.shape))
    beside = place[:longest] + [(place[longest] + 1) % entries.shape[longest]] + place[longest + 1:]
    return entries.at[tuple(place)].set(least).at[tuple(beside)].set(high)


def shard_levels(own_key, extent, shards, least, high):
    def one(dim, parts):
        steps = jax.random.uniform(jax.random.fold_in(jax.random.fold_in(own_key, 6), dim), (parts,), jnp.float32, least / len(shards), high / len(shards))
        return jnp.repeat(jnp.exp(steps), extent[dim] // parts).reshape((-1,) + (1,) * (len(extent) - dim - 1))

    level = one(*shards[0])
    for cut in shards[1:]:
        level = level * one(*cut)
    return level


def profile(amount, total, reach, skew):
    loads = [(1 << 20) // math.isqrt(standing ** skew) + 1 for standing in range(2, amount + 1)]
    surplus, given = total - reach - (amount - 1), [1] * (amount - 1)
    while surplus > 0:
        candidates = [i for i in range(amount - 1) if given[i] < reach]
        mass, remaining = sum([loads[i] for i in candidates]), surplus
        for i in candidates:
            extra = min(reach - given[i], max(1, remaining * loads[i] // mass), surplus)
            given[i] = given[i] + extra
            surplus = surplus - extra
    return np.array([reach] + given)


def uneven(rng, number_of, total, most, lean):
    if number_of == 2:
        one = jax.random.randint(rng, (), max(1, total - most), min(most, total - 1) + 1)
        return jnp.stack([one, total - one])
    sizes = jnp.asarray(profile(number_of, total, most, lean), jnp.int32)
    couples = (number_of - 1) // 2
    giver, receiver = sizes[1:1 + 2 * couples:2], sizes[2:2 + 2 * couples:2]
    margin = jnp.minimum(giver - 1, most - receiver)
    shifted = jax.random.randint(jax.random.fold_in(rng, 1), (couples,), 0, 1 << 20) % (margin + 1)
    sizes = sizes.at[1:1 + 2 * couples:2].set(giver - shifted).at[2:2 + 2 * couples:2].set(receiver + shifted)
    return sizes[jax.random.permutation(jax.random.fold_in(rng, 2), number_of)]


def normal_values(own_key, dims, width, most, shards=(), held_as=jnp.bfloat16):
    loudness = shard_levels(own_key, dims, shards, -0.22, 0.18) if shards else 1.0
    result = jax.random.normal(own_key, dims, jnp.float32) * width * loudness
    return jnp.minimum(jnp.maximum(result, -most), most).astype(held_as)


def setup_inputs(seed: int = 0) -> dict:
    streams_of = jax.random.split(jax.random.key(seed), 21)
    return {
        "tokens": normal_values(streams_of[0], (TOKENS, D), 1.0, 6.0, ((0, 32),)),
        "summaries": normal_values(streams_of[1], (SLOTS, NSUM, D), 1.0, 6.0, ((0, 32),)),
        "presence": set_ends((jax.random.randint(streams_of[2], (SLOTS, NSUM), 0, 4) < 3).astype(jnp.int32), jax.random.fold_in(streams_of[2], 1), 0, 1),
        "seg_counts": uneven(streams_of[3], ITEMS, SLOTS, 8, 2).astype(jnp.int32),
        "ln1_gain": jnp.clip(1.0 + 0.1 * jax.random.normal(streams_of[4], (D,), jnp.float32), 0.5, 1.5).astype(jnp.bfloat16),
        "ln1_bias": normal_values(streams_of[5], (D,), 0.2, 1.1953125, ((0, 32),)),
        "w_query": normal_values(streams_of[6], (D, D), D ** -0.5, 0.125, ((0, 32),)),
        "query_bias": normal_values(streams_of[7], (D,), 0.3, 1.796875, ((0, 32),)),
        "w_key": normal_values(streams_of[8], (D, D), D ** -0.5, 0.125, ((0, 32),)),
        "w_value": normal_values(streams_of[9], (D, D), D ** -0.5, 0.125, ((0, 32),)),
        "value_bias": normal_values(streams_of[10], (D,), 0.3, 1.796875, ((0, 32),)),
        "w_out": normal_values(streams_of[11], (D, D), (D // 8) ** -0.5, 0.375, ((0, 32),)),
        "out_bias": normal_values(streams_of[12], (D,), 0.3, 1.796875, ((0, 32),)),
        "ln2_gain": jnp.clip(1.0 + 0.1 * jax.random.normal(streams_of[13], (D,), jnp.float32), 0.5, 1.5).astype(jnp.bfloat16),
        "ln2_bias": normal_values(streams_of[14], (D,), 0.2, 1.1953125, ((0, 32),)),
        "w_up": normal_values(streams_of[15], (D, FF), D ** -0.5, 0.125, ((0, 32),)),
        "up_bias": normal_values(streams_of[16], (FF,), 0.3, 1.796875, ((0, 32),)),
        "w_down": normal_values(streams_of[17], (FF, D), FF ** -0.5, 0.0625, ((0, 32),)),
        "down_bias": normal_values(streams_of[18], (D,), 0.3, 1.796875, ((0, 32),)),
        "cotangent": normal_values(streams_of[19], (TOKENS, D), 1.0, 6.0, ((0, 32),)),
    }


@jax.custom_vjp
def low(v):
    return lax.optimization_barrier(v.astype(jnp.bfloat16)).astype(jnp.float32)

@jax.custom_vjp
def low_back(v):
    return v

def low_keep(v):
    return (low(v), None)

def low_pass(kept, grad):
    return (grad,)

def back_keep(v):
    return (v, None)

def back_low(kept, grad):
    return (low(grad),)
low.defvjp(low_keep, low_pass)
low_back.defvjp(back_keep, back_low)

def layer_norm(values, norm_gain, norm_bias):
    centre = values - lax.optimization_barrier(jnp.mean(values, axis=-1, keepdims=True))
    spread = lax.optimization_barrier(jnp.mean(centre * centre, axis=-1, keepdims=True))
    return centre * lax.rsqrt(spread + 1e-05) * norm_gain + norm_bias

def hdot(left, right):
    return jnp.dot(left, right, precision=lax.Precision.HIGHEST)

def reference(tokens, summaries, presence, seg_counts, ln1_gain, ln1_bias, w_query, query_bias, w_key, w_value, value_bias, w_out, out_bias, ln2_gain, ln2_bias, w_up, up_bias, w_down, down_bias, cotangent):
    starts = (jnp.cumsum(seg_counts) - seg_counts).astype(jnp.int32)
    slot_ids = jnp.arange(SLOTS, dtype=jnp.int32)
    has_prev = jnp.logical_not(jnp.any(slot_ids[:, None] == starts[None, :], axis=1))
    head_size = D // HEADS
    score_scale = head_size ** (-0.5)
    row_ids = jnp.arange(SEG, dtype=jnp.int32)[:, None]
    col_ids = jnp.arange(NSUM + SEG, dtype=jnp.int32)[None, :]
    causal = col_ids - NSUM <= row_ids

    def forward(token_vals, summary_vals, gain_first, bias_first, query_mat, query_off, key_mat, value_mat, value_off, out_mat, out_off, gain_second, bias_second, up_mat, up_off, down_mat, down_off):
        previous = jnp.concatenate([jnp.zeros((1, NSUM, D), jnp.float32), summary_vals[:-1]], 0)

        def segment(seg_tokens, seg_prior, present, prev_flag):
            normed = low(layer_norm(seg_tokens, gain_first, bias_first))
            prior_normed = low(layer_norm(seg_prior, gain_first, bias_first))
            joined = jnp.concatenate([prior_normed, normed], 0)
            queries = low_back(low(hdot(normed, query_mat) + query_off)).reshape(SEG, HEADS, head_size)
            key_rows = low_back(low(hdot(joined, key_mat))).reshape(NSUM + SEG, HEADS, head_size)
            value_rows = low_back(low(hdot(joined, value_mat) + value_off)).reshape(NSUM + SEG, HEADS, head_size)
            scores = jnp.einsum('qhd,khd->hqk', queries, key_rows, precision=lax.Precision.HIGHEST) * score_scale
            scores = low_back(scores)
            summary_ok = jnp.concatenate([jnp.logical_and(present == 1, prev_flag), jnp.ones((SEG,), dtype=jnp.bool_)])
            allowed = jnp.logical_and(summary_ok[None, :], causal)
            masked = jnp.where(allowed[None], scores, -1e+30)
            row_max = lax.optimization_barrier(jnp.max(masked, axis=-1, keepdims=True))
            expo_vals = jnp.exp(masked - row_max)
            probs = low(expo_vals / lax.optimization_barrier(jnp.sum(expo_vals, axis=-1, keepdims=True)))
            mixed = jnp.einsum('hqk,khd->qhd', probs, value_rows, precision=lax.Precision.HIGHEST).reshape(SEG, D)
            mixed = low_back(low(mixed))
            middle = seg_tokens + low_back(hdot(mixed, out_mat) + out_off)
            second = low(layer_norm(middle, gain_second, bias_second))
            hidden_pre = low_back(hdot(second, up_mat) + up_off)
            hidden = low(jax.nn.gelu(hidden_pre))
            return middle + hdot(hidden, down_mat) + down_off
        seg_block = jax.checkpoint(segment)

        def scan_step(state_acc, inputs_now):
            return (state_acc, seg_block(inputs_now[0], inputs_now[1], inputs_now[2], inputs_now[3]))
        _, seg_outs = lax.scan(scan_step, jnp.zeros((), jnp.float32), (token_vals.reshape(SLOTS, SEG, D), previous, presence, has_prev))
        return seg_outs.reshape(TOKENS, D)
    params = (ln1_gain, ln1_bias, w_query, query_bias, w_key, w_value, value_bias, w_out, out_bias, ln2_gain, ln2_bias, w_up, up_bias, w_down, down_bias)
    params = [piece.astype(jnp.float32) for piece in params]
    output, backward = jax.vjp(forward, tokens.astype(jnp.float32), summaries.astype(jnp.float32), *params)
    grads = backward(cotangent.astype(jnp.float32))
    return (output.astype(jnp.bfloat16), grads[0], grads[1], grads[2], grads[3], grads[4], grads[5], grads[6], grads[7], grads[8], grads[9], grads[10], grads[11], grads[12], grads[13], grads[14], grads[15], grads[16])
```

```python
import jax
import jax.numpy as jnp
from jax import lax
from jax.sharding import PartitionSpec as P

HEADS = 32
BOTH = ("fsdp", "dp")
PRIOR_ROWS = 64


def norm_parts(values):
    centre = values - jnp.mean(values, axis=-1, keepdims=True)
    spread = jnp.mean(centre * centre, axis=-1, keepdims=True)
    return centre, lax.rsqrt(spread + 1e-05)


def norm_apply(values, norm_gain, norm_bias):
    centre, inverse = norm_parts(values)
    return centre * inverse * norm_gain + norm_bias


def contract_rows(left, right):
    return lax.dot_general(
        left, right, (((0,), (0,)), ((), ())), preferred_element_type=jnp.float32
    )


def contract_cols(left, right):
    return lax.dot_general(
        left, right, (((1,), (1,)), ((), ())), preferred_element_type=jnp.float32
    )


def dot(left, right):
    return jnp.dot(left, right, preferred_element_type=jnp.float32)


def swap(value, rel):
    if rel == 0:
        return value
    count = lax.axis_size("fsdp")
    return lax.ppermute(value, "fsdp", [(i, i ^ rel) for i in range(count)])


def spread_out(value):
    return [swap(value, rel) for rel in range(lax.axis_size("fsdp"))]


def collect(parts):
    total = parts[0]
    for rel in range(1, len(parts)):
        total = total + swap(parts[rel].astype(jnp.bfloat16), rel).astype(jnp.float32)
    return total


def trade_blocks(blocks):
    count = lax.axis_size("fsdp")
    me = lax.axis_index("fsdp")
    out = blocks
    for rel in range(1, count):
        theirs = lax.dynamic_index_in_dim(blocks, me ^ rel, 0, keepdims=True)
        out = lax.dynamic_update_slice_in_dim(out, swap(theirs, rel), me ^ rel, 0)
    return out


def gather_small(row):
    total = lax.axis_size("fsdp") * lax.axis_size("dp")
    place = lax.axis_index(BOTH)
    step = 1
    while step < total:
        came = lax.ppermute(row, BOTH, [(i, i ^ step) for i in range(total)])
        high = (place & step) != 0
        row = jnp.concatenate([jnp.where(high, came, row), jnp.where(high, row, came)], 0)
        step *= 2
    return row


def scatter_small(rows):
    total = lax.axis_size("fsdp") * lax.axis_size("dp")
    place = lax.axis_index(BOTH)
    step = total // 2
    while step >= 1:
        high = (place & step) != 0
        lower, upper = rows[:step], rows[step:]
        sent = jnp.where(high, lower, upper)
        came = lax.ppermute(sent, BOTH, [(i, i ^ step) for i in range(total)])
        rows = jnp.where(high, upper, lower) + came
        step //= 2
    return rows[0]


def gather_dp(value, axis):
    return lax.all_gather(value, "dp", axis=axis, tiled=True)


def scatter_dp(value, axis):
    return lax.psum_scatter(value, "dp", scatter_dimension=axis, tiled=True)


def shards(
    tokens,
    summaries,
    presence,
    seg_counts,
    ln1_gain,
    ln1_bias,
    w_query,
    query_bias,
    w_key,
    w_value,
    value_bias,
    w_out,
    out_bias,
    ln2_gain,
    ln2_bias,
    w_up,
    up_bias,
    w_down,
    down_bias,
    cotangent,
):
    members = lax.axis_size("fsdp")
    columns = lax.axis_size("dp")
    total = members * columns
    me = lax.axis_index("fsdp")
    place = lax.axis_index(BOTH)
    seg_len, width = tokens.shape
    n_summary = summaries.shape[1]
    head_size = width // HEADS
    score_scale = head_size ** (-0.5)
    my_heads = HEADS // members
    my_cols = width // members
    my_ff = w_up.shape[1] // members
    row_share = w_query.shape[0]
    f32, bf16 = jnp.float32, jnp.bfloat16

    small_parts = (
        ln1_gain, ln1_bias, query_bias, value_bias, out_bias, ln2_gain, ln2_bias, up_bias,
        down_bias, presence[0].astype(bf16),
    )
    packed = gather_small(jnp.concatenate(small_parts)[None])
    smalls = []
    at = 0
    for part in small_parts:
        smalls.append(packed[:, at : at + part.shape[0]].astype(f32))
        at += part.shape[0]
    gain_one, bias_one, query_off, value_off, out_off, gain_two, bias_two, up_off, down_off = [
        part.reshape(-1) for part in smalls[:-1]
    ]
    present_all = smalls[-1]
    query_off = lax.dynamic_slice_in_dim(query_off, me * my_cols, my_cols)
    value_off = lax.dynamic_slice_in_dim(value_off, me * my_cols, my_cols)
    up_off = lax.dynamic_slice_in_dim(up_off, me * my_ff, my_ff)

    def blocks_of(weight):
        return weight.reshape(row_share, members, -1).swapaxes(0, 1)

    qkv_blocks = jnp.concatenate([blocks_of(w_query), blocks_of(w_key), blocks_of(w_value)], 2)
    qkv_mat = gather_dp(trade_blocks(qkv_blocks), 1).reshape(width, 3 * my_cols)
    out_mat = gather_dp(w_out, 0)
    up_mat = gather_dp(trade_blocks(blocks_of(w_up)), 1).reshape(width, my_ff)
    down_mat = gather_dp(w_down, 0)

    prior_own = jnp.pad(summaries[0], ((0, PRIOR_ROWS - n_summary), (0, 0)))
    group_tokens = jnp.concatenate(spread_out(tokens), 0)
    priors = []
    for rel in range(members):
        pairs = [((((i // columns) ^ rel) * columns + i % columns) - 1, i) for i in range(total)]
        priors.append(lax.ppermute(prior_own, BOTH, [pair for pair in pairs if pair[0] >= 0]))
    group_prior = jnp.concatenate(priors, 0)
    group_cot = jnp.concatenate(spread_out(cotangent), 0)

    starts = jnp.cumsum(seg_counts) - seg_counts
    group_places = (me ^ jnp.arange(members)) * columns + lax.axis_index("dp")
    has_prev = jnp.all(group_places[:, None] != starts[None, :], axis=1)
    presence_ok = present_all[group_places] == 1
    summary_ok = jnp.logical_and(presence_ok, has_prev[:, None])
    summary_ok = jnp.pad(summary_ok, ((0, 0), (0, PRIOR_ROWS - n_summary)))

    token_low = norm_apply(group_tokens.astype(f32), gain_one, bias_one).astype(bf16)
    prior_low = norm_apply(group_prior.astype(f32), gain_one, bias_one).astype(bf16)
    qkv_off = jnp.concatenate([query_off, jnp.zeros_like(query_off), value_off])
    qkv = (dot(token_low, qkv_mat) + qkv_off).astype(bf16)
    prior_kv = (dot(prior_low, qkv_mat[:, my_cols:]) + qkv_off[my_cols:]).astype(bf16)

    def heads_of(value, rows):
        return value.reshape(members, rows, my_heads, head_size)

    query_heads = heads_of(qkv[:, :my_cols], seg_len)
    key_heads = jnp.concatenate(
        [
            heads_of(qkv[:, my_cols : 2 * my_cols], seg_len),
            heads_of(prior_kv[:, :my_cols], PRIOR_ROWS),
        ],
        1,
    )
    value_heads = jnp.concatenate(
        [heads_of(qkv[:, 2 * my_cols :], seg_len), heads_of(prior_kv[:, my_cols:], PRIOR_ROWS)], 1
    )
    causal = jnp.arange(seg_len)[None, :] <= jnp.arange(seg_len)[:, None]
    allowed = jnp.concatenate(
        [
            jnp.broadcast_to(causal[None], (members, seg_len, seg_len)),
            jnp.broadcast_to(summary_ok[:, None, :], (members, seg_len, PRIOR_ROWS)),
        ],
        2,
    )[:, None]

    def masked_scores():
        scores = jnp.einsum("sqhd,skhd->shqk", query_heads, key_heads, preferred_element_type=f32)
        return jnp.where(allowed, scores * score_scale, -1e30)

    masked = masked_scores()
    row_max = jnp.max(masked, axis=-1, keepdims=True)
    expo_vals = jnp.exp(masked - row_max)
    row_total = jnp.sum(expo_vals, axis=-1, keepdims=True)
    log_total = row_max + jnp.log(row_total)
    probs_low = (expo_vals / row_total).astype(bf16)
    mixed_low = (
        jnp.einsum("shqk,skhd->sqhd", probs_low, value_heads, preferred_element_type=f32)
        .reshape(members * seg_len, my_cols)
        .astype(bf16)
    )

    def by_member(value):
        rows = value.shape[0] // members
        return [value[rel * rows : (rel + 1) * rows] for rel in range(members)]

    token_vals = tokens.astype(f32)
    middle = token_vals + collect(by_member(dot(mixed_low, out_mat))) + out_off
    second_own = norm_apply(middle, gain_two, bias_two).astype(bf16)
    second_low = jnp.concatenate(spread_out(second_own), 0)
    hidden_pre = dot(second_low, up_mat) + up_off
    hidden_low = jax.nn.gelu(hidden_pre).astype(bf16)
    output = (middle + collect(by_member(dot(hidden_low, down_mat))) + down_off).astype(bf16)

    cot_vals = cotangent.astype(f32)
    down_off_grad = jnp.sum(cot_vals, axis=0)
    hidden_grad = contract_cols(group_cot, down_mat)
    _, gelu_back = jax.vjp(jax.nn.gelu, hidden_pre)
    pre_low = gelu_back(hidden_grad)[0].astype(bf16)
    up_off_grad = jnp.sum(pre_low.astype(f32), axis=0)
    second_grad = collect(by_member(contract_cols(pre_low, up_mat)))
    _, second_back = jax.vjp(norm_apply, middle, gain_two, bias_two)
    middle_part, gain_two_grad, bias_two_grad = second_back(second_grad)
    middle_grad = cot_vals + middle_part
    down_grad = scatter_dp(contract_rows(hidden_low, group_cot).astype(bf16), 0).astype(f32)

    def to_owners(grad):
        share = scatter_dp(grad.astype(bf16).reshape(members, columns * row_share, -1), 1)
        return trade_blocks(share)

    up_blocks = to_owners(contract_rows(second_low, pre_low))
    up_grad = up_blocks.swapaxes(0, 1).reshape(row_share, members * my_ff).astype(f32)

    branch_low = middle_grad.astype(bf16)
    group_branch = jnp.concatenate(spread_out(branch_low), 0)
    out_grad = scatter_dp(contract_rows(mixed_low, group_branch).astype(bf16), 0).astype(f32)
    out_off_grad = jnp.sum(branch_low.astype(f32), axis=0)
    mixed_grad = heads_of(contract_cols(group_branch, out_mat).astype(bf16), seg_len)
    probs = jnp.exp(masked_scores() - log_total)
    probs_again = probs.astype(bf16)
    prob_grad = jnp.einsum("sqhd,skhd->shqk", mixed_grad, value_heads, preferred_element_type=f32)
    value_grad = jnp.einsum(
        "shqk,sqhd->skhd", probs_again, mixed_grad, preferred_element_type=f32
    ).astype(bf16)
    score_grad = (probs * (prob_grad - jnp.sum(prob_grad * probs, axis=-1, keepdims=True))).astype(
        bf16
    )
    query_grad = (
        jnp.einsum("shqk,skhd->sqhd", score_grad, key_heads, preferred_element_type=f32)
        * score_scale
    ).astype(bf16)
    key_grad = (
        jnp.einsum("shqk,sqhd->skhd", score_grad, query_heads, preferred_element_type=f32)
        * score_scale
    ).astype(bf16)

    def flat(value):
        return value.reshape(-1, my_cols)

    query_grad = flat(query_grad)
    query_off_grad = jnp.sum(query_grad.astype(f32), axis=0)
    value_off_grad = jnp.sum(value_grad.astype(f32), axis=(0, 1)).reshape(-1)
    token_grads = jnp.concatenate(
        [query_grad, flat(key_grad[:, :seg_len]), flat(value_grad[:, :seg_len])], 1
    )
    prior_grads = jnp.concatenate([flat(key_grad[:, seg_len:]), flat(value_grad[:, seg_len:])], 1)
    token_qkv_grad = contract_rows(token_low, token_grads)
    prior_kv_grad = contract_rows(prior_low, prior_grads)
    qkv_grad = jnp.concatenate(
        [token_qkv_grad[:, :my_cols], token_qkv_grad[:, my_cols:] + prior_kv_grad], 1
    )
    qkv_shares = to_owners(qkv_grad)
    query_mat_grad, key_mat_grad, value_mat_grad = [
        qkv_shares[:, :, part * my_cols : (part + 1) * my_cols]
        .swapaxes(0, 1)
        .reshape(row_share, width)
        .astype(f32)
        for part in range(3)
    ]
    normed_grad = collect(by_member(contract_cols(token_grads, qkv_mat)))
    prior_normed_grad = collect(by_member(contract_cols(prior_grads, qkv_mat[:, my_cols:])))
    _, first_back = jax.vjp(norm_apply, token_vals, gain_one, bias_one)
    token_part, gain_token, bias_token = first_back(normed_grad)
    prior_vals = priors[0][:n_summary].astype(f32)
    _, prior_back = jax.vjp(norm_apply, prior_vals, gain_one, bias_one)
    prior_part, gain_prior, bias_prior = prior_back(prior_normed_grad[:n_summary])
    tokens_grad = middle_grad + token_part
    summary_grad = lax.ppermute(
        prior_part.astype(bf16), BOTH, [(i + 1, i) for i in range(total - 1)]
    ).astype(f32)

    def whole(value):
        return value.reshape(total, -1)

    def sliced(value):
        mine = value.reshape(columns, -1)
        full = jnp.zeros((total, mine.shape[1]), f32)
        return lax.dynamic_update_slice_in_dim(full, mine, me * columns, 0)

    pieces = [
        whole(gain_token + gain_prior),
        whole(bias_token + bias_prior),
        sliced(query_off_grad),
        sliced(value_off_grad),
        whole(out_off_grad),
        whole(gain_two_grad),
        whole(bias_two_grad),
        sliced(up_off_grad),
        whole(down_off_grad),
    ]
    share = scatter_small(jnp.concatenate(pieces, 1))
    outs = []
    at = 0
    for piece in pieces:
        outs.append(share[at : at + piece.shape[1]])
        at += piece.shape[1]
    return (
        output,
        tokens_grad,
        summary_grad[None],
        outs[0],
        outs[1],
        query_mat_grad,
        outs[2],
        key_mat_grad,
        value_mat_grad,
        outs[3],
        out_grad,
        outs[4],
        outs[5],
        outs[6],
        up_grad,
        outs[7],
        down_grad,
        outs[8],
    )


def solution(mesh):
    rows, rows2, rows3 = P(BOTH), P(BOTH, None), P(BOTH, None, None)
    return jax.shard_map(
        shards,
        mesh=mesh,
        in_specs=(
            rows2, rows3, rows2, P(), rows, rows, rows2, rows, rows2, rows2, rows, rows2, rows,
            rows, rows, rows2, rows, rows2, rows, rows2,
        ),
        out_specs=(
            rows2, rows2, rows3, rows, rows, rows2, rows, rows2, rows2, rows, rows2, rows, rows,
            rows, rows2, rows, rows2, rows,
        ),
        check_vma=False,
    )
```

```python
import jax
import jax.numpy as jnp
from jax import lax
from jax.experimental import pallas as pl
from jax.experimental.pallas import tpu as pltpu
from jax.sharding import PartitionSpec as P

F32, BF16 = jnp.float32, jnp.bfloat16
HEADS = 32
BOTH = ("fsdp", "dp")
HEAD = 64
PAIR = 2 * HEAD
PRIOR_ROWS = 64
NORM_ROWS = 64
MASKED = -1e30
GELU_A, GELU_B = 0.7978845608028654, 0.044715
VMEM_LIMIT = 60 * 1024 * 1024
VMEM = pl.BlockSpec(memory_space=pltpu.VMEM)
HBM = pl.BlockSpec(memory_space=pl.ANY)


def dot(left, right):
    return jnp.dot(left, right, preferred_element_type=F32)


def dot_t(left, right):
    return lax.dot_general(left, right, (((1,), (1,)), ((), ())), preferred_element_type=F32)


def t_dot(left, right):
    return lax.dot_general(left, right, (((0,), (0,)), ((), ())), preferred_element_type=F32)


def norm_parts(values):
    centre = values - jnp.mean(values, axis=-1, keepdims=True)
    spread = jnp.mean(centre * centre, axis=-1, keepdims=True)
    return centre, lax.rsqrt(spread + 1e-05)


def norm_apply(values, norm_gain, norm_bias):
    centre, inverse = norm_parts(values)
    return centre * inverse * norm_gain + norm_bias


def in_pair(half, rows):
    lane = lax.broadcasted_iota(jnp.int32, (rows, PAIR), 1)
    return (lane >= HEAD) if half else (lane < HEAD)


def pair_at(base, pair):
    return pl.ds(pl.multiple_of(base + pair * PAIR, PAIR), PAIR)


def load_blocks(hbm, scratch, sems):
    copies = [
        pltpu.make_async_copy(hbm.at[:, block], scratch.at[block], sems.at[block])
        for block in range(scratch.shape[0])
    ]
    for copy in copies:
        copy.start()
    return copies


def load_rows(parts, scratch, sems):
    copies = []
    at = 0
    for index, part in enumerate(parts):
        rows = part.shape[0]
        copies.append(
            pltpu.make_async_copy(part, scratch.at[pl.ds(at, rows)], sems.at[index])
        )
        at += rows
    for copy in copies:
        copy.start()
    return copies


def wait_all(copies):
    for copy in copies:
        copy.wait()


def rows_of(ref, columns):
    value = ref[:, :, :, columns]
    return value.reshape(-1, value.shape[-1])


def block_of(ref, block, columns):
    value = ref[block, :, :, columns]
    return value.reshape(-1, value.shape[-1])


COST = 230_000_000


def kernel_params(cost):
    return dict(
        compiler_params=pltpu.CompilerParams(vmem_limit_bytes=VMEM_LIMIT),
        cost_estimate=pl.CostEstimate(flops=cost * COST, bytes_accessed=1, transcendentals=0),
    )


def shape_of(rows, columns, dtype=BF16):
    return jax.ShapeDtypeStruct((rows, columns), dtype)


def attn_forward_kernel(
    x_ref, prior_ref, gain_ref, bias_ref, off_ref, ok_ref, attn_hbm,
    low_ref, qkv_ref, lse_ref, mixed_ref, part_ref, weights, mask, sems,
):
    members = weights.shape[0]
    cols = mixed_ref.shape[1]
    seg = x_ref.shape[0]
    keys = low_ref.shape[0]
    copies = load_blocks(attn_hbm, weights, sems)
    row = lax.broadcasted_iota(jnp.int32, (seg, keys), 0)
    col = lax.broadcasted_iota(jnp.int32, (seg, keys), 1)
    mask[...] = jnp.where(jnp.logical_or(col <= row, ok_ref[...] > 0.5), 0.0, MASKED)
    gain, bias = gain_ref[...], bias_ref[...]

    def norm_rows(block, _):
        at = pl.ds(pl.multiple_of(block * NORM_ROWS, NORM_ROWS), NORM_ROWS)
        low_ref[at, :] = norm_apply(x_ref[at, :].astype(F32), gain, bias).astype(BF16)
        return _

    lax.fori_loop(0, seg // NORM_ROWS, norm_rows, 0)
    low_ref[seg:, :] = norm_apply(prior_ref[...].astype(F32), gain, bias).astype(BF16)
    wait_all(copies)

    def project(part, _):
        at = pl.ds(pl.multiple_of(part * cols, PAIR), cols)
        qkv_ref[:, at] = (dot(low_ref[...], rows_of(weights, at)) + off_ref[:, at]).astype(BF16)
        return _

    lax.fori_loop(0, 3, project, 0)
    lane = lax.broadcasted_iota(jnp.int32, (seg, PAIR), 1)

    def attend(pair, _):
        query = qkv_ref[:seg, pair_at(0, pair)] * jnp.asarray(HEAD**-0.5, BF16)
        key = qkv_ref[:, pair_at(cols, pair)]
        value = qkv_ref[:, pair_at(2 * cols, pair)]
        merged = None
        for half in range(2):
            inside = in_pair(half, seg)
            scores = dot_t(jnp.where(inside, query, jnp.zeros_like(query)), key) + mask[...]
            row_max = jnp.max(scores, axis=-1, keepdims=True)
            expo = jnp.exp(scores - row_max)
            row_total = jnp.sum(expo, axis=-1, keepdims=True)
            log_total = row_max + jnp.log(row_total)
            lse_ref[...] = jnp.where(lane == 2 * pair + half, log_total, lse_ref[...])
            mixed = dot((expo * (1.0 / row_total)).astype(BF16), value)
            merged = mixed if merged is None else jnp.where(inside, mixed, merged)
        mixed_ref[:, pair_at(0, pair)] = merged.astype(BF16)
        return _

    lse_ref[...] = jnp.zeros_like(lse_ref)
    lax.fori_loop(0, cols // PAIR, attend, 0)

    def project_out(block, _):
        at = pl.ds(pl.multiple_of(block * cols, PAIR), cols)
        weight = block_of(weights, block, pl.ds(3 * cols, cols))
        part_ref[:, at] = dot(mixed_ref[...], weight).astype(part_ref.dtype)
        return _

    lax.fori_loop(0, members, project_out, 0)


def attn_forward(x, prior, gain, bias, off, ok_row, attn_w, part_type):
    seg, width = x.shape
    keys = seg + PRIOR_ROWS
    columns, members, share, wide = attn_w.shape
    cols = wide // 4
    return pl.pallas_call(
        attn_forward_kernel,
        out_shape=(
            shape_of(keys, width),
            shape_of(keys, 3 * cols),
            shape_of(seg, PAIR, F32),
            shape_of(seg, cols),
            shape_of(seg, width, part_type),
        ),
        in_specs=[VMEM] * 6 + [HBM],
        out_specs=(VMEM,) * 5,
        scratch_shapes=[
            pltpu.VMEM((members, columns, share, wide), BF16),
            pltpu.VMEM((seg, keys), F32),
            pltpu.SemaphoreType.DMA((members,)),
        ],
        name="attn_forward",
        **kernel_params(15),
    )(x, prior, gain, bias, off, ok_row, attn_w)


def attn_backward_kernel(
    branch_ref, qkv_ref, lse_ref, ok_ref, attn_hbm,
    grads_ref, sums_ref, joined_ref, weights, mask, lse_t, mixed_grad, sems,
):
    members = weights.shape[0]
    cols = mixed_grad.shape[1]
    seg = branch_ref.shape[0]
    keys = qkv_ref.shape[0]
    copies = load_blocks(attn_hbm, weights, sems)
    row = lax.broadcasted_iota(jnp.int32, (keys, seg), 0)
    col = lax.broadcasted_iota(jnp.int32, (keys, seg), 1)
    mask[...] = jnp.where(jnp.logical_or(row <= col, ok_ref[:, :1] > 0.5), 0.0, MASKED)
    lse_t[...] = lse_ref[...].T
    grads_ref[seg:, :cols] = jnp.zeros((keys - seg, cols), BF16)
    total = 0.0
    for block in range(members):
        copies[block].wait()
        weight = block_of(weights, block, pl.ds(3 * cols, cols))
        total = total + dot_t(branch_ref[:, block * cols : (block + 1) * cols], weight)
    mixed_grad[...] = total.astype(BF16)

    def attend(pair, _):
        query = qkv_ref[:seg, pair_at(0, pair)]
        scaled = query * jnp.asarray(HEAD**-0.5, BF16)
        key = qkv_ref[:, pair_at(cols, pair)]
        value = qkv_ref[:, pair_at(2 * cols, pair)]
        mixed = mixed_grad[:, pair_at(0, pair)]
        query_grad = key_grad = value_grad = 0.0
        for half in range(2):
            inside, inside_key = in_pair(half, seg), in_pair(half, keys)
            zero = jnp.zeros_like(query)
            scores = dot_t(key, jnp.where(inside, scaled, zero)) + mask[...]
            probs = jnp.exp(scores - lse_t[pl.ds(2 * pair + half, 1), :])
            mixed_half = jnp.where(inside, mixed, zero)
            prob_grad = dot_t(value, mixed_half)
            value_grad = value_grad + dot(probs.astype(BF16), mixed_half)
            delta = jnp.sum(prob_grad * probs, axis=0, keepdims=True)
            score_grad = (probs * (prob_grad - delta)).astype(BF16)
            key_grad = key_grad + dot(score_grad, jnp.where(inside, query, zero))
            key_half = jnp.where(inside_key, key, jnp.zeros_like(key))
            query_grad = query_grad + t_dot(score_grad, key_half)
        grads_ref[:seg, pair_at(0, pair)] = (query_grad * HEAD**-0.5).astype(BF16)
        grads_ref[:, pair_at(cols, pair)] = (key_grad * HEAD**-0.5).astype(BF16)
        grads_ref[:, pair_at(2 * cols, pair)] = value_grad.astype(BF16)
        return _

    lax.fori_loop(0, cols // PAIR, attend, 0)

    def back(block, _):
        weight = block_of(weights, block, pl.ds(0, 3 * cols))
        at = pl.ds(pl.multiple_of(block * cols, PAIR), cols)
        joined_ref[:, at] = dot_t(grads_ref[...], weight).astype(joined_ref.dtype)
        return _

    lax.fori_loop(0, members, back, 0)
    sums_ref[...] = jnp.sum(grads_ref[...].astype(F32), axis=0, keepdims=True)


def attn_backward(branch, qkv, lse, ok_col, attn_w, joined_type):
    seg, width = branch.shape
    keys = qkv.shape[0]
    columns, members, share, wide = attn_w.shape
    cols = wide // 4
    return pl.pallas_call(
        attn_backward_kernel,
        out_shape=(
            shape_of(keys, 3 * cols),
            shape_of(1, 3 * cols, F32),
            shape_of(keys, width, joined_type),
        ),
        in_specs=[VMEM] * 4 + [HBM],
        out_specs=(VMEM,) * 3,
        scratch_shapes=[
            pltpu.VMEM((members, columns, share, wide), BF16),
            pltpu.VMEM((keys, seg), F32),
            pltpu.VMEM((PAIR, seg), F32),
            pltpu.VMEM((seg, cols), BF16),
            pltpu.SemaphoreType.DMA((members,)),
        ],
        name="attn_backward",
        **kernel_params(14),
    )(branch, qkv, lse, ok_col, attn_w)


def ffn_hidden(seconds, off, up_w):
    count = len(seconds)
    seg, width = seconds[0].shape
    columns, members, share, wide = up_w.shape
    step = 512

    def kernel(*refs):
        off_ref, up_hbm, hidden_ref, slope_ref, second, up, sems = refs[count:]
        copies = load_blocks(up_hbm, up, sems) + load_rows(refs[:count], second, sems.at[pl.ds(members, count)])
        wait_all(copies)

        def hidden(block, _):
            at = pl.ds(pl.multiple_of(block * step, step), step)
            weight = rows_of(up, at)
            for index in range(count):
                rows = pl.ds(index * seg, seg)
                pre = dot(second[rows, :], weight) + off_ref[:, at]
                square = pre * pre
                bent = jnp.tanh(GELU_A * pre * (1.0 + GELU_B * square))
                gate = 0.5 * (1.0 + bent)
                hidden_ref[rows, at] = (pre * gate).astype(BF16)
                rise = 0.5 * pre * (1.0 - bent * bent) * (GELU_A * (1.0 + 3.0 * GELU_B * square))
                slope_ref[rows, at] = (gate + rise).astype(BF16)
            return _

        lax.fori_loop(0, wide // step, hidden, 0)

    return pl.pallas_call(
        kernel,
        out_shape=(shape_of(count * seg, wide), shape_of(count * seg, wide)),
        in_specs=[HBM] * count + [VMEM, HBM],
        out_specs=(VMEM,) * 2,
        scratch_shapes=[
            pltpu.VMEM((count * seg, width), BF16),
            pltpu.VMEM((members, columns, share, wide), BF16),
            pltpu.SemaphoreType.DMA((members + count,)),
        ],
        name="ffn_hidden",
        **kernel_params(24),
    )(*seconds, off, up_w)


def ffn_back(cots, slope, start, up_w, down_w, types):
    count = len(cots)
    seg, width = cots[0].shape
    columns, members, share, wide = up_w.shape
    step = 512
    rows = count * seg

    def kernel(*refs):
        slope_hbm, up_hbm, down_hbm, pre_ref, sums_ref = refs[count : count + 5]
        backs = refs[count + 5 : 2 * count + 5]
        cot, slope_here, up, down, sems = refs[2 * count + 5 :]
        first = load_rows(refs[:count], cot, sems)
        first += load_rows([slope_hbm.at[pl.ds(start, rows)]], slope_here, sems.at[pl.ds(count, 1)])
        first += load_rows([down_hbm], down, sems.at[pl.ds(count + 1, 1)])
        later = load_blocks(up_hbm, up, sems.at[pl.ds(count + 2, members)])
        wait_all(first)

        def grad(block, _):
            at = pl.ds(pl.multiple_of(block * step, step), step)
            value = dot_t(cot[...], down[at, :]) * slope_here[:, at].astype(F32)
            value = value.astype(BF16)
            pre_ref[:, at] = value
            sums_ref[:, at] = jnp.sum(value.astype(F32), axis=0, keepdims=True)
            return _

        lax.fori_loop(0, wide // step, grad, 0)
        wait_all(later)
        deep = columns * share

        def back(block, _):
            at = pl.ds(pl.multiple_of(block * deep, PAIR), deep)
            value = dot_t(pre_ref[...], up[block].reshape(deep, wide))
            for index in range(count):
                backs[index][:, at] = value[index * seg : (index + 1) * seg].astype(types[index])
            return _

        lax.fori_loop(0, members, back, 0)

    return pl.pallas_call(
        kernel,
        out_shape=(
            shape_of(rows, wide),
            shape_of(1, wide, F32),
            *[shape_of(seg, width, dtype) for dtype in types],
        ),
        in_specs=[HBM] * (count + 3),
        out_specs=(VMEM,) * (2 + count),
        scratch_shapes=[
            pltpu.VMEM((rows, width), BF16),
            pltpu.VMEM((rows, wide), BF16),
            pltpu.VMEM((members, columns, share, wide), BF16),
            pltpu.VMEM((wide, width), BF16),
            pltpu.SemaphoreType.DMA((count + 2 + members,)),
        ],
        name="ffn_back",
        **kernel_params(19),
    )(*cots, slope, up_w, down_w)


def ffn_out(hidden, down_w, types):
    count = len(types)
    rows, wide = hidden.shape
    seg = rows // count
    width = down_w.shape[1]
    step = 512

    def kernel(hidden_ref, down_ref, *outs):
        def block(part, _):
            at = pl.ds(pl.multiple_of(part * step, step), step)
            value = dot(hidden_ref[...], down_ref[:, at])
            for index in range(count):
                outs[index][:, at] = value[index * seg : (index + 1) * seg].astype(types[index])
            return _

        lax.fori_loop(0, width // step, block, 0)

    return pl.pallas_call(
        kernel,
        out_shape=tuple(shape_of(seg, width, dtype) for dtype in types),
        in_specs=[VMEM] * 2,
        out_specs=(VMEM,) * count,
        name="ffn_out",
        **kernel_params(15),
    )(hidden, down_w)


GRAD_ROWS = 256


def weight_grad(lefts, rights):
    tall, wide = lefts[0].shape[1], rights[0].shape[1]
    deep = sum(left.shape[0] for left in lefts)
    counts = len(lefts), len(rights)
    both = sum(counts)

    def kernel(*refs):
        out_ref, left, right, sems = refs[both:]
        step = pl.program_id(0)

        @pl.when(step == 0)
        def _():
            copies = load_rows(refs[: counts[0]], left, sems)
            wait_all(copies + load_rows(refs[counts[0] : both], right, sems.at[pl.ds(counts[0], counts[1])]))

        at = pl.ds(pl.multiple_of(step * GRAD_ROWS, GRAD_ROWS), GRAD_ROWS)
        out_ref[...] = t_dot(left[:, at], right[...]).astype(BF16)

    return pl.pallas_call(
        kernel,
        grid=(tall // GRAD_ROWS,),
        out_shape=shape_of(tall, wide),
        in_specs=[HBM] * both,
        out_specs=pl.BlockSpec((GRAD_ROWS, wide), lambda i: (i, 0)),
        scratch_shapes=[
            pltpu.VMEM((deep, tall), BF16),
            pltpu.VMEM((deep, wide), BF16),
            pltpu.SemaphoreType.DMA((both,)),
        ],
        name="weight_grad",
        **kernel_params(17),
    )(*lefts, *rights)


def attn_weight_grad(lows, grads, mixeds, branches):
    count = len(lows)
    keys, width = lows[0].shape
    seg, cols = mixeds[0].shape
    halves = cols // GRAD_ROWS

    def kernel(*refs):
        out_ref, low, grad, mixed, branch, sems = refs[4 * count :]
        step = pl.program_id(0)

        @pl.when(step == 0)
        def _():
            copies = []
            for index, scratch in enumerate((low, grad, mixed, branch)):
                some = refs[index * count : (index + 1) * count]
                copies += load_rows(some, scratch, sems.at[pl.ds(index * count, count)])
            wait_all(copies)

        at = pl.ds(pl.multiple_of(step * GRAD_ROWS, GRAD_ROWS), GRAD_ROWS)
        out_ref[:, : 3 * cols] = t_dot(low[:, at], grad[...]).astype(BF16)
        half = pl.ds(pl.multiple_of((step % halves) * GRAD_ROWS, GRAD_ROWS), GRAD_ROWS)
        block = pl.ds(pl.multiple_of((step // halves) * cols, PAIR), cols)
        out_ref[:, 3 * cols :] = t_dot(mixed[:, half], branch[:, block]).astype(BF16)

    return pl.pallas_call(
        kernel,
        grid=(width // GRAD_ROWS,),
        out_shape=shape_of(width, 4 * cols),
        in_specs=[HBM] * (4 * count),
        out_specs=pl.BlockSpec((GRAD_ROWS, 4 * cols), lambda i: (i, 0)),
        scratch_shapes=[
            pltpu.VMEM((count * keys, width), BF16),
            pltpu.VMEM((count * keys, 3 * cols), BF16),
            pltpu.VMEM((count * seg, cols), BF16),
            pltpu.VMEM((count * seg, width), BF16),
            pltpu.SemaphoreType.DMA((4 * count,)),
        ],
        name="attn_weight_grad",
        **kernel_params(21),
    )(*lows, *grads, *mixeds, *branches)


def swap(value, rel):
    if rel == 0:
        return value
    count = lax.axis_size("fsdp")
    return lax.ppermute(value, "fsdp", [(i, i ^ rel) for i in range(count)])


def after(value, *others):
    return lax.optimization_barrier((value, *others))[0]


def trade_blocks(blocks):
    return lax.all_to_all(blocks, "fsdp", 0, 0, tiled=True)


def gather_small(row):
    total = lax.axis_size("fsdp") * lax.axis_size("dp")
    place = lax.axis_index(BOTH)
    step = 1
    while step < total:
        came = lax.ppermute(row, BOTH, [(i, i ^ step) for i in range(total)])
        high = (place & step) != 0
        row = jnp.concatenate([jnp.where(high, came, row), jnp.where(high, row, came)], 0)
        step *= 2
    return row


def scatter_small(rows):
    total = lax.axis_size("fsdp") * lax.axis_size("dp")
    place = lax.axis_index(BOTH)
    step = total // 2
    while step >= 1:
        high = (place & step) != 0
        lower, upper = rows[:step], rows[step:]
        sent = jnp.where(high, lower, upper)
        came = lax.ppermute(sent, BOTH, [(i, i ^ step) for i in range(total)])
        rows = jnp.where(high, upper, lower) + came
        step //= 2
    return rows[0]


def gather_dp(value):
    return lax.all_gather(value, "dp", axis=0, tiled=True)


def scatter_dp(value, axis):
    return lax.psum_scatter(value, "dp", scatter_dimension=axis, tiled=True)


def shards(
    tokens,
    summaries,
    presence,
    seg_counts,
    ln1_gain,
    ln1_bias,
    w_query,
    query_bias,
    w_key,
    w_value,
    value_bias,
    w_out,
    out_bias,
    ln2_gain,
    ln2_bias,
    w_up,
    up_bias,
    w_down,
    down_bias,
    cotangent,
):
    members = lax.axis_size("fsdp")
    columns = lax.axis_size("dp")
    total = members * columns
    me = lax.axis_index("fsdp")
    seg_len, width = tokens.shape
    n_summary = summaries.shape[1]
    my_cols = width // members
    my_ff = w_up.shape[1] // members
    row_share = w_query.shape[0]
    rels = list(range(members))
    own_last = rels[::-1]

    def blocks_of(weight):
        return weight.reshape(row_share, members, -1).swapaxes(0, 1)

    def gathered(blocks):
        rows = blocks.reshape(members * row_share, -1)
        return gather_dp(rows).reshape(columns, members, row_share, -1)

    qkv_blocks = jnp.concatenate([blocks_of(w_query), blocks_of(w_key), blocks_of(w_value)], 2)
    qkv_blocks = trade_blocks(qkv_blocks)
    up_blocks = trade_blocks(after(blocks_of(w_up), qkv_blocks))
    attn_w = gathered(jnp.concatenate([qkv_blocks, blocks_of(w_out)], 2))
    up_w = gathered(up_blocks)
    down_w = gather_dp(w_down)

    group_tokens = [swap(tokens, rel) for rel in rels]
    prior_own = jnp.pad(summaries[0], ((0, PRIOR_ROWS - n_summary), (0, 0)))
    priors = []
    for rel in rels:
        pairs = [((((i // columns) ^ rel) * columns + i % columns) - 1, i) for i in range(total)]
        priors.append(lax.ppermute(prior_own, BOTH, [pair for pair in pairs if pair[0] >= 0]))

    small_parts = (
        ln1_gain, ln1_bias, query_bias, value_bias, out_bias, ln2_gain, ln2_bias, up_bias,
        down_bias, presence[0].astype(BF16),
    )
    packed = gather_small(jnp.concatenate(small_parts)[None])
    smalls = []
    at = 0
    for part in small_parts:
        smalls.append(packed[:, at : at + part.shape[0]].astype(F32))
        at += part.shape[0]
    gain_one, bias_one, query_off, value_off, out_off, gain_two, bias_two, up_off, down_off = [
        part.reshape(1, -1) for part in smalls[:-1]
    ]
    present_all = smalls[-1]
    query_off = lax.dynamic_slice_in_dim(query_off, me * my_cols, my_cols, 1)
    value_off = lax.dynamic_slice_in_dim(value_off, me * my_cols, my_cols, 1)
    up_off = lax.dynamic_slice_in_dim(up_off, me * my_ff, my_ff, 1)
    qkv_off = jnp.concatenate([query_off, jnp.zeros_like(query_off), value_off], 1)

    starts = jnp.cumsum(seg_counts) - seg_counts
    group_places = (me ^ jnp.arange(members)) * columns + lax.axis_index("dp")
    has_prev = jnp.all(group_places[:, None] != starts[None, :], axis=1)
    summary_ok = jnp.logical_and(present_all[group_places] == 1, has_prev[:, None]).astype(F32)
    ok_rows = jnp.pad(summary_ok, ((0, 0), (seg_len, PRIOR_ROWS - n_summary)))
    ok_cols = jnp.broadcast_to(ok_rows[:, :, None], (*ok_rows.shape, PAIR))

    group_cot = [swap(cotangent, rel) for rel in rels]

    def part_type(rel):
        return BF16 if rel else F32

    attn = {}
    middle_parts = {}
    previous = None
    for rel in own_last:
        x = group_tokens[rel]
        if previous is not None:
            x = after(x, previous)
        low, qkv, lse, mixed, part = attn_forward(
            x, priors[rel], gain_one, bias_one, qkv_off, ok_rows[rel : rel + 1], attn_w,
            part_type(rel),
        )
        attn[rel] = (low, qkv, lse, mixed)
        middle_parts[rel] = swap(part, rel).astype(F32)
        previous = lse
    token_vals = tokens.astype(F32)
    middle = token_vals + sum(middle_parts[rel] for rel in rels) + out_off
    second_own = norm_apply(middle, gain_two, bias_two).astype(BF16)
    group_second = [swap(second_own, rel) for rel in rels]

    def ordered(values):
        return [values[rel] for rel in own_last]

    hidden, slope = ffn_hidden(ordered(group_second), up_off, up_w)
    down_partial = weight_grad([hidden], ordered(group_cot))
    down_grad = scatter_dp(down_partial, 0).astype(F32)
    pre, up_sums, second_parts = [], [], {}
    half = (members + 1) // 2
    for at in range(0, members, half):
        some = own_last[at : at + half]
        cots = [group_cot[rel] for rel in some]
        cots[0] = after(cots[0], *(pre[-1:] or [down_partial]))
        pre_some, sums, *backs = ffn_back(
            cots, slope, at * seg_len, up_w, down_w, [part_type(rel) for rel in some]
        )
        pre.append(pre_some)
        up_sums.append(sums)
        for rel, back in zip(some, backs):
            second_parts[rel] = swap(back, rel)
    up_partial = weight_grad(ordered(group_second), pre)
    output_parts = ffn_out(after(hidden, up_partial), down_w, [part_type(rel) for rel in own_last])
    output_parts = {rel: swap(part, rel) for rel, part in zip(own_last, output_parts)}

    def to_row_blocks(grad):
        return scatter_dp(grad.reshape(members, columns * row_share, -1), 1)

    up_share = to_row_blocks(up_partial)
    up_grad = trade_blocks(up_share).swapaxes(0, 1).reshape(row_share, members * my_ff).astype(F32)
    second_parts = after(second_parts, up_partial)
    cot_vals = cotangent.astype(F32)
    second_grad = sum(second_parts[rel].astype(F32) for rel in rels)
    _, second_back = jax.vjp(norm_apply, middle, gain_two, bias_two)
    middle_part, gain_two_grad, bias_two_grad = second_back(second_grad)
    middle_grad = cot_vals + middle_part
    branch_low = middle_grad.astype(BF16)
    group_branch = [swap(branch_low, rel) for rel in rels]
    output_sum = sum(output_parts[rel].astype(F32) for rel in rels)
    output = (middle + output_sum + down_off).astype(BF16)

    grads, qkv_sums, joined_parts = {}, {}, {}
    previous = None
    for rel in rels:
        x = group_branch[rel]
        if previous is not None:
            x = after(x, previous)
        _, qkv, lse, _ = attn[rel]
        grads[rel], qkv_sums[rel], joined = attn_backward(
            x, qkv, lse, ok_cols[rel], attn_w, part_type(rel)
        )
        joined_parts[rel] = swap(joined, rel)
        previous = qkv_sums[rel]
    attn_partial = attn_weight_grad(
        [attn[rel][0] for rel in rels],
        [grads[rel] for rel in rels],
        [attn[rel][3] for rel in rels],
        group_branch,
    )
    attn_share = to_row_blocks(attn_partial)
    joined_parts = after(joined_parts, attn_partial)
    out_grad = (
        attn_share[:, :, 3 * my_cols :].swapaxes(0, 1).reshape(row_share, width).astype(F32)
    )
    qkv_shares = trade_blocks(attn_share[:, :, : 3 * my_cols])
    query_mat_grad, key_mat_grad, value_mat_grad = [
        qkv_shares[:, :, part * my_cols : (part + 1) * my_cols]
        .swapaxes(0, 1)
        .reshape(row_share, width)
        .astype(F32)
        for part in range(3)
    ]
    joined_grad = sum(joined_parts[rel].astype(F32) for rel in rels)
    _, first_back = jax.vjp(norm_apply, token_vals, gain_one, bias_one)
    token_part, gain_token, bias_token = first_back(joined_grad[:seg_len])
    prior_vals = priors[0][:n_summary].astype(F32)
    _, prior_back = jax.vjp(norm_apply, prior_vals, gain_one, bias_one)
    prior_part, gain_prior, bias_prior = prior_back(joined_grad[seg_len : seg_len + n_summary])
    tokens_grad = middle_grad + token_part
    summary_grad = lax.ppermute(
        prior_part.astype(BF16), BOTH, [(i + 1, i) for i in range(total - 1)]
    ).astype(F32)

    def whole(value):
        return value.reshape(total, -1)

    def sliced(value):
        mine = value.reshape(columns, -1)
        full = jnp.zeros((total, mine.shape[1]), F32)
        return lax.dynamic_update_slice_in_dim(full, mine, me * columns, 0)

    qkv_sum = sum(qkv_sums[rel] for rel in rels)
    pieces = [
        whole(gain_token + gain_prior),
        whole(bias_token + bias_prior),
        sliced(qkv_sum[:, :my_cols]),
        sliced(qkv_sum[:, 2 * my_cols :]),
        whole(jnp.sum(branch_low.astype(F32), axis=0)),
        whole(gain_two_grad),
        whole(bias_two_grad),
        sliced(sum(up_sums)),
        whole(jnp.sum(cot_vals, axis=0)),
    ]
    share = scatter_small(jnp.concatenate(pieces, 1))
    outs = []
    at = 0
    for piece in pieces:
        outs.append(share[at : at + piece.shape[1]])
        at += piece.shape[1]
    return (
        output,
        tokens_grad,
        summary_grad[None],
        outs[0],
        outs[1],
        query_mat_grad,
        outs[2],
        key_mat_grad,
        value_mat_grad,
        outs[3],
        out_grad,
        outs[4],
        outs[5],
        outs[6],
        up_grad,
        outs[7],
        down_grad,
        outs[8],
    )


def solution(mesh):
    rows, rows2, rows3 = P(BOTH), P(BOTH, None), P(BOTH, None, None)
    return jax.shard_map(
        shards,
        mesh=mesh,
        in_specs=(
            rows2, rows3, rows2, P(), rows, rows, rows2, rows, rows2, rows2, rows, rows2, rows,
            rows, rows, rows2, rows, rows2, rows, rows2,
        ),
        out_specs=(
            rows2, rows2, rows3, rows, rows, rows2, rows, rows2, rows2, rows, rows2, rows, rows,
            rows, rows2, rows, rows2, rows,
        ),
        check_vma=False,
    )
```

```python
import functools
import jax
import jax.numpy as jnp
from jax import lax
from jax.experimental import pallas as pl
from jax.experimental.pallas import tpu as pltpu
from jax.sharding import PartitionSpec as P

F32, BF16 = jnp.float32, jnp.bfloat16
HEADS = 32
BOTH = ("fsdp", "dp")
HEAD = 64
PAIR = 2 * HEAD
PRIOR_ROWS = 64
NORM_ROWS = 64
MASKED = -1e30
GELU_A, GELU_B = 0.7978845608028654, 0.044715
VMEM_LIMIT = 60 * 1024 * 1024
VMEM = pl.BlockSpec(memory_space=pltpu.VMEM)
HBM = pl.BlockSpec(memory_space=pl.ANY)


def dot(left, right):
    return jnp.dot(left, right, preferred_element_type=F32)


def dot_t(left, right):
    return lax.dot_general(left, right, (((1,), (1,)), ((), ())), preferred_element_type=F32)


def t_dot(left, right):
    return lax.dot_general(left, right, (((0,), (0,)), ((), ())), preferred_element_type=F32)


def norm_parts(values):
    centre = values - jnp.mean(values, axis=-1, keepdims=True)
    spread = jnp.mean(centre * centre, axis=-1, keepdims=True)
    return centre, lax.rsqrt(spread + 1e-05)


def norm_apply(values, norm_gain, norm_bias):
    centre, inverse = norm_parts(values)
    return centre * inverse * norm_gain + norm_bias


def in_pair(half, rows):
    lane = lax.broadcasted_iota(jnp.int32, (rows, PAIR), 1)
    return (lane >= HEAD) if half else (lane < HEAD)


def pair_at(base, pair):
    return pl.ds(pl.multiple_of(base + pair * PAIR, PAIR), PAIR)


def load_blocks(hbm, scratch, sems):
    copies = [
        pltpu.make_async_copy(hbm.at[:, block], scratch.at[block], sems.at[block])
        for block in range(scratch.shape[0])
    ]
    for copy in copies:
        copy.start()
    return copies


def load_rows(parts, scratch, sems):
    copies = []
    at = 0
    for index, part in enumerate(parts):
        rows = part.shape[0]
        copies.append(
            pltpu.make_async_copy(part, scratch.at[pl.ds(at, rows)], sems.at[index])
        )
        at += rows
    for copy in copies:
        copy.start()
    return copies


def wait_all(copies):
    for copy in copies:
        copy.wait()


def rows_of(ref, columns):
    value = ref[:, :, :, columns]
    return value.reshape(-1, value.shape[-1])


def block_of(ref, block, columns):
    value = ref[block, :, :, columns]
    return value.reshape(-1, value.shape[-1])


COST = 1_000_000


def kernel_params(cost):
    return dict(
        compiler_params=pltpu.CompilerParams(vmem_limit_bytes=VMEM_LIMIT),
        cost_estimate=pl.CostEstimate(flops=cost * COST, bytes_accessed=1, transcendentals=0),
    )


def shape_of(rows, columns, dtype=BF16):
    return jax.ShapeDtypeStruct((rows, columns), dtype)


def attn_forward_kernel(
    count, *refs,
):
    gain_ref, bias_ref, off_ref, ok_ref, attn_hbm = refs[count : count + 5]
    low_ref, qkv_ref, lse_ref, mixed_ref, part_ref, x_ref, weights, mask, sems = refs[count + 5 :]
    members = weights.shape[0]
    seg, cols = mixed_ref.shape
    keys = low_ref.shape[0]
    x_copies = load_rows(refs[:count], x_ref, sems.at[pl.ds(members, count)])
    copies = load_blocks(attn_hbm, weights, sems)
    row = lax.broadcasted_iota(jnp.int32, (seg, keys), 0)
    col = lax.broadcasted_iota(jnp.int32, (seg, keys), 1)
    mask[...] = jnp.where(jnp.logical_or(col <= row, ok_ref[...] > 0.5), 0.0, MASKED)
    gain, bias = gain_ref[...], bias_ref[...]
    wait_all(x_copies)

    def norm_rows(block, _):
        at = pl.ds(pl.multiple_of(block * NORM_ROWS, NORM_ROWS), NORM_ROWS)
        low_ref[at, :] = norm_apply(x_ref[at, :].astype(F32), gain, bias).astype(BF16)
        return _

    lax.fori_loop(0, keys // NORM_ROWS, norm_rows, 0)
    wait_all(copies)

    def project(part, _):
        at = pl.ds(pl.multiple_of(part * cols, PAIR), cols)
        qkv_ref[:, at] = (dot(low_ref[...], rows_of(weights, at)) + off_ref[:, at]).astype(BF16)
        return _

    lax.fori_loop(0, 3, project, 0)
    lane = lax.broadcasted_iota(jnp.int32, (seg, PAIR), 1)

    def attend(pair, _):
        query = qkv_ref[:seg, pair_at(0, pair)] * jnp.asarray(HEAD**-0.5, BF16)
        key = qkv_ref[:, pair_at(cols, pair)]
        value = qkv_ref[:, pair_at(2 * cols, pair)]
        merged = None
        for half in range(2):
            inside = in_pair(half, seg)
            scores = dot_t(jnp.where(inside, query, jnp.zeros_like(query)), key) + mask[...]
            row_max = jnp.max(scores, axis=-1, keepdims=True)
            expo = jnp.exp(scores - row_max)
            row_total = jnp.sum(expo, axis=-1, keepdims=True)
            log_total = row_max + jnp.log(row_total)
            lse_ref[...] = jnp.where(lane == 2 * pair + half, log_total, lse_ref[...])
            mixed = dot((expo * (1.0 / row_total)).astype(BF16), value)
            merged = mixed if merged is None else jnp.where(inside, mixed, merged)
        mixed_ref[:, pair_at(0, pair)] = merged.astype(BF16)
        return _

    lse_ref[...] = jnp.zeros_like(lse_ref)
    lax.fori_loop(0, cols // PAIR, attend, 0)

    def project_out(block, _):
        at = pl.ds(pl.multiple_of(block * cols, PAIR), cols)
        weight = block_of(weights, block, pl.ds(3 * cols, cols))
        part_ref[:, at] = dot(mixed_ref[...], weight).astype(part_ref.dtype)
        return _

    lax.fori_loop(0, members, project_out, 0)


def attn_forward(x, gain, bias, off, ok_row, attn_w, part_type):
    keys, width = sum(piece.shape[0] for piece in x), x[0].shape[1]
    seg = keys - PRIOR_ROWS
    columns, members, share, wide = attn_w.shape
    cols = wide // 4
    return pl.pallas_call(
        functools.partial(attn_forward_kernel, len(x)),
        out_shape=(
            shape_of(keys, width),
            shape_of(keys, 3 * cols),
            shape_of(seg, PAIR, F32),
            shape_of(seg, cols),
            shape_of(seg, width, part_type),
        ),
        in_specs=[HBM] * len(x) + [VMEM] * 4 + [HBM],
        out_specs=(VMEM,) * 5,
        scratch_shapes=[
            pltpu.VMEM((keys, width), BF16),
            pltpu.VMEM((members, columns, share, wide), BF16),
            pltpu.VMEM((seg, keys), F32),
            pltpu.SemaphoreType.DMA((members + len(x),)),
        ],
        name="attn_forward",
        **kernel_params(15),
    )(*x, gain, bias, off, ok_row, attn_w)


def attn_backward_kernel(
    count, *refs,
):
    qkv_ref, lse_ref, ok_ref, attn_hbm, grads_ref, sums_ref, joined_ref = refs[count : count + 7]
    branch_ref, weights, mask, lse_t, mixed_grad, sems = refs[count + 7 :]
    members = weights.shape[0]
    cols = mixed_grad.shape[1]
    seg = branch_ref.shape[0]
    keys = qkv_ref.shape[0]
    branch_copies = load_rows(refs[:count], branch_ref, sems.at[pl.ds(members, count)])
    copies = load_blocks(attn_hbm, weights, sems)
    row = lax.broadcasted_iota(jnp.int32, (keys, seg), 0)
    col = lax.broadcasted_iota(jnp.int32, (keys, seg), 1)
    mask[...] = jnp.where(jnp.logical_or(row <= col, ok_ref[:, :1] > 0.5), 0.0, MASKED)
    lse_t[...] = lse_ref[...].T
    grads_ref[seg:, :cols] = jnp.zeros((keys - seg, cols), BF16)
    total = 0.0
    wait_all(branch_copies)
    for block in range(members):
        copies[block].wait()
        weight = block_of(weights, block, pl.ds(3 * cols, cols))
        total = total + dot_t(branch_ref[:, block * cols : (block + 1) * cols], weight)
    mixed_grad[...] = total.astype(BF16)

    def attend(pair, _):
        query = qkv_ref[:seg, pair_at(0, pair)]
        scaled = query * jnp.asarray(HEAD**-0.5, BF16)
        key = qkv_ref[:, pair_at(cols, pair)]
        value = qkv_ref[:, pair_at(2 * cols, pair)]
        mixed = mixed_grad[:, pair_at(0, pair)]
        query_grad = key_grad = value_grad = 0.0
        for half in range(2):
            inside, inside_key = in_pair(half, seg), in_pair(half, keys)
            zero = jnp.zeros_like(query)
            scores = dot_t(key, jnp.where(inside, scaled, zero)) + mask[...]
            probs = jnp.exp(scores - lse_t[pl.ds(2 * pair + half, 1), :])
            mixed_half = jnp.where(inside, mixed, zero)
            prob_grad = dot_t(value, mixed_half)
            value_grad = value_grad + dot(probs.astype(BF16), mixed_half)
            delta = jnp.sum(prob_grad * probs, axis=0, keepdims=True)
            score_grad = (probs * (prob_grad - delta)).astype(BF16)
            key_grad = key_grad + dot(score_grad, jnp.where(inside, query, zero))
            key_half = jnp.where(inside_key, key, jnp.zeros_like(key))
            query_grad = query_grad + t_dot(score_grad, key_half)
        grads_ref[:seg, pair_at(0, pair)] = (query_grad * HEAD**-0.5).astype(BF16)
        grads_ref[:, pair_at(cols, pair)] = (key_grad * HEAD**-0.5).astype(BF16)
        grads_ref[:, pair_at(2 * cols, pair)] = value_grad.astype(BF16)
        return _

    lax.fori_loop(0, cols // PAIR, attend, 0)

    def back(block, _):
        weight = block_of(weights, block, pl.ds(0, 3 * cols))
        at = pl.ds(pl.multiple_of(block * cols, PAIR), cols)
        joined_ref[:, at] = dot_t(grads_ref[...], weight).astype(joined_ref.dtype)
        return _

    lax.fori_loop(0, members, back, 0)
    sums_ref[...] = jnp.sum(grads_ref[...].astype(F32), axis=0, keepdims=True)


def attn_backward(branch, qkv, lse, ok_col, attn_w, joined_type):
    seg, width = sum(piece.shape[0] for piece in branch), branch[0].shape[1]
    keys = qkv.shape[0]
    columns, members, share, wide = attn_w.shape
    cols = wide // 4
    return pl.pallas_call(
        functools.partial(attn_backward_kernel, len(branch)),
        out_shape=(
            shape_of(keys, 3 * cols),
            shape_of(1, 3 * cols, F32),
            shape_of(keys, width, joined_type),
        ),
        in_specs=[HBM] * len(branch) + [VMEM] * 3 + [HBM],
        out_specs=(VMEM,) * 3,
        scratch_shapes=[
            pltpu.VMEM((seg, width), BF16),
            pltpu.VMEM((members, columns, share, wide), BF16),
            pltpu.VMEM((keys, seg), F32),
            pltpu.VMEM((PAIR, seg), F32),
            pltpu.VMEM((seg, cols), BF16),
            pltpu.SemaphoreType.DMA((members + len(branch),)),
        ],
        name="attn_backward",
        **kernel_params(14),
    )(*branch, qkv, lse, ok_col, attn_w)


def ffn_hidden(seconds, off, up_w):
    pieces = flat_list(seconds)
    given = len(pieces)
    width = pieces[0].shape[1]
    count = len(seconds)
    seg = sum(piece.shape[0] for piece in pieces) // count
    columns, members, share, wide = up_w.shape
    step = 512

    def kernel(*refs):
        off_ref, up_hbm = refs[given : given + 2]
        outs = refs[given + 2 : given + 2 + 2 * count]
        second, up, sems = refs[given + 2 + 2 * count :]
        copies = load_blocks(up_hbm, up, sems)
        wait_all(copies + load_rows(refs[:given], second, sems.at[pl.ds(members, given)]))

        def hidden(block, _):
            at = pl.ds(pl.multiple_of(block * step, step), step)
            weight = rows_of(up, at)
            for index in range(count):
                pre = dot(second[pl.ds(index * seg, seg), :], weight) + off_ref[:, at]
                square = pre * pre
                bent = jnp.tanh(GELU_A * pre * (1.0 + GELU_B * square))
                gate = 0.5 * (1.0 + bent)
                outs[index][:, at] = (pre * gate).astype(BF16)
                rise = 0.5 * pre * (1.0 - bent * bent) * (GELU_A * (1.0 + 3.0 * GELU_B * square))
                outs[count + index][:, at] = (gate + rise).astype(BF16)
            return _

        lax.fori_loop(0, wide // step, hidden, 0)

    outs = pl.pallas_call(
        kernel,
        out_shape=[shape_of(seg, wide)] * (2 * count),
        in_specs=[HBM] * given + [VMEM, HBM],
        out_specs=[VMEM] * (2 * count),
        scratch_shapes=[
            pltpu.VMEM((count * seg, width), BF16),
            pltpu.VMEM((members, columns, share, wide), BF16),
            pltpu.SemaphoreType.DMA((members + given,)),
        ],
        name="ffn_hidden",
        **kernel_params(6 * count),
    )(*pieces, off, up_w)
    return outs[:count], outs[count:]


def ffn_back(cots, slopes, up_w, down_w, types):
    pieces = flat_list(cots)
    given = len(pieces)
    count = len(slopes)
    seg, width = slopes[0].shape[0], pieces[0].shape[1]
    columns, members, share, wide = up_w.shape
    step = 512
    rows = count * seg
    loads = given + count

    def kernel(*refs):
        up_hbm, down_hbm, pre_ref, sums_ref = refs[loads : loads + 4]
        backs = refs[loads + 4 : loads + 4 + count]
        cot, slope, up, down, sems = refs[loads + 4 + count :]
        first = load_rows(refs[:given], cot, sems)
        first += load_rows([down_hbm], down, sems.at[pl.ds(loads, 1)])
        first += load_rows(refs[given:loads], slope, sems.at[pl.ds(given, count)])
        later = load_blocks(up_hbm, up, sems.at[pl.ds(loads + 1, members)])
        wait_all(first)

        def grad(block, _):
            at = pl.ds(pl.multiple_of(block * step, step), step)
            value = dot_t(cot[...], down[at, :]) * slope[:, at].astype(F32)
            value = value.astype(BF16)
            pre_ref[:, at] = value
            sums_ref[:, at] = jnp.sum(value.astype(F32), axis=0, keepdims=True)
            return _

        lax.fori_loop(0, wide // step, grad, 0)
        wait_all(later)
        deep = columns * share

        def back(block, _):
            at = pl.ds(pl.multiple_of(block * deep, PAIR), deep)
            value = dot_t(pre_ref[...], up[block].reshape(deep, wide))
            for index in range(count):
                backs[index][:, at] = value[index * seg : (index + 1) * seg].astype(types[index])
            return _

        lax.fori_loop(0, members, back, 0)

    return pl.pallas_call(
        kernel,
        out_shape=(
            shape_of(rows, wide),
            shape_of(1, wide, F32),
            *[shape_of(seg, width, dtype) for dtype in types],
        ),
        in_specs=[HBM] * (loads + 2),
        out_specs=(VMEM,) * (2 + count),
        scratch_shapes=[
            pltpu.VMEM((rows, width), BF16),
            pltpu.VMEM((rows, wide), BF16),
            pltpu.VMEM((members, columns, share, wide), BF16),
            pltpu.VMEM((wide, width), BF16),
            pltpu.SemaphoreType.DMA((loads + 1 + members,)),
        ],
        name="ffn_back",
        **kernel_params(10 * count),
    )(*pieces, *slopes, up_w, down_w)


def ffn_out(hiddens, down_w, types):
    count = len(types)
    seg, wide = hiddens[0].shape
    width = down_w.shape[1]
    step = 512

    def kernel(*refs):
        down_ref = refs[count]
        outs = refs[count + 1 : 2 * count + 1]
        hidden, sems = refs[2 * count + 1 :]
        wait_all(load_rows(refs[:count], hidden, sems))

        def block(part, _):
            at = pl.ds(pl.multiple_of(part * step, step), step)
            value = dot(hidden[...], down_ref[:, at])
            for index in range(count):
                outs[index][:, at] = value[index * seg : (index + 1) * seg].astype(types[index])
            return _

        lax.fori_loop(0, width // step, block, 0)

    return pl.pallas_call(
        kernel,
        out_shape=tuple(shape_of(seg, width, dtype) for dtype in types),
        in_specs=[HBM] * count + [VMEM],
        out_specs=(VMEM,) * count,
        scratch_shapes=[
            pltpu.VMEM((count * seg, wide), BF16),
            pltpu.SemaphoreType.DMA((count,)),
        ],
        name="ffn_out",
        **kernel_params(18),
    )(*hiddens, down_w)


GRAD_ROWS = 256


def weight_grad(lefts, rights):
    tall, wide = lefts[0].shape[1], rights[0].shape[1]
    deep = sum(left.shape[0] for left in lefts)
    counts = len(lefts), len(rights)
    both = sum(counts)

    def kernel(*refs):
        out_ref, left, right, sems = refs[both:]
        step = pl.program_id(0)

        @pl.when(step == 0)
        def _():
            copies = load_rows(refs[: counts[0]], left, sems)
            wait_all(copies + load_rows(refs[counts[0] : both], right, sems.at[pl.ds(counts[0], counts[1])]))

        at = pl.ds(pl.multiple_of(step * GRAD_ROWS, GRAD_ROWS), GRAD_ROWS)
        out_ref[...] = t_dot(left[:, at], right[...]).astype(BF16)

    return pl.pallas_call(
        kernel,
        grid=(tall // GRAD_ROWS,),
        out_shape=shape_of(tall, wide),
        in_specs=[HBM] * both,
        out_specs=pl.BlockSpec((GRAD_ROWS, wide), lambda i: (i, 0)),
        scratch_shapes=[
            pltpu.VMEM((deep, tall), BF16),
            pltpu.VMEM((deep, wide), BF16),
            pltpu.SemaphoreType.DMA((both,)),
        ],
        name="weight_grad",
        **kernel_params(17),
    )(*lefts, *rights)


def attn_weight_grad(lows, grads, mixeds, branches):
    lists = lows, grads, mixeds, branches
    width, cols = lows[0].shape[1], mixeds[0].shape[1]
    halves = cols // GRAD_ROWS
    ends = [0]
    for some in lists:
        ends.append(ends[-1] + len(some))

    def kernel(*refs):
        out_ref, low, grad, mixed, branch, sems = refs[ends[-1] :]
        step = pl.program_id(0)

        @pl.when(step == 0)
        def _():
            copies = []
            for first, last, scratch in zip(ends, ends[1:], (low, grad, mixed, branch)):
                copies += load_rows(refs[first:last], scratch, sems.at[pl.ds(first, last - first)])
            wait_all(copies)

        at = pl.ds(pl.multiple_of(step * GRAD_ROWS, GRAD_ROWS), GRAD_ROWS)
        out_ref[:, : 3 * cols] = t_dot(low[:, at], grad[...]).astype(BF16)
        half = pl.ds(pl.multiple_of((step % halves) * GRAD_ROWS, GRAD_ROWS), GRAD_ROWS)
        block = pl.ds(pl.multiple_of((step // halves) * cols, PAIR), cols)
        out_ref[:, 3 * cols :] = t_dot(mixed[:, half], branch[:, block]).astype(BF16)

    return pl.pallas_call(
        kernel,
        grid=(width // GRAD_ROWS,),
        out_shape=shape_of(width, 4 * cols),
        in_specs=[HBM] * ends[-1],
        out_specs=pl.BlockSpec((GRAD_ROWS, 4 * cols), lambda i: (i, 0)),
        scratch_shapes=[
            pltpu.VMEM((sum(one.shape[0] for one in some), some[0].shape[1]), BF16)
            for some in lists
        ]
        + [pltpu.SemaphoreType.DMA((ends[-1],))],
        name="attn_weight_grad",
        **kernel_params(21),
    )(*lows, *grads, *mixeds, *branches)


def norm_values(values):
    centre, inverse = norm_parts(values)
    return centre * inverse, inverse


def norm_back(hat, inverse, grad, gain):
    hat_grad = grad * gain
    mean = jnp.mean(hat_grad, axis=-1, keepdims=True)
    along = jnp.mean(hat_grad * hat, axis=-1, keepdims=True)
    return inverse * (hat_grad - mean - hat * along)


def column_sum(value):
    return jnp.sum(value, axis=0, keepdims=True)


def row_blocks(width, last=None):
    if last is None:
        return pl.BlockSpec((NORM_ROWS, width), lambda i: (i, 0))
    return pl.BlockSpec((NORM_ROWS, width), lambda i: (jnp.minimum(i, last), 0))


def kept(rows, width):
    return pl.BlockSpec((rows, width), lambda i: (0, 0))


def sum_parts(parts):
    total = parts[0][...].astype(F32)
    for part in parts[1:]:
        total = total + part[...].astype(F32)
    return total


def middle_norm(tokens, parts, off, gain, bias):
    seg, width = tokens.shape
    count = len(parts)

    def kernel(*refs):
        off_ref, gain_ref, bias_ref, middle_ref, second_ref = refs[count + 1 :]
        total = sum_parts(refs[: count + 1]) + off_ref[...]
        middle_ref[...] = total
        second_ref[...] = norm_apply(total, gain_ref[...], bias_ref[...]).astype(BF16)

    return pl.pallas_call(
        kernel,
        grid=(seg // NORM_ROWS,),
        out_shape=(shape_of(seg, width, F32), shape_of(seg, width)),
        in_specs=[row_blocks(width)] * (count + 1) + [kept(1, width)] * 3,
        out_specs=(row_blocks(width),) * 2,
        name="middle_norm",
        **kernel_params(5),
    )(tokens, *parts, off, gain, bias)


def middle_back(middle, cot, parts, gain):
    seg, width = middle.shape
    count = len(parts)

    def kernel(*refs):
        middle_ref, cot_ref, gain_ref, grad_ref, branch_ref, sums_ref = refs[count:]

        @pl.when(pl.program_id(0) == 0)
        def _():
            sums_ref[...] = jnp.zeros_like(sums_ref)

        grad = sum_parts(refs[:count])
        hat, inverse = norm_values(middle_ref[...])
        cots = cot_ref[...].astype(F32)
        total = cots + norm_back(hat, inverse, grad, gain_ref[...])
        low = total.astype(BF16)
        grad_ref[...] = total
        branch_ref[...] = low
        sums_ref[0:1, :] += column_sum(grad * hat)
        sums_ref[1:2, :] += column_sum(grad)
        sums_ref[2:3, :] += column_sum(low.astype(F32))
        sums_ref[3:4, :] += column_sum(cots)

    return pl.pallas_call(
        kernel,
        grid=(seg // NORM_ROWS,),
        out_shape=(shape_of(seg, width, F32), shape_of(seg, width), shape_of(4, width, F32)),
        in_specs=[row_blocks(width)] * (count + 2) + [kept(1, width)],
        out_specs=(row_blocks(width), row_blocks(width), kept(4, width)),
        name="middle_back",
        **kernel_params(5),
    )(*parts, middle, cot, gain)


def first_back(joined, parts, middle_grad, gain):
    seg, width = middle_grad.shape
    keys = joined.shape[0]
    count = len(parts)
    last = seg // NORM_ROWS - 1

    def kernel(*refs):
        joined_ref, middle_ref, gain_ref, tokens_ref, prior_ref, sums_ref = refs[count:]
        step = pl.program_id(0)

        @pl.when(step == 0)
        def _():
            sums_ref[...] = jnp.zeros_like(sums_ref)

        grad = sum_parts(refs[:count])
        hat, inverse = norm_values(joined_ref[...].astype(F32))
        sums_ref[0:1, :] += column_sum(grad * hat)
        sums_ref[1:2, :] += column_sum(grad)
        back = norm_back(hat, inverse, grad, gain_ref[...])

        @pl.when(step <= last)
        def _():
            tokens_ref[...] = middle_ref[...] + back

        @pl.when(step > last)
        def _():
            prior_ref[...] = back.astype(BF16)

    return pl.pallas_call(
        kernel,
        grid=(keys // NORM_ROWS,),
        out_shape=(
            shape_of(seg, width, F32),
            shape_of(keys - seg, width),
            shape_of(2, width, F32),
        ),
        in_specs=[row_blocks(width)] * (count + 1) + [row_blocks(width, last), kept(1, width)],
        out_specs=(row_blocks(width, last), kept(keys - seg, width), kept(2, width)),
        name="first_back",
        **kernel_params(500_000),
    )(*parts, joined, middle_grad, gain)


def swap(value, rel):
    if rel == 0:
        return value
    count = lax.axis_size("fsdp")
    return lax.ppermute(value, "fsdp", [(i, i ^ rel) for i in range(count)])


def spread_near(value):
    return [swap(value, rel) for rel in range(1, min(lax.axis_size("fsdp"), 3))]


def spread_far(value, near, *others):
    members = lax.axis_size("fsdp")
    near = list(lax.optimization_barrier((*near, others))[: len(near)])
    pieces = [[value]] + [[one] for one in near]
    if members > 3:
        rows = value.shape[0] // 2
        pieces.append([swap(near[0][:rows], 2), swap(near[1][rows:], 1)])
    return pieces + [[swap(value, rel)] for rel in range(4, members)]


def flat_list(lists):
    return [piece for some in lists for piece in some]


def after(value, *others):
    return lax.optimization_barrier((value, *others))[0]


def trade_blocks(blocks):
    return lax.all_to_all(blocks, "fsdp", 0, 0, tiled=True)


def doubled(rows, axis):
    size = lax.axis_size(axis)
    place = lax.axis_index(axis)
    step = 1
    while step < size:
        came = lax.ppermute(rows, axis, [(i, i ^ step) for i in range(size)])
        high = (place & step) != 0
        rows = jnp.concatenate([jnp.where(high, came, rows), jnp.where(high, rows, came)], 0)
        step *= 2
    return rows


def scatter_small(rows):
    return jnp.sum(lax.all_to_all(rows, BOTH, 0, 0, tiled=True), axis=0)


def gather_dp(value):
    return lax.all_gather(value, "dp", axis=0, tiled=True)


def scatter_dp(value, axis):
    return lax.psum_scatter(value, "dp", scatter_dimension=axis, tiled=True)


def shards(
    tokens,
    summaries,
    presence,
    seg_counts,
    ln1_gain,
    ln1_bias,
    w_query,
    query_bias,
    w_key,
    w_value,
    value_bias,
    w_out,
    out_bias,
    ln2_gain,
    ln2_bias,
    w_up,
    up_bias,
    w_down,
    down_bias,
    cotangent,
):
    members = lax.axis_size("fsdp")
    columns = lax.axis_size("dp")
    total = members * columns
    me = lax.axis_index("fsdp")
    seg_len, width = tokens.shape
    n_summary = summaries.shape[1]
    my_cols = width // members
    my_ff = w_up.shape[1] // members
    row_share = w_query.shape[0]
    rels = list(range(members))
    own_last = rels[::-1]

    def blocks_of(weight):
        return weight.reshape(row_share, members, -1).swapaxes(0, 1)

    def gathered(blocks):
        rows = blocks.reshape(members * row_share, -1)
        return gather_dp(rows).reshape(columns, members, row_share, -1)

    small_parts = (
        ln1_gain, ln1_bias, query_bias, value_bias, out_bias, ln2_gain, ln2_bias, up_bias,
        down_bias, presence[0].astype(BF16),
    )
    packed = doubled(jnp.concatenate(small_parts)[None], "fsdp")
    prior = jnp.pad(summaries[0], ((0, PRIOR_ROWS - n_summary), (0, 0)))
    prior = lax.ppermute(prior, BOTH, [(i, i + 1) for i in range(total - 1)])
    joined = jnp.concatenate([tokens, prior], 0)

    qkv_blocks = jnp.concatenate([blocks_of(w_query), blocks_of(w_key), blocks_of(w_value)], 2)
    qkv_blocks = trade_blocks(qkv_blocks)
    up_blocks, packed = lax.optimization_barrier((blocks_of(w_up), packed, qkv_blocks, joined))[:2]
    up_blocks = trade_blocks(up_blocks)
    attn_w = gathered(jnp.concatenate([qkv_blocks, blocks_of(w_out)], 2))
    up_w = gathered(up_blocks)
    down_w = gather_dp(w_down)

    joined_near = spread_near(after(joined, up_blocks))
    group_joined = spread_far(joined, joined_near)
    cot_near = spread_near(after(cotangent, *flat_list(group_joined[1:])))
    packed = doubled(packed, "dp").reshape(columns, members, -1).swapaxes(0, 1)
    packed = packed.reshape(total, -1)

    smalls = []
    at = 0
    for part in small_parts:
        smalls.append(packed[:, at : at + part.shape[0]].astype(F32))
        at += part.shape[0]
    gain_one, bias_one, query_off, value_off, out_off, gain_two, bias_two, up_off, down_off = [
        part.reshape(1, -1) for part in smalls[:-1]
    ]
    present_all = smalls[-1]
    query_off = lax.dynamic_slice_in_dim(query_off, me * my_cols, my_cols, 1)
    value_off = lax.dynamic_slice_in_dim(value_off, me * my_cols, my_cols, 1)
    up_off = lax.dynamic_slice_in_dim(up_off, me * my_ff, my_ff, 1)
    qkv_off = jnp.concatenate([query_off, jnp.zeros_like(query_off), value_off], 1)

    starts = jnp.cumsum(seg_counts) - seg_counts
    group_places = (me ^ jnp.arange(members)) * columns + lax.axis_index("dp")
    has_prev = jnp.all(group_places[:, None] != starts[None, :], axis=1)
    summary_ok = jnp.logical_and(present_all[group_places] == 1, has_prev[:, None]).astype(F32)
    ok_rows = jnp.pad(summary_ok, ((0, 0), (seg_len, PRIOR_ROWS - n_summary)))
    ok_cols = jnp.broadcast_to(ok_rows[:, :, None], (*ok_rows.shape, PAIR))


    def part_type(rel):
        return BF16 if rel else F32

    attn = {}
    middle_parts = {}
    previous = []
    for rel in own_last:
        x = group_joined[rel]
        if rel == 0:
            previous = previous + cot_near
        x = [after(x[0], *previous), *x[1:]]
        low, qkv, lse, mixed, part = attn_forward(
            x, gain_one, bias_one, qkv_off, ok_rows[rel : rel + 1], attn_w, part_type(rel)
        )
        attn[rel] = (low, qkv, lse, mixed)
        middle_parts[rel] = swap(part, rel)
        previous = [lse]
    middle, second_own = middle_norm(
        tokens, [middle_parts[rel] for rel in rels], out_off, gain_two, bias_two
    )
    def ordered(values):
        return [values[rel] for rel in own_last]

    second_near = spread_near(second_own)
    hidden_own, slope_own = ffn_hidden([[second_own]], up_off, up_w)
    group_second = spread_far(second_own, second_near, hidden_own)
    group_cot = spread_far(cotangent, cot_near, hidden_own, second_near)
    hidden, slope = {0: hidden_own[0]}, {0: slope_own[0]}
    previous = hidden_own
    cuts = [1, members - 1, members] if members > 2 else [1, members]
    for low_rel, high_rel in zip(cuts, cuts[1:]):
        some = rels[low_rel:high_rel]
        seconds = [group_second[rel] for rel in some]
        seconds[0] = [after(seconds[0][0], *previous), *seconds[0][1:]]
        hiddens, slopes = ffn_hidden(seconds, up_off, up_w)
        for rel, one, other in zip(some, hiddens, slopes):
            hidden[rel], slope[rel] = one, other
        previous = hiddens[:1]
    down_partial = weight_grad(ordered(hidden), flat_list(ordered(group_cot)))
    down_share = scatter_dp(down_partial, 0)
    down_grad = down_share.astype(F32)
    pre, up_sums, second_parts = [], [], {}
    for some in (own_last[:-1], [0]):
        if not some:
            continue
        cots = [group_cot[rel] for rel in some]
        cots[0] = [after(cots[0][0], *(pre[-1:] or [down_partial])), *cots[0][1:]]
        pre_some, sums, *backs = ffn_back(
            cots, [slope[rel] for rel in some], up_w, down_w, [part_type(rel) for rel in some]
        )
        pre.append(pre_some)
        up_sums.append(sums)
        for rel, back in zip(some, backs):
            second_parts[rel] = swap(back, rel)
    up_partial = weight_grad(flat_list(ordered(group_second)), pre)
    def to_row_blocks(grad):
        return scatter_dp(grad.reshape(members, columns * row_share, -1), 1)

    hiddens = ordered(hidden)
    hiddens[0] = after(hiddens[0], up_partial)
    output_parts = ffn_out(hiddens, down_w, [part_type(rel) for rel in own_last])
    second_parts = after(second_parts, output_parts)
    up_share = to_row_blocks(after(up_partial, second_parts))
    middle_grad, branch_low, middle_sums = middle_back(
        middle, cotangent, [second_parts[rel] for rel in rels], gain_two
    )

    branch_near = spread_near(branch_low)
    grads, qkv_sums, joined_parts = {}, {}, {}

    def back_of(rel, x, *others):
        _, qkv, lse, _ = attn[rel]
        x = [after(x[0], *others), *x[1:]]
        grads[rel], qkv_sums[rel], part = attn_backward(
            x, qkv, lse, ok_cols[rel], attn_w, part_type(rel)
        )
        joined_parts[rel] = swap(part, rel)

    back_of(0, [branch_low], down_share)
    group_branch = spread_far(branch_low, branch_near, qkv_sums[0])
    order = [0] + ([1, 3, 2] if members == 4 else rels[1:])
    for last, rel in zip(order, order[1:]):
        back_of(rel, group_branch[rel], qkv_sums[last])
    attn_partial = attn_weight_grad(
        [attn[rel][0] for rel in rels],
        [grads[rel] for rel in rels],
        [attn[rel][3] for rel in rels],
        flat_list(group_branch),
    )
    joined_parts = after(joined_parts, attn_partial)
    attn_share = to_row_blocks(after(attn_partial, up_share))
    output_parts = {
        rel: swap(part, rel)
        for rel, part in zip(own_last, after(output_parts, joined_parts))
    }
    out_grad = (
        attn_share[:, :, 3 * my_cols :].swapaxes(0, 1).reshape(row_share, width).astype(F32)
    )
    qkv_shares = trade_blocks(attn_share[:, :, : 3 * my_cols])
    query_mat_grad, key_mat_grad, value_mat_grad = [
        qkv_shares[:, :, part * my_cols : (part + 1) * my_cols]
        .swapaxes(0, 1)
        .reshape(row_share, width)
        .astype(F32)
        for part in range(3)
    ]
    tokens_grad, prior_part, first_sums = first_back(
        joined, [joined_parts[rel] for rel in rels], middle_grad, gain_one
    )
    summary_grad = lax.ppermute(
        prior_part[:n_summary], BOTH, [(i + 1, i) for i in range(total - 1)]
    ).astype(F32)
    def whole(value):
        return value.reshape(total, -1)

    def sliced(value):
        mine = value.reshape(columns, -1)
        full = jnp.zeros((total, mine.shape[1]), F32)
        return lax.dynamic_update_slice_in_dim(full, mine, me * columns, 0)

    qkv_sum = sum(qkv_sums[rel] for rel in rels)
    pieces = [
        whole(first_sums[0]),
        whole(first_sums[1]),
        sliced(qkv_sum[:, :my_cols]),
        sliced(qkv_sum[:, 2 * my_cols :]),
        whole(middle_sums[2]),
        whole(middle_sums[0]),
        whole(middle_sums[1]),
        sliced(sum(up_sums)),
        whole(middle_sums[3]),
    ]
    share = scatter_small(after(jnp.concatenate(pieces, 1), output_parts))
    up_blocks = trade_blocks(after(up_share, share))
    up_grad = up_blocks.swapaxes(0, 1).reshape(row_share, members * my_ff).astype(F32)
    output_sum = sum(output_parts[rel].astype(F32) for rel in rels)
    output = (middle + output_sum + down_off).astype(BF16)
    outs = []
    at = 0
    for piece in pieces:
        outs.append(share[at : at + piece.shape[1]])
        at += piece.shape[1]
    return (
        output,
        tokens_grad,
        summary_grad[None],
        outs[0],
        outs[1],
        query_mat_grad,
        outs[2],
        key_mat_grad,
        value_mat_grad,
        outs[3],
        out_grad,
        outs[4],
        outs[5],
        outs[6],
        up_grad,
        outs[7],
        down_grad,
        outs[8],
    )


def solution(mesh):
    rows, rows2, rows3 = P(BOTH), P(BOTH, None), P(BOTH, None, None)
    return jax.shard_map(
        shards,
        mesh=mesh,
        in_specs=(
            rows2, rows3, rows2, P(), rows, rows, rows2, rows, rows2, rows2, rows, rows2, rows,
            rows, rows, rows2, rows, rows2, rows, rows2,
        ),
        out_specs=(
            rows2, rows2, rows3, rows, rows, rows2, rows, rows2, rows2, rows, rows2, rows, rows,
            rows, rows2, rows, rows2, rows,
        ),
        check_vma=False,
    )
```

```python
import functools
import jax
import jax.numpy as jnp
from jax import lax
from jax.experimental import pallas as pl
from jax.experimental.pallas import tpu as pltpu
from jax.sharding import PartitionSpec as P

F32, BF16 = jnp.float32, jnp.bfloat16
HEADS = 32
BOTH = ("fsdp", "dp")
HEAD = 64
PAIR = 2 * HEAD
PRIOR_ROWS = 64
NORM_ROWS = 64
MASKED = -1e30
GELU_A, GELU_B = 0.7978845608028654, 0.044715
VMEM_LIMIT = 60 * 1024 * 1024
VMEM = pl.BlockSpec(memory_space=pltpu.VMEM)
HBM = pl.BlockSpec(memory_space=pl.ANY)


def dot(left, right):
    return jnp.dot(left, right, preferred_element_type=F32)


def dot_t(left, right):
    return lax.dot_general(left, right, (((1,), (1,)), ((), ())), preferred_element_type=F32)


def t_dot(left, right):
    return lax.dot_general(left, right, (((0,), (0,)), ((), ())), preferred_element_type=F32)


def norm_parts(values):
    centre = values - jnp.mean(values, axis=-1, keepdims=True)
    spread = jnp.mean(centre * centre, axis=-1, keepdims=True)
    return centre, lax.rsqrt(spread + 1e-05)


def norm_apply(values, norm_gain, norm_bias):
    centre, inverse = norm_parts(values)
    return centre * inverse * norm_gain + norm_bias


def in_pair(half, rows):
    lane = lax.broadcasted_iota(jnp.int32, (rows, PAIR), 1)
    return (lane >= HEAD) if half else (lane < HEAD)


def pair_at(base, pair):
    return pl.ds(pl.multiple_of(base + pair * PAIR, PAIR), PAIR)


def load_blocks(hbm, scratch, sems):
    copies = [
        pltpu.make_async_copy(hbm.at[:, block], scratch.at[block], sems.at[block])
        for block in range(scratch.shape[0])
    ]
    for copy in copies:
        copy.start()
    return copies


def load_rows(parts, scratch, sems):
    copies = []
    at = 0
    for index, part in enumerate(parts):
        rows = part.shape[0]
        copies.append(
            pltpu.make_async_copy(part, scratch.at[pl.ds(at, rows)], sems.at[index])
        )
        at += rows
    for copy in copies:
        copy.start()
    return copies


def flat_list(lists):
    return [piece for some in lists for piece in some]


def wait_all(copies):
    for copy in copies:
        copy.wait()


def rows_of(ref, columns):
    value = ref[:, :, :, columns]
    return value.reshape(-1, value.shape[-1])


def block_of(ref, block, columns):
    value = ref[block, :, :, columns]
    return value.reshape(-1, value.shape[-1])


COST = 1_000_000


def kernel_params(cost):
    return dict(
        compiler_params=pltpu.CompilerParams(vmem_limit_bytes=VMEM_LIMIT),
        cost_estimate=pl.CostEstimate(flops=cost * COST, bytes_accessed=1, transcendentals=0),
    )


def shape_of(rows, columns, dtype=BF16):
    return jax.ShapeDtypeStruct((rows, columns), dtype)


def attn_forward(xs, gain, bias, off, ok_rows, attn_w, types):
    count = len(xs)
    pieces = flat_list(xs)
    given = len(pieces)
    keys, width = sum(piece.shape[0] for piece in xs[0]), pieces[0].shape[1]
    seg = keys - PRIOR_ROWS
    columns, members, share, wide = attn_w.shape
    cols = wide // 4

    def kernel(*refs):
        gain_ref, bias_ref, off_ref, ok_ref, attn_hbm = refs[given : given + 5]
        outs = refs[given + 5 : given + 5 + 5 * count]
        x_all, weights, mask, sems = refs[given + 5 + 5 * count :]
        x_copies = load_rows(refs[:given], x_all, sems.at[pl.ds(members, given)])
        copies = load_blocks(attn_hbm, weights, sems)
        gain, bias = gain_ref[...], bias_ref[...]
        wait_all(x_copies)
        for index in range(count):
            low_ref = outs[5 * index]

            def norm_rows(block, _):
                start = pl.multiple_of(block * NORM_ROWS, NORM_ROWS)
                values = x_all[pl.ds(index * keys + start, NORM_ROWS), :].astype(F32)
                low_ref[pl.ds(start, NORM_ROWS), :] = norm_apply(values, gain, bias).astype(BF16)
                return _

            lax.fori_loop(0, keys // NORM_ROWS, norm_rows, 0)
        wait_all(copies)
        for index in range(count):
            attend_segment(ok_ref[index : index + 1, :], off_ref, weights, mask, outs[5 * index : 5 * index + 5])

    def attend_segment(ok_row, off_ref, weights, mask, refs):
        low_ref, qkv_ref, lse_ref, mixed_ref, part_ref = refs
        row = lax.broadcasted_iota(jnp.int32, (seg, keys), 0)
        col = lax.broadcasted_iota(jnp.int32, (seg, keys), 1)
        mask[...] = jnp.where(jnp.logical_or(col <= row, ok_row > 0.5), 0.0, MASKED)

        def project(part, _):
            at = pl.ds(pl.multiple_of(part * cols, PAIR), cols)
            value = dot(low_ref[...], rows_of(weights, at)) + off_ref[:, at]
            qkv_ref[:, at] = value.astype(BF16)
            return _

        lax.fori_loop(0, 3, project, 0)
        lane = lax.broadcasted_iota(jnp.int32, (seg, PAIR), 1)

        def attend(pair, _):
            query = qkv_ref[:seg, pair_at(0, pair)] * jnp.asarray(HEAD**-0.5, BF16)
            key = qkv_ref[:, pair_at(cols, pair)]
            value = qkv_ref[:, pair_at(2 * cols, pair)]
            merged = None
            for half in range(2):
                inside = in_pair(half, seg)
                scores = dot_t(jnp.where(inside, query, jnp.zeros_like(query)), key) + mask[...]
                row_max = jnp.max(scores, axis=-1, keepdims=True)
                expo = jnp.exp(scores - row_max)
                row_total = jnp.sum(expo, axis=-1, keepdims=True)
                log_total = row_max + jnp.log(row_total)
                lse_ref[...] = jnp.where(lane == 2 * pair + half, log_total, lse_ref[...])
                mixed = dot((expo * (1.0 / row_total)).astype(BF16), value)
                merged = mixed if merged is None else jnp.where(inside, mixed, merged)
            mixed_ref[:, pair_at(0, pair)] = merged.astype(BF16)
            return _

        lse_ref[...] = jnp.zeros_like(lse_ref)
        lax.fori_loop(0, cols // PAIR, attend, 0)

        def project_out(block, _):
            at = pl.ds(pl.multiple_of(block * cols, PAIR), cols)
            weight = block_of(weights, block, pl.ds(3 * cols, cols))
            part_ref[:, at] = dot(mixed_ref[...], weight).astype(part_ref.dtype)
            return _

        lax.fori_loop(0, members, project_out, 0)

    shapes = []
    for dtype in types:
        shapes += [
            shape_of(keys, width),
            shape_of(keys, 3 * cols),
            shape_of(seg, PAIR, F32),
            shape_of(seg, cols),
            shape_of(seg, width, dtype),
        ]
    outs = pl.pallas_call(
        kernel,
        out_shape=shapes,
        in_specs=[HBM] * given + [VMEM] * 4 + [HBM],
        out_specs=[VMEM] * len(shapes),
        scratch_shapes=[
            pltpu.VMEM((count * keys, width), BF16),
            pltpu.VMEM((members, columns, share, wide), BF16),
            pltpu.VMEM((seg, keys), F32),
            pltpu.SemaphoreType.DMA((members + given,)),
        ],
        name="attn_forward",
        **kernel_params(12 * count),
    )(*pieces, gain, bias, off, ok_rows, attn_w)
    return [outs[5 * index : 5 * index + 5] for index in range(count)]


def attn_backward(branches, qkvs, lses, ok_cols, attn_w, types):
    count = len(branches)
    pieces = flat_list(branches)
    given = len(pieces)
    seg, width = sum(piece.shape[0] for piece in branches[0]), pieces[0].shape[1]
    keys = qkvs[0].shape[0]
    columns, members, share, wide = attn_w.shape
    cols = wide // 4

    def kernel(*refs):
        ins = refs[given : given + 3 * count]
        attn_hbm = refs[given + 3 * count]
        outs = refs[given + 3 * count + 1 : given + 6 * count + 1]
        branch_all, weights, mask, lse_t, mixed_grad, sems = refs[given + 6 * count + 1 :]
        branch_copies = load_rows(refs[:given], branch_all, sems.at[pl.ds(members, given)])
        copies = load_blocks(attn_hbm, weights, sems)
        wait_all(branch_copies)
        for index in range(count):
            branch = branch_all.at[pl.ds(index * seg, seg)]
            some_in = [ins[index], ins[count + index], ins[2 * count + index]]
            some_out = outs[3 * index : 3 * index + 3]
            waits = copies if index == 0 else []
            back_segment(branch, *some_in, *some_out, weights, mask, lse_t, mixed_grad, waits)

    def back_segment(
        branch_ref, qkv_ref, lse_ref, ok_ref, grads_ref, sums_ref, joined_ref,
        weights, mask, lse_t, mixed_grad, waits,
    ):
        row = lax.broadcasted_iota(jnp.int32, (keys, seg), 0)
        col = lax.broadcasted_iota(jnp.int32, (keys, seg), 1)
        mask[...] = jnp.where(jnp.logical_or(row <= col, ok_ref[:, :1] > 0.5), 0.0, MASKED)
        lse_t[...] = lse_ref[...].T
        grads_ref[seg:, :cols] = jnp.zeros((keys - seg, cols), BF16)
        total = 0.0
        for block in range(members):
            wait_all(waits[block : block + 1])
            weight = block_of(weights, block, pl.ds(3 * cols, cols))
            total = total + dot_t(branch_ref[:, block * cols : (block + 1) * cols], weight)
        mixed_grad[...] = total.astype(BF16)

        def attend(pair, _):
            query = qkv_ref[:seg, pair_at(0, pair)]
            scaled = query * jnp.asarray(HEAD**-0.5, BF16)
            key = qkv_ref[:, pair_at(cols, pair)]
            value = qkv_ref[:, pair_at(2 * cols, pair)]
            mixed = mixed_grad[:, pair_at(0, pair)]
            query_grad = key_grad = value_grad = 0.0
            for half in range(2):
                inside, inside_key = in_pair(half, seg), in_pair(half, keys)
                zero = jnp.zeros_like(query)
                scores = dot_t(key, jnp.where(inside, scaled, zero)) + mask[...]
                probs = jnp.exp(scores - lse_t[pl.ds(2 * pair + half, 1), :])
                mixed_half = jnp.where(inside, mixed, zero)
                prob_grad = dot_t(value, mixed_half)
                value_grad = value_grad + dot(probs.astype(BF16), mixed_half)
                delta = jnp.sum(prob_grad * probs, axis=0, keepdims=True)
                score_grad = (probs * (prob_grad - delta)).astype(BF16)
                key_grad = key_grad + dot(score_grad, jnp.where(inside, query, zero))
                key_half = jnp.where(inside_key, key, jnp.zeros_like(key))
                query_grad = query_grad + t_dot(score_grad, key_half)
            grads_ref[:seg, pair_at(0, pair)] = (query_grad * HEAD**-0.5).astype(BF16)
            grads_ref[:, pair_at(cols, pair)] = (key_grad * HEAD**-0.5).astype(BF16)
            grads_ref[:, pair_at(2 * cols, pair)] = value_grad.astype(BF16)
            return _

        lax.fori_loop(0, cols // PAIR, attend, 0)

        def back(block, _):
            weight = block_of(weights, block, pl.ds(0, 3 * cols))
            at = pl.ds(pl.multiple_of(block * cols, PAIR), cols)
            joined_ref[:, at] = dot_t(grads_ref[...], weight).astype(joined_ref.dtype)
            return _

        lax.fori_loop(0, members, back, 0)
        sums_ref[...] = jnp.sum(grads_ref[...].astype(F32), axis=0, keepdims=True)

    shapes = []
    for dtype in types:
        shapes += [
            shape_of(keys, 3 * cols),
            shape_of(1, 3 * cols, F32),
            shape_of(keys, width, dtype),
        ]
    outs = pl.pallas_call(
        kernel,
        out_shape=shapes,
        in_specs=[HBM] * given + [VMEM] * (3 * count) + [HBM],
        out_specs=[VMEM] * len(shapes),
        scratch_shapes=[
            pltpu.VMEM((count * seg, width), BF16),
            pltpu.VMEM((members, columns, share, wide), BF16),
            pltpu.VMEM((keys, seg), F32),
            pltpu.VMEM((PAIR, seg), F32),
            pltpu.VMEM((seg, cols), BF16),
            pltpu.SemaphoreType.DMA((members + given,)),
        ],
        name="attn_backward",
        **kernel_params(12 * count),
    )(*pieces, *qkvs, *lses, *ok_cols, attn_w)
    return [outs[3 * index : 3 * index + 3] for index in range(count)]


def ffn_hidden(seconds, off, up_w):
    pieces = flat_list(seconds)
    given = len(pieces)
    width = pieces[0].shape[1]
    count = len(seconds)
    seg = sum(piece.shape[0] for piece in pieces) // count
    columns, members, share, wide = up_w.shape
    step = 512

    def kernel(*refs):
        off_ref, up_hbm = refs[given : given + 2]
        outs = refs[given + 2 : given + 2 + 2 * count]
        second, up, sems = refs[given + 2 + 2 * count :]
        copies = load_blocks(up_hbm, up, sems)
        wait_all(copies + load_rows(refs[:given], second, sems.at[pl.ds(members, given)]))

        def hidden(block, _):
            at = pl.ds(pl.multiple_of(block * step, step), step)
            weight = rows_of(up, at)
            for index in range(count):
                pre = dot(second[pl.ds(index * seg, seg), :], weight) + off_ref[:, at]
                square = pre * pre
                bent = jnp.tanh(GELU_A * pre * (1.0 + GELU_B * square))
                gate = 0.5 * (1.0 + bent)
                outs[index][:, at] = (pre * gate).astype(BF16)
                rise = 0.5 * pre * (1.0 - bent * bent) * (GELU_A * (1.0 + 3.0 * GELU_B * square))
                outs[count + index][:, at] = (gate + rise).astype(BF16)
            return _

        lax.fori_loop(0, wide // step, hidden, 0)

    outs = pl.pallas_call(
        kernel,
        out_shape=[shape_of(seg, wide)] * (2 * count),
        in_specs=[HBM] * given + [VMEM, HBM],
        out_specs=[VMEM] * (2 * count),
        scratch_shapes=[
            pltpu.VMEM((count * seg, width), BF16),
            pltpu.VMEM((members, columns, share, wide), BF16),
            pltpu.SemaphoreType.DMA((members + given,)),
        ],
        name="ffn_hidden",
        **kernel_params(6 * count),
    )(*pieces, off, up_w)
    return outs[:count], outs[count:]


def ffn_back(cots, slopes, up_w, down_w, types):
    pieces = flat_list(cots)
    given = len(pieces)
    count = len(slopes)
    seg, width = slopes[0].shape[0], pieces[0].shape[1]
    columns, members, share, wide = up_w.shape
    step = 512
    rows = count * seg
    loads = given + count

    def kernel(*refs):
        up_hbm, down_hbm, pre_ref, sums_ref = refs[loads : loads + 4]
        backs = refs[loads + 4 : loads + 4 + count]
        cot, slope, up, down, sems = refs[loads + 4 + count :]
        first = load_rows(refs[:given], cot, sems)
        first += load_rows([down_hbm], down, sems.at[pl.ds(loads, 1)])
        first += load_rows(refs[given:loads], slope, sems.at[pl.ds(given, count)])
        later = load_blocks(up_hbm, up, sems.at[pl.ds(loads + 1, members)])
        wait_all(first)

        def grad(block, _):
            at = pl.ds(pl.multiple_of(block * step, step), step)
            value = dot_t(cot[...], down[at, :]) * slope[:, at].astype(F32)
            value = value.astype(BF16)
            pre_ref[:, at] = value
            sums_ref[:, at] = jnp.sum(value.astype(F32), axis=0, keepdims=True)
            return _

        lax.fori_loop(0, wide // step, grad, 0)
        wait_all(later)
        deep = columns * share

        def back(block, _):
            at = pl.ds(pl.multiple_of(block * deep, PAIR), deep)
            value = dot_t(pre_ref[...], up[block].reshape(deep, wide))
            for index in range(count):
                backs[index][:, at] = value[index * seg : (index + 1) * seg].astype(types[index])
            return _

        lax.fori_loop(0, members, back, 0)

    return pl.pallas_call(
        kernel,
        out_shape=(
            shape_of(rows, wide),
            shape_of(1, wide, F32),
            *[shape_of(seg, width, dtype) for dtype in types],
        ),
        in_specs=[HBM] * (loads + 2),
        out_specs=(VMEM,) * (2 + count),
        scratch_shapes=[
            pltpu.VMEM((rows, width), BF16),
            pltpu.VMEM((rows, wide), BF16),
            pltpu.VMEM((members, columns, share, wide), BF16),
            pltpu.VMEM((wide, width), BF16),
            pltpu.SemaphoreType.DMA((loads + 1 + members,)),
        ],
        name="ffn_back",
        **kernel_params(10 * count),
    )(*pieces, *slopes, up_w, down_w)


def ffn_out(hiddens, down_w, types):
    count = len(types)
    seg, wide = hiddens[0].shape
    rows = seg // 2
    width = down_w.shape[1]
    step = 512

    def kernel(*refs):
        down_ref = refs[count]
        outs = refs[count + 1 : 3 * count + 1]
        hidden, sems = refs[3 * count + 1 :]
        wait_all(load_rows(refs[:count], hidden, sems))

        def block(part, _):
            at = pl.ds(pl.multiple_of(part * step, step), step)
            value = dot(hidden[...], down_ref[:, at])
            for index in range(2 * count):
                half = value[index * rows : (index + 1) * rows]
                outs[index][:, at] = half.astype(types[index // 2])
            return _

        lax.fori_loop(0, width // step, block, 0)

    outs = pl.pallas_call(
        kernel,
        out_shape=[shape_of(rows, width, types[index // 2]) for index in range(2 * count)],
        in_specs=[HBM] * count + [VMEM],
        out_specs=[VMEM] * (2 * count),
        scratch_shapes=[
            pltpu.VMEM((count * seg, wide), BF16),
            pltpu.SemaphoreType.DMA((count,)),
        ],
        name="ffn_out",
        **kernel_params(18),
    )(*hiddens, down_w)
    return [outs[2 * index : 2 * index + 2] for index in range(count)]


GRAD_ROWS = 256


def weight_grad(lefts, rights):
    tall, wide = lefts[0].shape[1], rights[0].shape[1]
    deep = sum(left.shape[0] for left in lefts)
    counts = len(lefts), len(rights)
    both = sum(counts)

    def kernel(*refs):
        out_ref, left, right, sems = refs[both:]
        step = pl.program_id(0)

        @pl.when(step == 0)
        def _():
            copies = load_rows(refs[: counts[0]], left, sems)
            wait_all(copies + load_rows(refs[counts[0] : both], right, sems.at[pl.ds(counts[0], counts[1])]))

        at = pl.ds(pl.multiple_of(step * GRAD_ROWS, GRAD_ROWS), GRAD_ROWS)
        out_ref[...] = t_dot(left[:, at], right[...]).astype(BF16)

    return pl.pallas_call(
        kernel,
        grid=(tall // GRAD_ROWS,),
        out_shape=shape_of(tall, wide),
        in_specs=[HBM] * both,
        out_specs=pl.BlockSpec((GRAD_ROWS, wide), lambda i: (i, 0)),
        scratch_shapes=[
            pltpu.VMEM((deep, tall), BF16),
            pltpu.VMEM((deep, wide), BF16),
            pltpu.SemaphoreType.DMA((both,)),
        ],
        name="weight_grad",
        **kernel_params(17),
    )(*lefts, *rights)


def attn_weight_grad(lows, grads, mixeds, branches):
    lists = lows, grads, mixeds, branches
    width, cols = lows[0].shape[1], mixeds[0].shape[1]
    halves = cols // GRAD_ROWS
    ends = [0]
    for some in lists:
        ends.append(ends[-1] + len(some))

    def kernel(*refs):
        out_ref, low, grad, mixed, branch, sems = refs[ends[-1] :]
        step = pl.program_id(0)

        @pl.when(step == 0)
        def _():
            copies = []
            for first, last, scratch in zip(ends, ends[1:], (low, grad, mixed, branch)):
                copies += load_rows(refs[first:last], scratch, sems.at[pl.ds(first, last - first)])
            wait_all(copies)

        at = pl.ds(pl.multiple_of(step * GRAD_ROWS, GRAD_ROWS), GRAD_ROWS)
        out_ref[:, : 3 * cols] = t_dot(low[:, at], grad[...]).astype(BF16)
        half = pl.ds(pl.multiple_of((step % halves) * GRAD_ROWS, GRAD_ROWS), GRAD_ROWS)
        block = pl.ds(pl.multiple_of((step // halves) * cols, PAIR), cols)
        out_ref[:, 3 * cols :] = t_dot(mixed[:, half], branch[:, block]).astype(BF16)

    return pl.pallas_call(
        kernel,
        grid=(width // GRAD_ROWS,),
        out_shape=shape_of(width, 4 * cols),
        in_specs=[HBM] * ends[-1],
        out_specs=pl.BlockSpec((GRAD_ROWS, 4 * cols), lambda i: (i, 0)),
        scratch_shapes=[
            pltpu.VMEM((sum(one.shape[0] for one in some), some[0].shape[1]), BF16)
            for some in lists
        ]
        + [pltpu.SemaphoreType.DMA((ends[-1],))],
        name="attn_weight_grad",
        **kernel_params(21),
    )(*lows, *grads, *mixeds, *branches)


def norm_values(values):
    centre, inverse = norm_parts(values)
    return centre * inverse, inverse


def norm_back(hat, inverse, grad, gain):
    hat_grad = grad * gain
    mean = jnp.mean(hat_grad, axis=-1, keepdims=True)
    along = jnp.mean(hat_grad * hat, axis=-1, keepdims=True)
    return inverse * (hat_grad - mean - hat * along)


def column_sum(value):
    return jnp.sum(value, axis=0, keepdims=True)


def row_blocks(width, last=None, rows=NORM_ROWS):
    if last is None:
        return pl.BlockSpec((rows, width), lambda i: (i, 0))
    return pl.BlockSpec((rows, width), lambda i: (jnp.minimum(i, last), 0))


def store_half(refs, value):
    for half, ref in enumerate(refs):

        @pl.when(pl.program_id(0) == half)
        def _(ref=ref):
            ref[...] = value


def kept(rows, width):
    return pl.BlockSpec((rows, width), lambda i: (0, 0))


def sum_parts(parts):
    total = parts[0][...].astype(F32)
    for part in parts[1:]:
        total = total + part[...].astype(F32)
    return total


def middle_norm(tokens, parts, off, gain, bias):
    seg, width = tokens.shape
    count = len(parts)

    rows = seg // 2

    def kernel(*refs):
        off_ref, gain_ref, bias_ref, middle_ref, *seconds = refs[count + 1 :]
        total = sum_parts(refs[: count + 1]) + off_ref[...]
        middle_ref[...] = total
        store_half(seconds, norm_apply(total, gain_ref[...], bias_ref[...]).astype(BF16))

    return pl.pallas_call(
        kernel,
        grid=(2,),
        out_shape=(shape_of(seg, width, F32), shape_of(rows, width), shape_of(rows, width)),
        in_specs=[row_blocks(width, rows=rows)] * (count + 1) + [kept(1, width)] * 3,
        out_specs=(row_blocks(width, rows=rows), kept(rows, width), kept(rows, width)),
        name="middle_norm",
        **kernel_params(5),
    )(tokens, *parts, off, gain, bias)


def middle_back(middle, cot, parts, gain):
    seg, width = middle.shape
    count = len(parts)
    rows = seg // 2

    def kernel(*refs):
        middle_ref, cot_ref, gain_ref, grad_ref, top_ref, bottom_ref, sums_ref = refs[count:]

        @pl.when(pl.program_id(0) == 0)
        def _():
            sums_ref[...] = jnp.zeros_like(sums_ref)

        grad = sum_parts(refs[:count])
        hat, inverse = norm_values(middle_ref[...])
        cots = cot_ref[...].astype(F32)
        total = cots + norm_back(hat, inverse, grad, gain_ref[...])
        low = total.astype(BF16)
        grad_ref[...] = total
        store_half([top_ref, bottom_ref], low)
        sums_ref[0:1, :] += column_sum(grad * hat)
        sums_ref[1:2, :] += column_sum(grad)
        sums_ref[2:3, :] += column_sum(low.astype(F32))
        sums_ref[3:4, :] += column_sum(cots)

    return pl.pallas_call(
        kernel,
        grid=(2,),
        out_shape=(
            shape_of(seg, width, F32),
            shape_of(rows, width),
            shape_of(rows, width),
            shape_of(4, width, F32),
        ),
        in_specs=[row_blocks(width, rows=rows)] * (count + 2) + [kept(1, width)],
        out_specs=(
            row_blocks(width, rows=rows),
            kept(rows, width),
            kept(rows, width),
            kept(4, width),
        ),
        name="middle_back",
        **kernel_params(5),
    )(*parts, middle, cot, gain)


def first_back(joined, parts, middle_grad, gain):
    seg, width = middle_grad.shape
    keys = joined.shape[0]
    count = len(parts)
    last = seg // NORM_ROWS - 1

    def kernel(*refs):
        joined_ref, middle_ref, gain_ref, tokens_ref, prior_ref, sums_ref = refs[count:]
        step = pl.program_id(0)

        @pl.when(step == 0)
        def _():
            sums_ref[...] = jnp.zeros_like(sums_ref)

        grad = sum_parts(refs[:count])
        hat, inverse = norm_values(joined_ref[...].astype(F32))
        sums_ref[0:1, :] += column_sum(grad * hat)
        sums_ref[1:2, :] += column_sum(grad)
        back = norm_back(hat, inverse, grad, gain_ref[...])

        @pl.when(step <= last)
        def _():
            tokens_ref[...] = middle_ref[...] + back

        @pl.when(step > last)
        def _():
            prior_ref[...] = back.astype(BF16)

    return pl.pallas_call(
        kernel,
        grid=(keys // NORM_ROWS,),
        out_shape=(
            shape_of(seg, width, F32),
            shape_of(keys - seg, width),
            shape_of(2, width, F32),
        ),
        in_specs=[row_blocks(width)] * (count + 1) + [row_blocks(width, last), kept(1, width)],
        out_specs=(row_blocks(width, last), kept(keys - seg, width), kept(2, width)),
        name="first_back",
        **kernel_params(500_000),
    )(*parts, joined, middle_grad, gain)


def swap(value, rel):
    if rel == 0:
        return value
    count = lax.axis_size("fsdp")
    return lax.ppermute(value, "fsdp", [(i, i ^ rel) for i in range(count)])


def halves_of(value):
    rows = value.shape[0] // 2
    return [value[:rows], value[rows:]]


def spread_near(halves):
    near = range(1, min(lax.axis_size("fsdp"), 3))
    return [[swap(half, rel) for half in halves] for rel in near]


def spread_far(halves, near, *others):
    members = lax.axis_size("fsdp")
    near = lax.optimization_barrier((near, others))[0]
    pieces = [halves, *near]
    if members > 3:
        top, bottom = near[0][0], near[1][-1]
        if len(halves) == 1:
            top, bottom = halves_of(top)[0], halves_of(bottom)[1]
        pieces.append([swap(top, 2), swap(bottom, 1)])
    return pieces + [[swap(half, rel) for half in halves] for rel in range(4, members)]


def after(value, *others):
    return lax.optimization_barrier((value, *others))[0]


def add_low(left, right):
    return (left.astype(F32) + right.astype(F32)).astype(BF16)


def trade_blocks(blocks):
    return lax.all_to_all(blocks, "fsdp", 0, 0, tiled=True)


def doubled(rows, axis):
    size = lax.axis_size(axis)
    place = lax.axis_index(axis)
    step = 1
    while step < size:
        came = lax.ppermute(rows, axis, [(i, i ^ step) for i in range(size)])
        high = (place & step) != 0
        rows = jnp.concatenate([jnp.where(high, came, rows), jnp.where(high, rows, came)], 0)
        step *= 2
    return rows


def scatter_small(rows):
    return jnp.sum(lax.all_to_all(rows, BOTH, 0, 0, tiled=True), axis=0)


def gather_dp(value):
    return lax.all_gather(value, "dp", axis=0, tiled=True)


def scatter_dp(value, axis):
    return lax.psum_scatter(value, "dp", scatter_dimension=axis, tiled=True)


def shards(
    tokens,
    summaries,
    presence,
    seg_counts,
    ln1_gain,
    ln1_bias,
    w_query,
    query_bias,
    w_key,
    w_value,
    value_bias,
    w_out,
    out_bias,
    ln2_gain,
    ln2_bias,
    w_up,
    up_bias,
    w_down,
    down_bias,
    cotangent,
):
    members = lax.axis_size("fsdp")
    columns = lax.axis_size("dp")
    total = members * columns
    me = lax.axis_index("fsdp")
    seg_len, width = tokens.shape
    n_summary = summaries.shape[1]
    my_cols = width // members
    my_ff = w_up.shape[1] // members
    row_share = w_query.shape[0]
    rels = list(range(members))
    own_last = rels[::-1]

    def blocks_of(weight):
        return weight.reshape(row_share, members, -1).swapaxes(0, 1)

    def gathered(blocks):
        rows = blocks.reshape(members * row_share, -1)
        return gather_dp(rows).reshape(columns, members, row_share, -1)

    small_parts = (
        ln1_gain, ln1_bias, query_bias, value_bias, out_bias, ln2_gain, ln2_bias, up_bias,
        down_bias, presence[0].astype(BF16),
    )
    packed = doubled(jnp.concatenate(small_parts)[None], "fsdp")
    prior = jnp.pad(summaries[0], ((0, PRIOR_ROWS - n_summary), (0, 0)))
    prior = lax.ppermute(prior, BOTH, [(i, i + 1) for i in range(total - 1)])
    joined = jnp.concatenate([tokens, prior], 0)

    qkv_blocks = jnp.concatenate([blocks_of(w_query), blocks_of(w_key), blocks_of(w_value)], 2)
    qkv_blocks = trade_blocks(qkv_blocks)
    up_blocks, packed = lax.optimization_barrier((blocks_of(w_up), packed, qkv_blocks, joined))[:2]
    up_blocks = trade_blocks(up_blocks)
    attn_w = gathered(jnp.concatenate([qkv_blocks, blocks_of(w_out)], 2))
    up_w = gathered(up_blocks)
    down_w = gather_dp(w_down)

    joined_rows = [joined]
    joined_near = spread_near(after(joined_rows, up_blocks))
    group_joined = spread_far(joined_rows, joined_near)
    cot_rows = [cotangent]
    cot_near = spread_near(after(cot_rows, group_joined))
    packed = doubled(packed, "dp").reshape(columns, members, -1).swapaxes(0, 1)
    packed = packed.reshape(total, -1)

    smalls = []
    at = 0
    for part in small_parts:
        smalls.append(packed[:, at : at + part.shape[0]].astype(F32))
        at += part.shape[0]
    gain_one, bias_one, query_off, value_off, out_off, gain_two, bias_two, up_off, down_off = [
        part.reshape(1, -1) for part in smalls[:-1]
    ]
    present_all = smalls[-1]
    query_off = lax.dynamic_slice_in_dim(query_off, me * my_cols, my_cols, 1)
    value_off = lax.dynamic_slice_in_dim(value_off, me * my_cols, my_cols, 1)
    up_off = lax.dynamic_slice_in_dim(up_off, me * my_ff, my_ff, 1)
    qkv_off = jnp.concatenate([query_off, jnp.zeros_like(query_off), value_off], 1)

    starts = jnp.cumsum(seg_counts) - seg_counts
    group_places = (me ^ jnp.arange(members)) * columns + lax.axis_index("dp")
    has_prev = jnp.all(group_places[:, None] != starts[None, :], axis=1)
    summary_ok = jnp.logical_and(present_all[group_places] == 1, has_prev[:, None]).astype(F32)
    ok_rows = jnp.pad(summary_ok, ((0, 0), (seg_len, PRIOR_ROWS - n_summary)))
    ok_cols = jnp.broadcast_to(ok_rows[:, :, None], (*ok_rows.shape, PAIR))


    def part_type(rel):
        return BF16 if rel else F32

    attn = {}
    middle_parts = {}
    previous = []
    for some in ([[3], [1, 2], [0]] if members == 4 else [[rel] for rel in own_last]):
        xs = [group_joined[rel] for rel in some]
        if some == [0]:
            previous = previous + flat_list(cot_near)
        xs[0] = [after(xs[0][0], *previous), *xs[0][1:]]
        oks = jnp.concatenate([ok_rows[rel : rel + 1] for rel in some], 0)
        outs = attn_forward(
            xs, gain_one, bias_one, qkv_off, oks, attn_w, [part_type(rel) for rel in some]
        )
        for rel, (low, qkv, lse, mixed, part) in zip(some, outs):
            attn[rel] = (low, qkv, lse, mixed)
            middle_parts[rel] = swap(part, rel)
            previous = [lse]
    middle, *second_own = middle_norm(
        tokens, [middle_parts[rel] for rel in rels], out_off, gain_two, bias_two
    )
    def ordered(values):
        return [values[rel] for rel in own_last]

    second_near = spread_near(second_own)
    hidden_own, slope_own = ffn_hidden([second_own], up_off, up_w)
    group_second = spread_far(second_own, second_near, hidden_own)
    hidden, slope = {0: hidden_own[0]}, {0: slope_own[0]}
    previous = hidden_own
    cuts = [1, members - 1, members] if members > 2 else [1, members]
    for low_rel, high_rel in zip(cuts, cuts[1:]):
        some = rels[low_rel:high_rel]
        seconds = [group_second[rel] for rel in some]
        seconds[0] = [after(seconds[0][0], *previous), *seconds[0][1:]]
        hiddens, slopes = ffn_hidden(seconds, up_off, up_w)
        for rel, one, other in zip(some, hiddens, slopes):
            hidden[rel], slope[rel] = one, other
        previous = hiddens[:1]
        if low_rel == 1:
            group_cot = spread_far(cot_rows, cot_near, previous)
    down_partial = weight_grad(ordered(hidden), flat_list(ordered(group_cot)))
    down_share = scatter_dp(down_partial, 0)
    pre, up_sums, second_parts = [], [], {}
    for some in (own_last[:-1], [0]):
        if not some:
            continue
        cots = [group_cot[rel] for rel in some]
        cots[0] = [after(cots[0][0], *(pre[-1:] or [down_partial])), *cots[0][1:]]
        pre_some, sums, *backs = ffn_back(
            cots, [slope[rel] for rel in some], up_w, down_w, [part_type(rel) for rel in some]
        )
        pre.append(pre_some)
        up_sums.append(sums)
        for rel, back in zip(some, backs):
            second_parts[rel] = swap(back, rel)
    up_partial = weight_grad(flat_list(ordered(group_second)), pre)
    def to_row_blocks(grad):
        return scatter_dp(grad.reshape(members, columns * row_share, -1), 1)

    hiddens = ordered(hidden)
    hiddens[0] = after(hiddens[0], up_partial)
    output_parts = ffn_out(hiddens, down_w, [part_type(rel) for rel in own_last])
    output_parts = dict(zip(own_last, output_parts))
    second_parts = after(second_parts, output_parts)
    up_share = to_row_blocks(after(up_partial, second_parts))
    middle_grad, *branch_low, middle_sums = middle_back(
        middle, cotangent, [second_parts[rel] for rel in rels], gain_two
    )

    branch_near = spread_near(branch_low)
    grads, qkv_sums, joined_parts = {}, {}, {}

    def back_of(some, branches, *others):
        first = [after(branches[0][0], *others), *branches[0][1:]]
        outs = attn_backward(
            [first, *branches[1:]],
            [attn[rel][1] for rel in some],
            [attn[rel][2] for rel in some],
            [ok_cols[rel] for rel in some],
            attn_w,
            [part_type(rel) for rel in some],
        )
        for rel, (grad, sums, part) in zip(some, outs):
            grads[rel], qkv_sums[rel] = grad, sums
            joined_parts[rel] = swap(part, rel)

    back_of([0], [branch_low], down_share)
    group_branch = spread_far(branch_low, branch_near, qkv_sums[0])
    output_over = []
    if members > 3:
        far = after(output_parts.pop(3), qkv_sums[0])
        output_over = [swap(far[0], 1), swap(far[1], 2)]
    last = 0
    for some in ([[1, 2], [3]] if members == 4 else [[rel] for rel in rels[1:]]):
        others = output_over if some == [3] else []
        back_of(some, [group_branch[rel] for rel in some], qkv_sums[last], *others)
        last = some[-1]
    attn_partial = attn_weight_grad(
        [attn[rel][0] for rel in rels],
        [grads[rel] for rel in rels],
        [attn[rel][3] for rel in rels],
        flat_list(group_branch),
    )
    up_blocks = trade_blocks(after(up_share, attn_partial))
    joined_parts = after(joined_parts, attn_partial, up_blocks)
    attn_share = to_row_blocks(after(attn_partial, up_share))
    out_grad = (
        attn_share[:, :, 3 * my_cols :].swapaxes(0, 1).reshape(row_share, width).astype(F32)
    )
    qkv_shares = trade_blocks(attn_share[:, :, : 3 * my_cols])
    query_mat_grad, key_mat_grad, value_mat_grad = [
        qkv_shares[:, :, part * my_cols : (part + 1) * my_cols]
        .swapaxes(0, 1)
        .reshape(row_share, width)
        .astype(F32)
        for part in range(3)
    ]
    tokens_grad, prior_part, first_sums = first_back(
        joined, [joined_parts[rel] for rel in rels], middle_grad, gain_one
    )
    summary_grad = lax.ppermute(
        prior_part[:n_summary], BOTH, [(i + 1, i) for i in range(total - 1)]
    ).astype(F32)
    def whole(value):
        return value.reshape(total, -1)

    def sliced(value):
        mine = value.reshape(columns, -1)
        full = jnp.zeros((total, mine.shape[1]), F32)
        return lax.dynamic_update_slice_in_dim(full, mine, me * columns, 0)

    qkv_sums, middle_sums, up_sums = after((qkv_sums, middle_sums, up_sums), first_sums)
    qkv_sum = sum(qkv_sums[rel] for rel in rels)
    pieces = [
        whole(first_sums[0]),
        whole(first_sums[1]),
        sliced(qkv_sum[:, :my_cols]),
        sliced(qkv_sum[:, 2 * my_cols :]),
        whole(middle_sums[2]),
        whole(middle_sums[0]),
        whole(middle_sums[1]),
        sliced(sum(up_sums)),
        whole(middle_sums[3]),
    ]
    share = scatter_small(jnp.concatenate(pieces, 1))
    output_parts = after(output_parts, share)
    if output_over:
        two, one = output_parts[2], output_parts[1]
        output_parts[2] = [add_low(two[0], output_over[0]), two[1]]
        output_parts[1] = [one[0], add_low(one[1], output_over[1])]
    output_parts = {
        rel: [swap(half, rel) for half in halves] for rel, halves in output_parts.items()
    }
    down_grad = after(down_share, share).astype(F32)
    up_grad = up_blocks.swapaxes(0, 1).reshape(row_share, members * my_ff).astype(F32)
    output_sum = jnp.concatenate(
        [sum(halves[half].astype(F32) for halves in output_parts.values()) for half in range(2)], 0
    )
    output = (middle + output_sum + down_off).astype(BF16)
    outs = []
    at = 0
    for piece in pieces:
        outs.append(share[at : at + piece.shape[1]])
        at += piece.shape[1]
    return (
        output,
        tokens_grad,
        summary_grad[None],
        outs[0],
        outs[1],
        query_mat_grad,
        outs[2],
        key_mat_grad,
        value_mat_grad,
        outs[3],
        out_grad,
        outs[4],
        outs[5],
        outs[6],
        up_grad,
        outs[7],
        down_grad,
        outs[8],
    )


def solution(mesh):
    rows, rows2, rows3 = P(BOTH), P(BOTH, None), P(BOTH, None, None)
    return jax.shard_map(
        shards,
        mesh=mesh,
        in_specs=(
            rows2, rows3, rows2, P(), rows, rows, rows2, rows, rows2, rows2, rows, rows2, rows,
            rows, rows, rows2, rows, rows2, rows, rows2,
        ),
        out_specs=(
            rows2, rows2, rows3, rows, rows, rows2, rows, rows2, rows2, rows, rows2, rows, rows,
            rows, rows2, rows, rows2, rows,
        ),
        check_vma=False,
    )
```

```python
import functools
import jax
import jax.numpy as jnp
from jax import lax
from jax.experimental import pallas as pl
from jax.experimental.pallas import tpu as pltpu
from jax.sharding import PartitionSpec as P

F32, BF16 = jnp.float32, jnp.bfloat16
HEADS = 32
BOTH = ("fsdp", "dp")
HEAD = 64
PAIR = 2 * HEAD
PRIOR_ROWS = 64
NORM_ROWS = 64
MASKED = -1e30
GELU_A, GELU_B = 0.7978845608028654, 0.044715
VMEM_LIMIT = 53 * 1024 * 1024
VMEM = pl.BlockSpec(memory_space=pltpu.VMEM)
HBM = pl.BlockSpec(memory_space=pl.ANY)


def dot(left, right):
    return jnp.dot(left, right, preferred_element_type=F32)


def dot_t(left, right):
    return lax.dot_general(left, right, (((1,), (1,)), ((), ())), preferred_element_type=F32)


def t_dot(left, right):
    return lax.dot_general(left, right, (((0,), (0,)), ((), ())), preferred_element_type=F32)


def norm_parts(values):
    centre = values - jnp.mean(values, axis=-1, keepdims=True)
    spread = jnp.mean(centre * centre, axis=-1, keepdims=True)
    return centre, lax.rsqrt(spread + 1e-05)


def norm_apply(values, norm_gain, norm_bias):
    centre, inverse = norm_parts(values)
    return centre * inverse * norm_gain + norm_bias


def in_pair(half, rows):
    lane = lax.broadcasted_iota(jnp.int32, (rows, PAIR), 1)
    return (lane >= HEAD) if half else (lane < HEAD)


def pair_at(base, pair):
    return pl.ds(pl.multiple_of(base + pair * PAIR, PAIR), PAIR)


def load_blocks(hbm, scratch, sems):
    copies = [
        pltpu.make_async_copy(hbm.at[:, block], scratch.at[block], sems.at[block])
        for block in range(scratch.shape[0])
    ]
    for copy in copies:
        copy.start()
    return copies


def load_rows(parts, scratch, sems):
    copies = []
    at = 0
    for index, part in enumerate(parts):
        rows = part.shape[0]
        copies.append(
            pltpu.make_async_copy(part, scratch.at[pl.ds(at, rows)], sems.at[index])
        )
        at += rows
    for copy in copies:
        copy.start()
    return copies


def flat_list(lists):
    return [piece for some in lists for piece in some]


def wait_all(copies):
    for copy in copies:
        copy.wait()


def rows_of(ref, columns):
    value = ref[:, :, :, columns]
    return value.reshape(-1, value.shape[-1])


def block_of(ref, block, columns):
    value = ref[block, :, :, columns]
    return value.reshape(-1, value.shape[-1])


COST = 1_000_000


def kernel_params(cost):
    return dict(
        compiler_params=pltpu.CompilerParams(vmem_limit_bytes=VMEM_LIMIT),
        cost_estimate=pl.CostEstimate(flops=cost * COST, bytes_accessed=1, transcendentals=0),
    )


def shape_of(rows, columns, dtype=BF16):
    return jax.ShapeDtypeStruct((rows, columns), dtype)


def attn_forward(xs, gain, bias, off, ok_rows, attn_w, types):
    count = len(xs)
    pieces = flat_list(xs)
    given = len(pieces)
    keys, width = sum(piece.shape[0] for piece in xs[0]), pieces[0].shape[1]
    seg = keys - PRIOR_ROWS
    columns, members, share, wide = attn_w.shape
    cols = wide // 4

    def kernel(*refs):
        gain_ref, bias_ref, off_ref, ok_ref, attn_hbm = refs[given : given + 5]
        outs = refs[given + 5 : given + 5 + 6 * count]
        x_all, weights, mask, sems = refs[given + 5 + 6 * count :]
        x_copies = load_rows(refs[:given], x_all, sems.at[pl.ds(members, given)])
        copies = load_blocks(attn_hbm, weights, sems)
        gain, bias = gain_ref[...], bias_ref[...]
        wait_all(x_copies)
        for index in range(count):
            low_ref = outs[6 * index]

            def norm_rows(block, _):
                start = pl.multiple_of(block * NORM_ROWS, NORM_ROWS)
                values = x_all[pl.ds(index * keys + start, NORM_ROWS), :].astype(F32)
                low_ref[pl.ds(start, NORM_ROWS), :] = norm_apply(values, gain, bias).astype(BF16)
                return _

            lax.fori_loop(0, keys // NORM_ROWS, norm_rows, 0)
        wait_all(copies)
        for index in range(count):
            attend_segment(ok_ref[index : index + 1, :], off_ref, weights, mask, outs[6 * index : 6 * index + 6])

    def attend_segment(ok_row, off_ref, weights, mask, refs):
        low_ref, qkv_ref, lse_ref, mixed_ref, *parts = refs
        row = lax.broadcasted_iota(jnp.int32, (seg, keys), 0)
        col = lax.broadcasted_iota(jnp.int32, (seg, keys), 1)
        mask[...] = jnp.where(jnp.logical_or(col <= row, ok_row > 0.5), 0.0, MASKED)

        def project(part, _):
            at = pl.ds(pl.multiple_of(part * cols, PAIR), cols)
            value = dot(low_ref[...], rows_of(weights, at)) + off_ref[:, at]
            qkv_ref[:, at] = value.astype(BF16)
            return _

        lax.fori_loop(0, 3, project, 0)
        lane = lax.broadcasted_iota(jnp.int32, (seg, PAIR), 1)

        def attend(pair, _):
            query = qkv_ref[:seg, pair_at(0, pair)] * jnp.asarray(HEAD**-0.5, BF16)
            key = qkv_ref[:, pair_at(cols, pair)]
            value = qkv_ref[:, pair_at(2 * cols, pair)]
            merged = None
            for half in range(2):
                inside = in_pair(half, seg)
                scores = dot_t(jnp.where(inside, query, jnp.zeros_like(query)), key) + mask[...]
                row_max = jnp.max(scores, axis=-1, keepdims=True)
                expo = jnp.exp(scores - row_max)
                row_total = jnp.sum(expo, axis=-1, keepdims=True)
                log_total = row_max + jnp.log(row_total)
                lse_ref[...] = jnp.where(lane == 2 * pair + half, log_total, lse_ref[...])
                mixed = dot((expo * (1.0 / row_total)).astype(BF16), value)
                merged = mixed if merged is None else jnp.where(inside, mixed, merged)
            mixed_ref[:, pair_at(0, pair)] = merged.astype(BF16)
            return _

        lse_ref[...] = jnp.zeros_like(lse_ref)
        lax.fori_loop(0, cols // PAIR, attend, 0)

        def project_out(block, _):
            at = pl.ds(pl.multiple_of(block * cols, PAIR), cols)
            weight = block_of(weights, block, pl.ds(3 * cols, cols))
            value = dot(mixed_ref[...], weight)
            for half, part in enumerate(parts):
                part[:, at] = value[half * seg // 2 : (half + 1) * seg // 2].astype(part.dtype)
            return _

        lax.fori_loop(0, members, project_out, 0)

    shapes = []
    for dtype in types:
        shapes += [
            shape_of(keys, width),
            shape_of(keys, 3 * cols),
            shape_of(seg, PAIR, F32),
            shape_of(seg, cols),
            shape_of(seg // 2, width, dtype),
            shape_of(seg // 2, width, dtype),
        ]
    outs = pl.pallas_call(
        kernel,
        out_shape=shapes,
        in_specs=[HBM] * given + [VMEM] * 4 + [HBM],
        out_specs=[VMEM] * len(shapes),
        scratch_shapes=[
            pltpu.VMEM((count * keys, width), BF16),
            pltpu.VMEM((members, columns, share, wide), BF16),
            pltpu.VMEM((seg, keys), F32),
            pltpu.SemaphoreType.DMA((members + given,)),
        ],
        name="attn_forward",
        **kernel_params(12 * count),
    )(*pieces, gain, bias, off, ok_rows, attn_w)
    return [outs[6 * index : 6 * index + 6] for index in range(count)]


def attn_backward(branches, qkvs, lses, ok_cols, attn_w, types):
    count = len(branches)
    pieces = flat_list(branches)
    given = len(pieces)
    seg, width = sum(piece.shape[0] for piece in branches[0]), pieces[0].shape[1]
    keys = qkvs[0].shape[0]
    columns, members, share, wide = attn_w.shape
    cols = wide // 4

    def kernel(*refs):
        ins = refs[given : given + 3 * count]
        attn_hbm = refs[given + 3 * count]
        outs = refs[given + 3 * count + 1 : given + 6 * count + 1]
        branch_all, weights, mask, lse_t, mixed_grad, sems = refs[given + 6 * count + 1 :]
        branch_copies = load_rows(refs[:given], branch_all, sems.at[pl.ds(members, given)])
        copies = load_blocks(attn_hbm, weights, sems)
        wait_all(branch_copies)
        for index in range(count):
            branch = branch_all.at[pl.ds(index * seg, seg)]
            some_in = [ins[index], ins[count + index], ins[2 * count + index]]
            some_out = outs[3 * index : 3 * index + 3]
            waits = copies if index == 0 else []
            back_segment(branch, *some_in, *some_out, weights, mask, lse_t, mixed_grad, waits)

    def back_segment(
        branch_ref, qkv_ref, lse_ref, ok_ref, grads_ref, sums_ref, joined_ref,
        weights, mask, lse_t, mixed_grad, waits,
    ):
        row = lax.broadcasted_iota(jnp.int32, (keys, seg), 0)
        col = lax.broadcasted_iota(jnp.int32, (keys, seg), 1)
        mask[...] = jnp.where(jnp.logical_or(row <= col, ok_ref[:, :1] > 0.5), 0.0, MASKED)
        lse_t[...] = lse_ref[...].T
        grads_ref[seg:, :cols] = jnp.zeros((keys - seg, cols), BF16)
        total = 0.0
        for block in range(members):
            wait_all(waits[block : block + 1])
            weight = block_of(weights, block, pl.ds(3 * cols, cols))
            total = total + dot_t(branch_ref[:, block * cols : (block + 1) * cols], weight)
        mixed_grad[...] = total.astype(BF16)

        def attend(pair, _):
            query = qkv_ref[:seg, pair_at(0, pair)]
            scaled = query * jnp.asarray(HEAD**-0.5, BF16)
            key = qkv_ref[:, pair_at(cols, pair)]
            value = qkv_ref[:, pair_at(2 * cols, pair)]
            mixed = mixed_grad[:, pair_at(0, pair)]
            query_grad = key_grad = value_grad = 0.0
            for half in range(2):
                inside, inside_key = in_pair(half, seg), in_pair(half, keys)
                zero = jnp.zeros_like(query)
                scores = dot_t(key, jnp.where(inside, scaled, zero)) + mask[...]
                probs = jnp.exp(scores - lse_t[pl.ds(2 * pair + half, 1), :])
                mixed_half = jnp.where(inside, mixed, zero)
                prob_grad = dot_t(value, mixed_half)
                value_grad = value_grad + dot(probs.astype(BF16), mixed_half)
                delta = jnp.sum(prob_grad * probs, axis=0, keepdims=True)
                score_grad = (probs * (prob_grad - delta)).astype(BF16)
                key_grad = key_grad + dot(score_grad, jnp.where(inside, query, zero))
                key_half = jnp.where(inside_key, key, jnp.zeros_like(key))
                query_grad = query_grad + t_dot(score_grad, key_half)
            grads_ref[:seg, pair_at(0, pair)] = (query_grad * HEAD**-0.5).astype(BF16)
            grads_ref[:, pair_at(cols, pair)] = (key_grad * HEAD**-0.5).astype(BF16)
            grads_ref[:, pair_at(2 * cols, pair)] = value_grad.astype(BF16)
            return _

        lax.fori_loop(0, cols // PAIR, attend, 0)

        def back(block, _):
            weight = block_of(weights, block, pl.ds(0, 3 * cols))
            at = pl.ds(pl.multiple_of(block * cols, PAIR), cols)
            joined_ref[:, at] = dot_t(grads_ref[...], weight).astype(joined_ref.dtype)
            return _

        lax.fori_loop(0, members, back, 0)
        sums_ref[...] = jnp.sum(grads_ref[...].astype(F32), axis=0, keepdims=True)

    shapes = []
    for dtype in types:
        shapes += [
            shape_of(keys, 3 * cols),
            shape_of(1, 3 * cols, F32),
            shape_of(keys, width, dtype),
        ]
    outs = pl.pallas_call(
        kernel,
        out_shape=shapes,
        in_specs=[HBM] * given + [VMEM] * (3 * count) + [HBM],
        out_specs=[VMEM] * len(shapes),
        scratch_shapes=[
            pltpu.VMEM((count * seg, width), BF16),
            pltpu.VMEM((members, columns, share, wide), BF16),
            pltpu.VMEM((keys, seg), F32),
            pltpu.VMEM((PAIR, seg), F32),
            pltpu.VMEM((seg, cols), BF16),
            pltpu.SemaphoreType.DMA((members + given,)),
        ],
        name="attn_backward",
        **kernel_params(12 * count),
    )(*pieces, *qkvs, *lses, *ok_cols, attn_w)
    return [outs[3 * index : 3 * index + 3] for index in range(count)]


def ffn_hidden(seconds, off, up_w):
    pieces = flat_list(seconds)
    given = len(pieces)
    width = pieces[0].shape[1]
    count = len(seconds)
    seg = sum(piece.shape[0] for piece in pieces) // count
    columns, members, share, wide = up_w.shape
    step = 512

    def kernel(*refs):
        off_ref, up_hbm = refs[given : given + 2]
        outs = refs[given + 2 : given + 2 + 2 * count]
        second, up, sems = refs[given + 2 + 2 * count :]
        copies = load_blocks(up_hbm, up, sems)
        wait_all(copies + load_rows(refs[:given], second, sems.at[pl.ds(members, given)]))

        def hidden(block, _):
            at = pl.ds(pl.multiple_of(block * step, step), step)
            weight = rows_of(up, at)
            for index in range(count):
                pre = dot(second[pl.ds(index * seg, seg), :], weight) + off_ref[:, at]
                square = pre * pre
                bent = jnp.tanh(GELU_A * pre * (1.0 + GELU_B * square))
                gate = 0.5 * (1.0 + bent)
                outs[index][:, at] = (pre * gate).astype(BF16)
                rise = 0.5 * pre * (1.0 - bent * bent) * (GELU_A * (1.0 + 3.0 * GELU_B * square))
                outs[count + index][:, at] = (gate + rise).astype(BF16)
            return _

        lax.fori_loop(0, wide // step, hidden, 0)

    outs = pl.pallas_call(
        kernel,
        out_shape=[shape_of(seg, wide)] * (2 * count),
        in_specs=[HBM] * given + [VMEM, HBM],
        out_specs=[VMEM] * (2 * count),
        scratch_shapes=[
            pltpu.VMEM((count * seg, width), BF16),
            pltpu.VMEM((members, columns, share, wide), BF16),
            pltpu.SemaphoreType.DMA((members + given,)),
        ],
        name="ffn_hidden",
        **kernel_params(6 * count),
    )(*pieces, off, up_w)
    return outs[:count], outs[count:]


def ffn_back(cots, slopes, up_w, down_w, types):
    pieces = flat_list(cots)
    given = len(pieces)
    count = len(slopes)
    seg, width = slopes[0].shape[0], pieces[0].shape[1]
    columns, members, share, wide = up_w.shape
    step = 512
    rows = count * seg
    loads = given + count

    def kernel(*refs):
        up_hbm, down_hbm, pre_ref, sums_ref = refs[loads : loads + 4]
        backs = refs[loads + 4 : loads + 4 + count]
        cot, slope, up, down, sems = refs[loads + 4 + count :]
        first = load_rows(refs[:given], cot, sems)
        first += load_rows([down_hbm], down, sems.at[pl.ds(loads, 1)])
        first += load_rows(refs[given:loads], slope, sems.at[pl.ds(given, count)])
        later = load_blocks(up_hbm, up, sems.at[pl.ds(loads + 1, members)])
        wait_all(first)

        def grad(block, _):
            at = pl.ds(pl.multiple_of(block * step, step), step)
            value = dot_t(cot[...], down[at, :]) * slope[:, at].astype(F32)
            value = value.astype(BF16)
            pre_ref[:, at] = value
            sums_ref[:, at] = jnp.sum(value.astype(F32), axis=0, keepdims=True)
            return _

        lax.fori_loop(0, wide // step, grad, 0)
        wait_all(later)
        deep = columns * share

        def back(block, _):
            at = pl.ds(pl.multiple_of(block * deep, PAIR), deep)
            value = dot_t(pre_ref[...], up[block].reshape(deep, wide))
            for index in range(count):
                backs[index][:, at] = value[index * seg : (index + 1) * seg].astype(types[index])
            return _

        lax.fori_loop(0, members, back, 0)

    return pl.pallas_call(
        kernel,
        out_shape=(
            shape_of(rows, wide),
            shape_of(1, wide, F32),
            *[shape_of(seg, width, dtype) for dtype in types],
        ),
        in_specs=[HBM] * (loads + 2),
        out_specs=(VMEM,) * (2 + count),
        scratch_shapes=[
            pltpu.VMEM((rows, width), BF16),
            pltpu.VMEM((rows, wide), BF16),
            pltpu.VMEM((members, columns, share, wide), BF16),
            pltpu.VMEM((wide, width), BF16),
            pltpu.SemaphoreType.DMA((loads + 1 + members,)),
        ],
        name="ffn_back",
        **kernel_params(10 * count),
    )(*pieces, *slopes, up_w, down_w)


def ffn_out(hiddens, down_w, types):
    count = len(types)
    seg, wide = hiddens[0].shape
    rows = seg // 2
    width = down_w.shape[1]
    step = 512

    def kernel(*refs):
        down_ref = refs[count]
        outs = refs[count + 1 : 3 * count + 1]
        hidden, sems = refs[3 * count + 1 :]
        wait_all(load_rows(refs[:count], hidden, sems))

        def block(part, _):
            at = pl.ds(pl.multiple_of(part * step, step), step)
            value = dot(hidden[...], down_ref[:, at])
            for index in range(2 * count):
                half = value[index * rows : (index + 1) * rows]
                outs[index][:, at] = half.astype(types[index // 2])
            return _

        lax.fori_loop(0, width // step, block, 0)

    outs = pl.pallas_call(
        kernel,
        out_shape=[shape_of(rows, width, types[index // 2]) for index in range(2 * count)],
        in_specs=[HBM] * count + [VMEM],
        out_specs=[VMEM] * (2 * count),
        scratch_shapes=[
            pltpu.VMEM((count * seg, wide), BF16),
            pltpu.SemaphoreType.DMA((count,)),
        ],
        name="ffn_out",
        **kernel_params(18),
    )(*hiddens, down_w)
    return [outs[2 * index : 2 * index + 2] for index in range(count)]


GRAD_ROWS = 256


def weight_grad(lefts, rights):
    tall, wide = lefts[0].shape[1], rights[0].shape[1]
    deep = sum(left.shape[0] for left in lefts)
    counts = len(lefts), len(rights)
    both = sum(counts)

    def kernel(*refs):
        out_ref, left, right, sems = refs[both:]
        step = pl.program_id(0)

        @pl.when(step == 0)
        def _():
            copies = load_rows(refs[: counts[0]], left, sems)
            wait_all(copies + load_rows(refs[counts[0] : both], right, sems.at[pl.ds(counts[0], counts[1])]))

        at = pl.ds(pl.multiple_of(step * GRAD_ROWS, GRAD_ROWS), GRAD_ROWS)
        out_ref[...] = t_dot(left[:, at], right[...]).astype(BF16)

    return pl.pallas_call(
        kernel,
        grid=(tall // GRAD_ROWS,),
        out_shape=shape_of(tall, wide),
        in_specs=[HBM] * both,
        out_specs=pl.BlockSpec((GRAD_ROWS, wide), lambda i: (i, 0)),
        scratch_shapes=[
            pltpu.VMEM((deep, tall), BF16),
            pltpu.VMEM((deep, wide), BF16),
            pltpu.SemaphoreType.DMA((both,)),
        ],
        name="weight_grad",
        **kernel_params(17),
    )(*lefts, *rights)


def attn_weight_grad(lows, grads, mixeds, branches):
    lists = lows, grads, mixeds, branches
    width, cols = lows[0].shape[1], mixeds[0].shape[1]
    halves = cols // GRAD_ROWS
    ends = [0]
    for some in lists:
        ends.append(ends[-1] + len(some))

    def kernel(*refs):
        out_ref, low, grad, mixed, branch, sems = refs[ends[-1] :]
        step = pl.program_id(0)

        @pl.when(step == 0)
        def _():
            copies = []
            for first, last, scratch in zip(ends, ends[1:], (low, grad, mixed, branch)):
                copies += load_rows(refs[first:last], scratch, sems.at[pl.ds(first, last - first)])
            wait_all(copies)

        at = pl.ds(pl.multiple_of(step * GRAD_ROWS, GRAD_ROWS), GRAD_ROWS)
        out_ref[:, : 3 * cols] = t_dot(low[:, at], grad[...]).astype(BF16)
        half = pl.ds(pl.multiple_of((step % halves) * GRAD_ROWS, GRAD_ROWS), GRAD_ROWS)
        block = pl.ds(pl.multiple_of((step // halves) * cols, PAIR), cols)
        out_ref[:, 3 * cols :] = t_dot(mixed[:, half], branch[:, block]).astype(BF16)

    return pl.pallas_call(
        kernel,
        grid=(width // GRAD_ROWS,),
        out_shape=shape_of(width, 4 * cols),
        in_specs=[HBM] * ends[-1],
        out_specs=pl.BlockSpec((GRAD_ROWS, 4 * cols), lambda i: (i, 0)),
        scratch_shapes=[
            pltpu.VMEM((sum(one.shape[0] for one in some), some[0].shape[1]), BF16)
            for some in lists
        ]
        + [pltpu.SemaphoreType.DMA((ends[-1],))],
        name="attn_weight_grad",
        **kernel_params(21),
    )(*lows, *grads, *mixeds, *branches)


def norm_values(values):
    centre, inverse = norm_parts(values)
    return centre * inverse, inverse


def norm_back(hat, inverse, grad, gain):
    hat_grad = grad * gain
    mean = jnp.mean(hat_grad, axis=-1, keepdims=True)
    along = jnp.mean(hat_grad * hat, axis=-1, keepdims=True)
    return inverse * (hat_grad - mean - hat * along)


def column_sum(value):
    return jnp.sum(value, axis=0, keepdims=True)


def row_blocks(width, last=None, rows=NORM_ROWS):
    if last is None:
        return pl.BlockSpec((rows, width), lambda i: (i, 0))
    return pl.BlockSpec((rows, width), lambda i: (jnp.minimum(i, last), 0))


def store_half(refs, value):
    for half, ref in enumerate(refs):

        @pl.when(pl.program_id(0) == half)
        def _(ref=ref):
            ref[...] = value


def kept(rows, width):
    return pl.BlockSpec((rows, width), lambda i: (0, 0))


def sum_parts(parts):
    total = parts[0][...].astype(F32)
    for part in parts[1:]:
        total = total + part[...].astype(F32)
    return total


def middle_norm(tokens, parts, off, gain, bias):
    seg, width = tokens.shape
    count = len(parts)
    rows = seg // 2
    step = 32

    def kernel(*refs):
        tokens_ref, off_ref, gain_ref, bias_ref, middle_ref, *seconds = refs[2 * count :]
        off, gain, bias = off_ref[...], gain_ref[...], bias_ref[...]
        for half in range(2):

            def body(block, _):
                start = pl.multiple_of(block * step, step)
                at, whole = pl.ds(start, step), pl.ds(half * rows + start, step)
                total = tokens_ref[whole, :].astype(F32)
                for index in range(count):
                    total = total + refs[2 * index + half][at, :].astype(F32)
                total = total + off
                middle_ref[whole, :] = total
                seconds[half][at, :] = norm_apply(total, gain, bias).astype(BF16)
                return _

            lax.fori_loop(0, rows // step, body, 0)

    return pl.pallas_call(
        kernel,
        out_shape=(shape_of(seg, width, F32), shape_of(rows, width), shape_of(rows, width)),
        in_specs=[VMEM] * (2 * count + 4),
        out_specs=(VMEM,) * 3,
        name="middle_norm",
        **kernel_params(5),
    )(*flat_list(parts), tokens, off, gain, bias)


def middle_back(middle, cot, parts, gain):
    seg, width = middle.shape
    count = len(parts)
    rows = seg // 2

    def kernel(*refs):
        middle_ref, cot_ref, gain_ref, grad_ref, top_ref, bottom_ref, sums_ref = refs[count:]

        @pl.when(pl.program_id(0) == 0)
        def _():
            sums_ref[...] = jnp.zeros_like(sums_ref)

        grad = sum_parts(refs[:count])
        hat, inverse = norm_values(middle_ref[...])
        cots = cot_ref[...].astype(F32)
        total = cots + norm_back(hat, inverse, grad, gain_ref[...])
        low = total.astype(BF16)
        grad_ref[...] = total
        store_half([top_ref, bottom_ref], low)
        sums_ref[0:1, :] += column_sum(grad * hat)
        sums_ref[1:2, :] += column_sum(grad)
        sums_ref[2:3, :] += column_sum(low.astype(F32))
        sums_ref[3:4, :] += column_sum(cots)

    return pl.pallas_call(
        kernel,
        grid=(2,),
        out_shape=(
            shape_of(seg, width, F32),
            shape_of(rows, width),
            shape_of(rows, width),
            shape_of(4, width, F32),
        ),
        in_specs=[row_blocks(width, rows=rows)] * (count + 2) + [kept(1, width)],
        out_specs=(
            row_blocks(width, rows=rows),
            kept(rows, width),
            kept(rows, width),
            kept(4, width),
        ),
        name="middle_back",
        **kernel_params(5),
    )(*parts, middle, cot, gain)


def first_back(joined, parts, middle_grad, gain):
    seg, width = middle_grad.shape
    keys = joined.shape[0]
    count = len(parts)
    last = seg // NORM_ROWS - 1

    def kernel(*refs):
        joined_ref, middle_ref, gain_ref, tokens_ref, prior_ref, sums_ref = refs[count:]
        step = pl.program_id(0)

        @pl.when(step == 0)
        def _():
            sums_ref[...] = jnp.zeros_like(sums_ref)

        grad = sum_parts(refs[:count])
        hat, inverse = norm_values(joined_ref[...].astype(F32))
        sums_ref[0:1, :] += column_sum(grad * hat)
        sums_ref[1:2, :] += column_sum(grad)
        back = norm_back(hat, inverse, grad, gain_ref[...])

        @pl.when(step <= last)
        def _():
            tokens_ref[...] = middle_ref[...] + back

        @pl.when(step > last)
        def _():
            prior_ref[...] = back.astype(BF16)

    return pl.pallas_call(
        kernel,
        grid=(keys // NORM_ROWS,),
        out_shape=(
            shape_of(seg, width, F32),
            shape_of(keys - seg, width),
            shape_of(2, width, F32),
        ),
        in_specs=[row_blocks(width)] * (count + 1) + [row_blocks(width, last), kept(1, width)],
        out_specs=(row_blocks(width, last), kept(keys - seg, width), kept(2, width)),
        name="first_back",
        **kernel_params(500_000),
    )(*parts, joined, middle_grad, gain)


def swap(value, rel):
    if rel == 0:
        return value
    count = lax.axis_size("fsdp")
    return lax.ppermute(value, "fsdp", [(i, i ^ rel) for i in range(count)])


def halves_of(value):
    rows = value.shape[0] // 2
    return [value[:rows], value[rows:]]


def spread_near(halves):
    near = range(1, min(lax.axis_size("fsdp"), 3))
    return [[swap(half, rel) for half in halves] for rel in near]


def spread_far(halves, near, *others):
    members = lax.axis_size("fsdp")
    near = lax.optimization_barrier((near, others))[0]
    pieces = [halves, *near]
    if members > 3:
        top, bottom = near[0][0], near[1][-1]
        if len(halves) == 1:
            top, bottom = halves_of(top)[0], halves_of(bottom)[1]
        pieces.append([swap(top, 2), swap(bottom, 1)])
    return pieces + [[swap(half, rel) for half in halves] for rel in range(4, members)]


def after(value, *others):
    return lax.optimization_barrier((value, *others))[0]


def add_low(left, right):
    return (left.astype(F32) + right.astype(F32)).astype(BF16)


def output_halves(rel, halves, over, early):
    if over and rel == 2:
        return [add_low(halves[0], over[0]), early[1]], [False, True]
    if over and rel == 1:
        return [early[0], add_low(halves[1], over[1])], [True, False]
    return halves, [False, False]


def trade_blocks(blocks):
    return lax.all_to_all(blocks, "fsdp", 0, 0, tiled=True)


def doubled(rows, axis):
    size = lax.axis_size(axis)
    place = lax.axis_index(axis)
    step = 1
    while step < size:
        came = lax.ppermute(rows, axis, [(i, i ^ step) for i in range(size)])
        high = (place & step) != 0
        rows = jnp.concatenate([jnp.where(high, came, rows), jnp.where(high, rows, came)], 0)
        step *= 2
    return rows


def scatter_small(rows):
    return jnp.sum(lax.all_to_all(rows, BOTH, 0, 0, tiled=True), axis=0)


def gather_dp(value):
    return lax.all_gather(value, "dp", axis=0, tiled=True)


def scatter_dp(value, axis):
    return lax.psum_scatter(value, "dp", scatter_dimension=axis, tiled=True)


def shards(
    tokens,
    summaries,
    presence,
    seg_counts,
    ln1_gain,
    ln1_bias,
    w_query,
    query_bias,
    w_key,
    w_value,
    value_bias,
    w_out,
    out_bias,
    ln2_gain,
    ln2_bias,
    w_up,
    up_bias,
    w_down,
    down_bias,
    cotangent,
):
    members = lax.axis_size("fsdp")
    columns = lax.axis_size("dp")
    total = members * columns
    me = lax.axis_index("fsdp")
    seg_len, width = tokens.shape
    n_summary = summaries.shape[1]
    my_cols = width // members
    my_ff = w_up.shape[1] // members
    row_share = w_query.shape[0]
    rels = list(range(members))
    own_last = rels[::-1]

    def blocks_of(weight):
        return weight.reshape(row_share, members, -1).swapaxes(0, 1)

    def gathered(blocks):
        rows = blocks.reshape(members * row_share, -1)
        return gather_dp(rows).reshape(columns, members, row_share, -1)

    small_parts = (
        ln1_gain, ln1_bias, query_bias, value_bias, out_bias, ln2_gain, ln2_bias, up_bias,
        down_bias, presence[0].astype(BF16),
    )
    packed = doubled(jnp.concatenate(small_parts)[None], "fsdp")
    prior = jnp.pad(summaries[0], ((0, PRIOR_ROWS - n_summary), (0, 0)))
    prior = lax.ppermute(prior, BOTH, [(i, i + 1) for i in range(total - 1)])
    joined = jnp.concatenate([tokens, prior], 0)

    qkv_blocks = jnp.concatenate([blocks_of(w_query), blocks_of(w_key), blocks_of(w_value)], 2)
    qkv_blocks = trade_blocks(qkv_blocks)
    up_blocks, packed = lax.optimization_barrier((blocks_of(w_up), packed, qkv_blocks, joined))[:2]
    up_blocks = trade_blocks(up_blocks)
    attn_w = gathered(jnp.concatenate([qkv_blocks, blocks_of(w_out)], 2))
    up_w = gathered(up_blocks)
    down_w = gather_dp(w_down)

    joined_rows = [joined]
    joined_near = spread_near(after(joined_rows, up_blocks))
    group_joined = spread_far(joined_rows, joined_near)
    cot_rows = [cotangent]
    cot_near = spread_near(after(cot_rows, group_joined))
    packed = doubled(packed, "dp").reshape(columns, members, -1).swapaxes(0, 1)
    packed = packed.reshape(total, -1)

    smalls = []
    at = 0
    for part in small_parts:
        smalls.append(packed[:, at : at + part.shape[0]].astype(F32))
        at += part.shape[0]
    gain_one, bias_one, query_off, value_off, out_off, gain_two, bias_two, up_off, down_off = [
        part.reshape(1, -1) for part in smalls[:-1]
    ]
    present_all = smalls[-1]
    query_off = lax.dynamic_slice_in_dim(query_off, me * my_cols, my_cols, 1)
    value_off = lax.dynamic_slice_in_dim(value_off, me * my_cols, my_cols, 1)
    up_off = lax.dynamic_slice_in_dim(up_off, me * my_ff, my_ff, 1)
    qkv_off = jnp.concatenate([query_off, jnp.zeros_like(query_off), value_off], 1)

    starts = jnp.cumsum(seg_counts) - seg_counts
    group_places = (me ^ jnp.arange(members)) * columns + lax.axis_index("dp")
    has_prev = jnp.all(group_places[:, None] != starts[None, :], axis=1)
    summary_ok = jnp.logical_and(present_all[group_places] == 1, has_prev[:, None]).astype(F32)
    ok_rows = jnp.pad(summary_ok, ((0, 0), (seg_len, PRIOR_ROWS - n_summary)))
    ok_cols = jnp.broadcast_to(ok_rows[:, :, None], (*ok_rows.shape, PAIR))


    def part_type(rel):
        return BF16 if rel else F32

    attn = {}
    middle_parts = {}
    previous = []
    for some in ([[3], [1, 2], [0]] if members == 4 else [[rel] for rel in own_last]):
        xs = [group_joined[rel] for rel in some]
        if some == [0]:
            previous = previous + flat_list(cot_near)
        xs[0] = [after(xs[0][0], *previous), *xs[0][1:]]
        oks = jnp.concatenate([ok_rows[rel : rel + 1] for rel in some], 0)
        outs = attn_forward(
            xs, gain_one, bias_one, qkv_off, oks, attn_w, [part_type(rel) for rel in some]
        )
        for rel, (low, qkv, lse, mixed, *part) in zip(some, outs):
            attn[rel] = (low, qkv, lse, mixed)
            middle_parts[rel] = part
            previous = [lse]
        if members > 3 and some == [3]:
            over = middle_parts.pop(3)
            middle_over = [swap(over[0], 1), swap(over[1], 2)]
    if members > 3:
        two, one = middle_parts[2], middle_parts[1]
        middle_parts[2] = [add_low(two[0], middle_over[0]), two[1]]
        middle_parts[1] = [one[0], add_low(one[1], middle_over[1])]
    middle_parts = {rel: [swap(half, rel) for half in part] for rel, part in middle_parts.items()}
    middle, *second_own = middle_norm(
        tokens, list(middle_parts.values()), out_off, gain_two, bias_two
    )
    def ordered(values):
        return [values[rel] for rel in own_last]

    second_near = spread_near(second_own)
    hidden_own, slope_own = ffn_hidden([second_own], up_off, up_w)
    group_second = spread_far(second_own, second_near, hidden_own)
    hidden, slope = {0: hidden_own[0]}, {0: slope_own[0]}
    previous = hidden_own
    cuts = [1, members - 1, members] if members > 2 else [1, members]
    for low_rel, high_rel in zip(cuts, cuts[1:]):
        some = rels[low_rel:high_rel]
        seconds = [group_second[rel] for rel in some]
        seconds[0] = [after(seconds[0][0], *previous), *seconds[0][1:]]
        hiddens, slopes = ffn_hidden(seconds, up_off, up_w)
        for rel, one, other in zip(some, hiddens, slopes):
            hidden[rel], slope[rel] = one, other
        previous = hiddens[:1]
        if low_rel == 1:
            group_cot = spread_far(cot_rows, cot_near, previous)
    down_partial = weight_grad(ordered(hidden), flat_list(ordered(group_cot)))
    down_share = scatter_dp(down_partial, 0)
    pre, up_sums, second_parts = [], [], {}
    for some in (own_last[:-1], [0]):
        if not some:
            continue
        cots = [group_cot[rel] for rel in some]
        cots[0] = [after(cots[0][0], *(pre[-1:] or [down_partial])), *cots[0][1:]]
        pre_some, sums, *backs = ffn_back(
            cots, [slope[rel] for rel in some], up_w, down_w, [part_type(rel) for rel in some]
        )
        pre.append(pre_some)
        up_sums.append(sums)
        for rel, back in zip(some, backs):
            second_parts[rel] = swap(back, rel)
    up_partial = weight_grad(flat_list(ordered(group_second)), pre)
    def to_row_blocks(grad):
        return scatter_dp(grad.reshape(members, columns * row_share, -1), 1)

    hiddens = ordered(hidden)
    hiddens[0] = after(hiddens[0], up_partial)
    output_parts = ffn_out(hiddens, down_w, [part_type(rel) for rel in own_last])
    output_parts = dict(zip(own_last, output_parts))
    second_parts = after(second_parts, output_parts)
    up_share = to_row_blocks(after(up_partial, second_parts))
    middle_grad, *branch_low, middle_sums = middle_back(
        middle, cotangent, [second_parts[rel] for rel in rels], gain_two
    )

    branch_near = spread_near(branch_low)
    grads, qkv_sums, joined_parts = {}, {}, {}

    def back_of(some, branches, *others):
        first = [after(branches[0][0], *others), *branches[0][1:]]
        outs = attn_backward(
            [first, *branches[1:]],
            [attn[rel][1] for rel in some],
            [attn[rel][2] for rel in some],
            [ok_cols[rel] for rel in some],
            attn_w,
            [part_type(rel) for rel in some],
        )
        for rel, (grad, sums, part) in zip(some, outs):
            grads[rel], qkv_sums[rel] = grad, sums
            joined_parts[rel] = swap(part, rel)

    back_of([0], [branch_low], down_share)
    group_branch = spread_far(branch_low, branch_near, qkv_sums[0])
    output_over = []
    if members > 3:
        far = after(output_parts.pop(3), qkv_sums[0])
        output_over = [swap(far[0], 1), swap(far[1], 2)]
    last = 0
    for some in ([[1, 2], [3]] if members == 4 else [[rel] for rel in rels[1:]]):
        others = output_over if some == [3] else []
        back_of(some, [group_branch[rel] for rel in some], qkv_sums[last], *others)
        last = some[-1]
    output_early = []
    if members > 3:
        early = after([output_parts[1][0], output_parts[2][1]], qkv_sums[2])
        output_early = [swap(early[0], 1), swap(early[1], 2)]
    attn_partial = attn_weight_grad(
        [attn[rel][0] for rel in rels],
        [grads[rel] for rel in rels],
        [attn[rel][3] for rel in rels],
        flat_list(group_branch),
    )
    joined_parts = after(joined_parts, attn_partial, output_early)
    attn_share = to_row_blocks(after(attn_partial, up_share))
    out_grad = (
        attn_share[:, :, 3 * my_cols :].swapaxes(0, 1).reshape(row_share, width).astype(F32)
    )
    qkv_shares = trade_blocks(attn_share[:, :, : 3 * my_cols])
    query_mat_grad, key_mat_grad, value_mat_grad = [
        qkv_shares[:, :, part * my_cols : (part + 1) * my_cols]
        .swapaxes(0, 1)
        .reshape(row_share, width)
        .astype(F32)
        for part in range(3)
    ]
    tokens_grad, prior_part, first_sums = first_back(
        joined, [joined_parts[rel] for rel in rels], middle_grad, gain_one
    )
    summary_grad = lax.ppermute(
        prior_part[:n_summary], BOTH, [(i + 1, i) for i in range(total - 1)]
    ).astype(F32)
    def whole(value):
        return value.reshape(total, -1)

    def sliced(value):
        mine = value.reshape(columns, -1)
        full = jnp.zeros((total, mine.shape[1]), F32)
        return lax.dynamic_update_slice_in_dim(full, mine, me * columns, 0)

    qkv_sums, middle_sums, up_sums = after((qkv_sums, middle_sums, up_sums), first_sums)
    qkv_sum = sum(qkv_sums[rel] for rel in rels)
    pieces = [
        whole(first_sums[0]),
        whole(first_sums[1]),
        sliced(qkv_sum[:, :my_cols]),
        sliced(qkv_sum[:, 2 * my_cols :]),
        whole(middle_sums[2]),
        whole(middle_sums[0]),
        whole(middle_sums[1]),
        sliced(sum(up_sums)),
        whole(middle_sums[3]),
    ]
    share = scatter_small(jnp.concatenate(pieces, 1))
    up_blocks = trade_blocks(after(up_share, share))
    output_parts = after(output_parts, share)
    output_parts = {
        rel: [half if early else swap(half, rel) for half, early in zip(*halves)]
        for rel, halves in (
            (rel, (output_halves(rel, halves, output_over, output_early)))
            for rel, halves in output_parts.items()
        )
    }
    down_grad = after(down_share, share).astype(F32)
    up_grad = up_blocks.swapaxes(0, 1).reshape(row_share, members * my_ff).astype(F32)
    output_sum = jnp.concatenate(
        [sum(halves[half].astype(F32) for halves in output_parts.values()) for half in range(2)], 0
    )
    output = (middle + output_sum + down_off).astype(BF16)
    outs = []
    at = 0
    for piece in pieces:
        outs.append(share[at : at + piece.shape[1]])
        at += piece.shape[1]
    return (
        output,
        tokens_grad,
        summary_grad[None],
        outs[0],
        outs[1],
        query_mat_grad,
        outs[2],
        key_mat_grad,
        value_mat_grad,
        outs[3],
        out_grad,
        outs[4],
        outs[5],
        outs[6],
        up_grad,
        outs[7],
        down_grad,
        outs[8],
    )


def solution(mesh):
    rows, rows2, rows3 = P(BOTH), P(BOTH, None), P(BOTH, None, None)
    return jax.shard_map(
        shards,
        mesh=mesh,
        in_specs=(
            rows2, rows3, rows2, P(), rows, rows, rows2, rows, rows2, rows2, rows, rows2, rows,
            rows, rows, rows2, rows, rows2, rows, rows2,
        ),
        out_specs=(
            rows2, rows2, rows3, rows, rows, rows2, rows, rows2, rows2, rows, rows2, rows, rows,
            rows, rows2, rows, rows2, rows,
        ),
        check_vma=False,
    )
```

```python
import functools
import jax
import jax.numpy as jnp
from jax import lax
from jax.experimental import pallas as pl
from jax.experimental.pallas import tpu as pltpu
from jax.sharding import PartitionSpec as P

F32, BF16 = jnp.float32, jnp.bfloat16
HEADS = 32
BOTH = ("fsdp", "dp")
HEAD = 64
PAIR = 2 * HEAD
PRIOR_ROWS = 64
NORM_ROWS = 64
MASKED = -1e30
GELU_A, GELU_B = 0.7978845608028654, 0.044715
VMEM_LIMIT = 53 * 1024 * 1024
VMEM = pl.BlockSpec(memory_space=pltpu.VMEM)
HBM = pl.BlockSpec(memory_space=pl.ANY)


def dot(left, right):
    return jnp.dot(left, right, preferred_element_type=F32)


def dot_t(left, right):
    return lax.dot_general(left, right, (((1,), (1,)), ((), ())), preferred_element_type=F32)


def t_dot(left, right):
    return lax.dot_general(left, right, (((0,), (0,)), ((), ())), preferred_element_type=F32)


def norm_parts(values):
    centre = values - jnp.mean(values, axis=-1, keepdims=True)
    spread = jnp.mean(centre * centre, axis=-1, keepdims=True)
    return centre, lax.rsqrt(spread + 1e-05)


def norm_apply(values, norm_gain, norm_bias):
    centre, inverse = norm_parts(values)
    return centre * inverse * norm_gain + norm_bias


def in_pair(half, rows):
    lane = lax.broadcasted_iota(jnp.int32, (rows, PAIR), 1)
    return (lane >= HEAD) if half else (lane < HEAD)


def pair_at(base, pair):
    return pl.ds(pl.multiple_of(base + pair * PAIR, PAIR), PAIR)


def load_blocks(hbm, scratch, sems):
    copies = [
        pltpu.make_async_copy(hbm.at[:, block], scratch.at[block], sems.at[block])
        for block in range(scratch.shape[0])
    ]
    for copy in copies:
        copy.start()
    return copies


def load_rows(parts, scratch, sems):
    copies = []
    at = 0
    for index, part in enumerate(parts):
        rows = part.shape[0]
        copies.append(
            pltpu.make_async_copy(part, scratch.at[pl.ds(at, rows)], sems.at[index])
        )
        at += rows
    for copy in copies:
        copy.start()
    return copies


def flat_list(lists):
    return [piece for some in lists for piece in some]


def wait_all(copies):
    for copy in copies:
        copy.wait()


def rows_of(ref, columns):
    value = ref[:, :, :, columns]
    return value.reshape(-1, value.shape[-1])


def block_of(ref, block, columns):
    value = ref[block, :, :, columns]
    return value.reshape(-1, value.shape[-1])


COST = 1_000_000


def kernel_params(cost):
    return dict(
        compiler_params=pltpu.CompilerParams(vmem_limit_bytes=VMEM_LIMIT),
        cost_estimate=pl.CostEstimate(flops=cost * COST, bytes_accessed=1, transcendentals=0),
    )


def shape_of(rows, columns, dtype=BF16):
    return jax.ShapeDtypeStruct((rows, columns), dtype)


def attn_forward(xs, gain, bias, off, ok_rows, attn_w, types):
    count = len(xs)
    pieces = flat_list(xs)
    given = len(pieces)
    keys, width = sum(piece.shape[0] for piece in xs[0]), pieces[0].shape[1]
    seg = keys - PRIOR_ROWS
    columns, members, share, wide = attn_w.shape
    cols = wide // 4

    def kernel(*refs):
        gain_ref, bias_ref, off_ref, ok_ref, attn_hbm = refs[given : given + 5]
        outs = refs[given + 5 : given + 5 + 6 * count]
        x_all, weights, mask, sems = refs[given + 5 + 6 * count :]
        x_copies = load_rows(refs[:given], x_all, sems.at[pl.ds(members, given)])
        copies = load_blocks(attn_hbm, weights, sems)
        gain, bias = gain_ref[...], bias_ref[...]
        wait_all(x_copies)
        for index in range(count):
            low_ref = outs[6 * index]

            def norm_rows(block, _):
                start = pl.multiple_of(block * NORM_ROWS, NORM_ROWS)
                values = x_all[pl.ds(index * keys + start, NORM_ROWS), :].astype(F32)
                low_ref[pl.ds(start, NORM_ROWS), :] = norm_apply(values, gain, bias).astype(BF16)
                return _

            lax.fori_loop(0, keys // NORM_ROWS, norm_rows, 0)
        wait_all(copies)
        for index in range(count):
            attend_segment(ok_ref[index : index + 1, :], off_ref, weights, mask, outs[6 * index : 6 * index + 6])

    def attend_segment(ok_row, off_ref, weights, mask, refs):
        low_ref, qkv_ref, lse_ref, mixed_ref, *parts = refs
        row = lax.broadcasted_iota(jnp.int32, (seg, keys), 0)
        col = lax.broadcasted_iota(jnp.int32, (seg, keys), 1)
        mask[...] = jnp.where(jnp.logical_or(col <= row, ok_row > 0.5), 0.0, MASKED)

        def project(part, _):
            at = pl.ds(pl.multiple_of(part * cols, PAIR), cols)
            value = dot(low_ref[...], rows_of(weights, at)) + off_ref[:, at]
            qkv_ref[:, at] = value.astype(BF16)
            return _

        lax.fori_loop(0, 3, project, 0)
        lane = lax.broadcasted_iota(jnp.int32, (seg, PAIR), 1)

        def attend(pair, _):
            query = qkv_ref[:seg, pair_at(0, pair)] * jnp.asarray(HEAD**-0.5, BF16)
            key = qkv_ref[:, pair_at(cols, pair)]
            value = qkv_ref[:, pair_at(2 * cols, pair)]
            merged = None
            for half in range(2):
                inside = in_pair(half, seg)
                scores = dot_t(jnp.where(inside, query, jnp.zeros_like(query)), key) + mask[...]
                row_max = jnp.max(scores, axis=-1, keepdims=True)
                expo = jnp.exp(scores - row_max)
                row_total = jnp.sum(expo, axis=-1, keepdims=True)
                log_total = row_max + jnp.log(row_total)
                lse_ref[...] = jnp.where(lane == 2 * pair + half, log_total, lse_ref[...])
                mixed = dot((expo * (1.0 / row_total)).astype(BF16), value)
                merged = mixed if merged is None else jnp.where(inside, mixed, merged)
            mixed_ref[:, pair_at(0, pair)] = merged.astype(BF16)
            return _

        lse_ref[...] = jnp.zeros_like(lse_ref)
        lax.fori_loop(0, cols // PAIR, attend, 0)

        def project_out(block, _):
            at = pl.ds(pl.multiple_of(block * cols, PAIR), cols)
            weight = block_of(weights, block, pl.ds(3 * cols, cols))
            value = dot(mixed_ref[...], weight)
            for half, part in enumerate(parts):
                part[:, at] = value[half * seg // 2 : (half + 1) * seg // 2].astype(part.dtype)
            return _

        lax.fori_loop(0, members, project_out, 0)

    shapes = []
    for dtype in types:
        shapes += [
            shape_of(keys, width),
            shape_of(keys, 3 * cols),
            shape_of(seg, PAIR, F32),
            shape_of(seg, cols),
            shape_of(seg // 2, width, dtype),
            shape_of(seg // 2, width, dtype),
        ]
    outs = pl.pallas_call(
        kernel,
        out_shape=shapes,
        in_specs=[HBM] * given + [VMEM] * 4 + [HBM],
        out_specs=[VMEM] * len(shapes),
        scratch_shapes=[
            pltpu.VMEM((count * keys, width), BF16),
            pltpu.VMEM((members, columns, share, wide), BF16),
            pltpu.VMEM((seg, keys), F32),
            pltpu.SemaphoreType.DMA((members + given,)),
        ],
        name="attn_forward",
        **kernel_params(12 * count),
    )(*pieces, gain, bias, off, ok_rows, attn_w)
    return [outs[6 * index : 6 * index + 6] for index in range(count)]


def attn_backward(branches, qkvs, lses, ok_cols, attn_w, types):
    count = len(branches)
    pieces = flat_list(branches)
    given = len(pieces)
    seg, width = sum(piece.shape[0] for piece in branches[0]), pieces[0].shape[1]
    keys = qkvs[0].shape[0]
    columns, members, share, wide = attn_w.shape
    cols = wide // 4

    def kernel(*refs):
        ins = refs[given : given + 3 * count]
        attn_hbm = refs[given + 3 * count]
        outs = refs[given + 3 * count + 1 : given + 6 * count + 1]
        branch_all, weights, mask, lse_t, mixed_grad, sems = refs[given + 6 * count + 1 :]
        branch_copies = load_rows(refs[:given], branch_all, sems.at[pl.ds(members, given)])
        copies = load_blocks(attn_hbm, weights, sems)
        wait_all(branch_copies)
        for index in range(count):
            branch = branch_all.at[pl.ds(index * seg, seg)]
            some_in = [ins[index], ins[count + index], ins[2 * count + index]]
            some_out = outs[3 * index : 3 * index + 3]
            waits = copies if index == 0 else []
            back_segment(branch, *some_in, *some_out, weights, mask, lse_t, mixed_grad, waits)

    def back_segment(
        branch_ref, qkv_ref, lse_ref, ok_ref, grads_ref, sums_ref, joined_ref,
        weights, mask, lse_t, mixed_grad, waits,
    ):
        row = lax.broadcasted_iota(jnp.int32, (keys, seg), 0)
        col = lax.broadcasted_iota(jnp.int32, (keys, seg), 1)
        mask[...] = jnp.where(jnp.logical_or(row <= col, ok_ref[:, :1] > 0.5), 0.0, MASKED)
        lse_t[...] = lse_ref[...].T
        grads_ref[seg:, :cols] = jnp.zeros((keys - seg, cols), BF16)
        total = 0.0
        for block in range(members):
            wait_all(waits[block : block + 1])
            weight = block_of(weights, block, pl.ds(3 * cols, cols))
            total = total + dot_t(branch_ref[:, block * cols : (block + 1) * cols], weight)
        mixed_grad[...] = total.astype(BF16)

        def attend(pair, _):
            query = qkv_ref[:seg, pair_at(0, pair)]
            scaled = query * jnp.asarray(HEAD**-0.5, BF16)
            key = qkv_ref[:, pair_at(cols, pair)]
            value = qkv_ref[:, pair_at(2 * cols, pair)]
            mixed = mixed_grad[:, pair_at(0, pair)]
            query_grad = key_grad = value_grad = 0.0
            for half in range(2):
                inside, inside_key = in_pair(half, seg), in_pair(half, keys)
                zero = jnp.zeros_like(query)
                scores = dot_t(key, jnp.where(inside, scaled, zero)) + mask[...]
                probs = jnp.exp(scores - lse_t[pl.ds(2 * pair + half, 1), :])
                mixed_half = jnp.where(inside, mixed, zero)
                prob_grad = dot_t(value, mixed_half)
                value_grad = value_grad + dot(probs.astype(BF16), mixed_half)
                delta = jnp.sum(prob_grad * probs, axis=0, keepdims=True)
                score_grad = (probs * (prob_grad - delta)).astype(BF16)
                key_grad = key_grad + dot(score_grad, jnp.where(inside, query, zero))
                key_half = jnp.where(inside_key, key, jnp.zeros_like(key))
                query_grad = query_grad + t_dot(score_grad, key_half)
            grads_ref[:seg, pair_at(0, pair)] = (query_grad * HEAD**-0.5).astype(BF16)
            grads_ref[:, pair_at(cols, pair)] = (key_grad * HEAD**-0.5).astype(BF16)
            grads_ref[:, pair_at(2 * cols, pair)] = value_grad.astype(BF16)
            return _

        lax.fori_loop(0, cols // PAIR, attend, 0)

        def back(block, _):
            weight = block_of(weights, block, pl.ds(0, 3 * cols))
            at = pl.ds(pl.multiple_of(block * cols, PAIR), cols)
            joined_ref[:, at] = dot_t(grads_ref[...], weight).astype(joined_ref.dtype)
            return _

        lax.fori_loop(0, members, back, 0)
        sums_ref[...] = jnp.sum(grads_ref[...].astype(F32), axis=0, keepdims=True)

    shapes = []
    for dtype in types:
        shapes += [
            shape_of(keys, 3 * cols),
            shape_of(1, 3 * cols, F32),
            shape_of(keys, width, dtype),
        ]
    outs = pl.pallas_call(
        kernel,
        out_shape=shapes,
        in_specs=[HBM] * given + [VMEM] * (3 * count) + [HBM],
        out_specs=[VMEM] * len(shapes),
        scratch_shapes=[
            pltpu.VMEM((count * seg, width), BF16),
            pltpu.VMEM((members, columns, share, wide), BF16),
            pltpu.VMEM((keys, seg), F32),
            pltpu.VMEM((PAIR, seg), F32),
            pltpu.VMEM((seg, cols), BF16),
            pltpu.SemaphoreType.DMA((members + given,)),
        ],
        name="attn_backward",
        **kernel_params(12 * count),
    )(*pieces, *qkvs, *lses, *ok_cols, attn_w)
    return [outs[3 * index : 3 * index + 3] for index in range(count)]


def ffn_hidden(seconds, off, up_w):
    pieces = flat_list(seconds)
    given = len(pieces)
    width = pieces[0].shape[1]
    count = len(seconds)
    seg = sum(piece.shape[0] for piece in pieces) // count
    columns, members, share, wide = up_w.shape
    step = 512

    def kernel(*refs):
        off_ref, up_hbm = refs[given : given + 2]
        outs = refs[given + 2 : given + 2 + 2 * count]
        second, up, sems = refs[given + 2 + 2 * count :]
        copies = load_blocks(up_hbm, up, sems)
        wait_all(copies + load_rows(refs[:given], second, sems.at[pl.ds(members, given)]))

        def hidden(block, _):
            at = pl.ds(pl.multiple_of(block * step, step), step)
            weight = rows_of(up, at)
            for index in range(count):
                pre = dot(second[pl.ds(index * seg, seg), :], weight) + off_ref[:, at]
                square = pre * pre
                bent = jnp.tanh(GELU_A * pre * (1.0 + GELU_B * square))
                gate = 0.5 * (1.0 + bent)
                outs[index][:, at] = (pre * gate).astype(BF16)
                rise = 0.5 * pre * (1.0 - bent * bent) * (GELU_A * (1.0 + 3.0 * GELU_B * square))
                outs[count + index][:, at] = (gate + rise).astype(BF16)
            return _

        lax.fori_loop(0, wide // step, hidden, 0)

    outs = pl.pallas_call(
        kernel,
        out_shape=[shape_of(seg, wide)] * (2 * count),
        in_specs=[HBM] * given + [VMEM, HBM],
        out_specs=[VMEM] * (2 * count),
        scratch_shapes=[
            pltpu.VMEM((count * seg, width), BF16),
            pltpu.VMEM((members, columns, share, wide), BF16),
            pltpu.SemaphoreType.DMA((members + given,)),
        ],
        name="ffn_hidden",
        **kernel_params(6 * count),
    )(*pieces, off, up_w)
    return outs[:count], outs[count:]


def ffn_back(cots, slopes, up_w, down_w, types):
    pieces = flat_list(cots)
    given = len(pieces)
    count = len(slopes)
    seg, width = slopes[0].shape[0], pieces[0].shape[1]
    columns, members, share, wide = up_w.shape
    step = 512
    rows = count * seg
    loads = given + count

    def kernel(*refs):
        up_hbm, down_hbm, pre_ref, sums_ref = refs[loads : loads + 4]
        backs = refs[loads + 4 : loads + 4 + count]
        cot, slope, up, down, sems = refs[loads + 4 + count :]
        first = load_rows(refs[:given], cot, sems)
        first += load_rows([down_hbm], down, sems.at[pl.ds(loads, 1)])
        first += load_rows(refs[given:loads], slope, sems.at[pl.ds(given, count)])
        later = load_blocks(up_hbm, up, sems.at[pl.ds(loads + 1, members)])
        wait_all(first)

        def grad(block, _):
            at = pl.ds(pl.multiple_of(block * step, step), step)
            value = dot_t(cot[...], down[at, :]) * slope[:, at].astype(F32)
            value = value.astype(BF16)
            pre_ref[:, at] = value
            sums_ref[:, at] = jnp.sum(value.astype(F32), axis=0, keepdims=True)
            return _

        lax.fori_loop(0, wide // step, grad, 0)
        wait_all(later)
        deep = columns * share

        def back(block, _):
            at = pl.ds(pl.multiple_of(block * deep, PAIR), deep)
            value = dot_t(pre_ref[...], up[block].reshape(deep, wide))
            for index in range(count):
                backs[index][:, at] = value[index * seg : (index + 1) * seg].astype(types[index])
            return _

        lax.fori_loop(0, members, back, 0)

    return pl.pallas_call(
        kernel,
        out_shape=(
            shape_of(rows, wide),
            shape_of(1, wide, F32),
            *[shape_of(seg, width, dtype) for dtype in types],
        ),
        in_specs=[HBM] * (loads + 2),
        out_specs=(VMEM,) * (2 + count),
        scratch_shapes=[
            pltpu.VMEM((rows, width), BF16),
            pltpu.VMEM((rows, wide), BF16),
            pltpu.VMEM((members, columns, share, wide), BF16),
            pltpu.VMEM((wide, width), BF16),
            pltpu.SemaphoreType.DMA((loads + 1 + members,)),
        ],
        name="ffn_back",
        **kernel_params(10 * count),
    )(*pieces, *slopes, up_w, down_w)


def ffn_out(hiddens, down_w, types):
    count = len(types)
    seg, wide = hiddens[0].shape
    rows = seg // 2
    width = down_w.shape[1]
    step = 512

    def kernel(*refs):
        down_ref = refs[count]
        outs = refs[count + 1 : 3 * count + 1]
        hidden, sems = refs[3 * count + 1 :]
        wait_all(load_rows(refs[:count], hidden, sems))

        def block(part, _):
            at = pl.ds(pl.multiple_of(part * step, step), step)
            value = dot(hidden[...], down_ref[:, at])
            for index in range(2 * count):
                half = value[index * rows : (index + 1) * rows]
                outs[index][:, at] = half.astype(types[index // 2])
            return _

        lax.fori_loop(0, width // step, block, 0)

    outs = pl.pallas_call(
        kernel,
        out_shape=[shape_of(rows, width, types[index // 2]) for index in range(2 * count)],
        in_specs=[HBM] * count + [VMEM],
        out_specs=[VMEM] * (2 * count),
        scratch_shapes=[
            pltpu.VMEM((count * seg, wide), BF16),
            pltpu.SemaphoreType.DMA((count,)),
        ],
        name="ffn_out",
        **kernel_params(18),
    )(*hiddens, down_w)
    return [outs[2 * index : 2 * index + 2] for index in range(count)]


GRAD_ROWS = 256


def weight_grad(lefts, rights):
    tall, wide = lefts[0].shape[1], rights[0].shape[1]
    deep = sum(left.shape[0] for left in lefts)
    counts = len(lefts), len(rights)
    both = sum(counts)

    def kernel(*refs):
        out_ref, left, right, sems = refs[both:]
        step = pl.program_id(0)

        @pl.when(step == 0)
        def _():
            copies = load_rows(refs[: counts[0]], left, sems)
            wait_all(copies + load_rows(refs[counts[0] : both], right, sems.at[pl.ds(counts[0], counts[1])]))

        at = pl.ds(pl.multiple_of(step * GRAD_ROWS, GRAD_ROWS), GRAD_ROWS)
        out_ref[...] = t_dot(left[:, at], right[...]).astype(BF16)

    return pl.pallas_call(
        kernel,
        grid=(tall // GRAD_ROWS,),
        out_shape=shape_of(tall, wide),
        in_specs=[HBM] * both,
        out_specs=pl.BlockSpec((GRAD_ROWS, wide), lambda i: (i, 0)),
        scratch_shapes=[
            pltpu.VMEM((deep, tall), BF16),
            pltpu.VMEM((deep, wide), BF16),
            pltpu.SemaphoreType.DMA((both,)),
        ],
        name="weight_grad",
        **kernel_params(17),
    )(*lefts, *rights)


def attn_weight_grad(lows, grads, mixeds, branches):
    lists = lows, grads, mixeds, branches
    width, cols = lows[0].shape[1], mixeds[0].shape[1]
    halves = cols // GRAD_ROWS
    ends = [0]
    for some in lists:
        ends.append(ends[-1] + len(some))

    def kernel(*refs):
        out_ref, low, grad, mixed, branch, sems = refs[ends[-1] :]
        step = pl.program_id(0)

        @pl.when(step == 0)
        def _():
            copies = []
            for first, last, scratch in zip(ends, ends[1:], (low, grad, mixed, branch)):
                copies += load_rows(refs[first:last], scratch, sems.at[pl.ds(first, last - first)])
            wait_all(copies)

        at = pl.ds(pl.multiple_of(step * GRAD_ROWS, GRAD_ROWS), GRAD_ROWS)
        out_ref[:, : 3 * cols] = t_dot(low[:, at], grad[...]).astype(BF16)
        half = pl.ds(pl.multiple_of((step % halves) * GRAD_ROWS, GRAD_ROWS), GRAD_ROWS)
        block = pl.ds(pl.multiple_of((step // halves) * cols, PAIR), cols)
        out_ref[:, 3 * cols :] = t_dot(mixed[:, half], branch[:, block]).astype(BF16)

    return pl.pallas_call(
        kernel,
        grid=(width // GRAD_ROWS,),
        out_shape=shape_of(width, 4 * cols),
        in_specs=[HBM] * ends[-1],
        out_specs=pl.BlockSpec((GRAD_ROWS, 4 * cols), lambda i: (i, 0)),
        scratch_shapes=[
            pltpu.VMEM((sum(one.shape[0] for one in some), some[0].shape[1]), BF16)
            for some in lists
        ]
        + [pltpu.SemaphoreType.DMA((ends[-1],))],
        name="attn_weight_grad",
        **kernel_params(21),
    )(*lows, *grads, *mixeds, *branches)


def norm_values(values):
    centre, inverse = norm_parts(values)
    return centre * inverse, inverse


def norm_back(hat, inverse, grad, gain):
    hat_grad = grad * gain
    mean = jnp.mean(hat_grad, axis=-1, keepdims=True)
    along = jnp.mean(hat_grad * hat, axis=-1, keepdims=True)
    return inverse * (hat_grad - mean - hat * along)


def column_sum(value):
    return jnp.sum(value, axis=0, keepdims=True)


def row_blocks(width, last=None, rows=NORM_ROWS):
    if last is None:
        return pl.BlockSpec((rows, width), lambda i: (i, 0))
    return pl.BlockSpec((rows, width), lambda i: (jnp.minimum(i, last), 0))


def store_half(refs, value):
    for half, ref in enumerate(refs):

        @pl.when(pl.program_id(0) == half)
        def _(ref=ref):
            ref[...] = value


def kept(rows, width):
    return pl.BlockSpec((rows, width), lambda i: (0, 0))


def sum_parts(parts):
    total = parts[0][...].astype(F32)
    for part in parts[1:]:
        total = total + part[...].astype(F32)
    return total


def middle_norm(tokens, parts, off, gain, bias):
    seg, width = tokens.shape
    count = len(parts)
    rows = seg // 2
    step = 32

    def kernel(*refs):
        tokens_ref, off_ref, gain_ref, bias_ref, middle_ref, *seconds = refs[2 * count :]
        off, gain, bias = off_ref[...], gain_ref[...], bias_ref[...]
        for half in range(2):

            def body(block, _):
                start = pl.multiple_of(block * step, step)
                at, whole = pl.ds(start, step), pl.ds(half * rows + start, step)
                total = tokens_ref[whole, :].astype(F32)
                for index in range(count):
                    total = total + refs[2 * index + half][at, :].astype(F32)
                total = total + off
                middle_ref[whole, :] = total
                seconds[half][at, :] = norm_apply(total, gain, bias).astype(BF16)
                return _

            lax.fori_loop(0, rows // step, body, 0)

    return pl.pallas_call(
        kernel,
        out_shape=(shape_of(seg, width, F32), shape_of(rows, width), shape_of(rows, width)),
        in_specs=[VMEM] * (2 * count + 4),
        out_specs=(VMEM,) * 3,
        name="middle_norm",
        **kernel_params(5),
    )(*flat_list(parts), tokens, off, gain, bias)


def middle_back(middle, cot, parts, gain):
    seg, width = middle.shape
    count = len(parts)
    rows = seg // 2

    def kernel(*refs):
        middle_ref, cot_ref, gain_ref, grad_ref, top_ref, bottom_ref, sums_ref = refs[count:]

        @pl.when(pl.program_id(0) == 0)
        def _():
            sums_ref[...] = jnp.zeros_like(sums_ref)

        grad = sum_parts(refs[:count])
        hat, inverse = norm_values(middle_ref[...])
        cots = cot_ref[...].astype(F32)
        total = cots + norm_back(hat, inverse, grad, gain_ref[...])
        low = total.astype(BF16)
        grad_ref[...] = total
        store_half([top_ref, bottom_ref], low)
        sums_ref[0:1, :] += column_sum(grad * hat)
        sums_ref[1:2, :] += column_sum(grad)
        sums_ref[2:3, :] += column_sum(low.astype(F32))
        sums_ref[3:4, :] += column_sum(cots)

    return pl.pallas_call(
        kernel,
        grid=(2,),
        out_shape=(
            shape_of(seg, width, F32),
            shape_of(rows, width),
            shape_of(rows, width),
            shape_of(4, width, F32),
        ),
        in_specs=[row_blocks(width, rows=rows)] * (count + 2) + [kept(1, width)],
        out_specs=(
            row_blocks(width, rows=rows),
            kept(rows, width),
            kept(rows, width),
            kept(4, width),
        ),
        name="middle_back",
        **kernel_params(5),
    )(*parts, middle, cot, gain)


def first_back(joined, parts, middle_grad, gain):
    seg, width = middle_grad.shape
    keys = joined.shape[0]
    count = len(parts)
    last = seg // NORM_ROWS - 1

    def kernel(*refs):
        joined_ref, middle_ref, gain_ref, tokens_ref, prior_ref, sums_ref = refs[count:]
        step = pl.program_id(0)

        @pl.when(step == 0)
        def _():
            sums_ref[...] = jnp.zeros_like(sums_ref)

        grad = sum_parts(refs[:count])
        hat, inverse = norm_values(joined_ref[...].astype(F32))
        sums_ref[0:1, :] += column_sum(grad * hat)
        sums_ref[1:2, :] += column_sum(grad)
        back = norm_back(hat, inverse, grad, gain_ref[...])

        @pl.when(step <= last)
        def _():
            tokens_ref[...] = middle_ref[...] + back

        @pl.when(step > last)
        def _():
            prior_ref[...] = back.astype(BF16)

    return pl.pallas_call(
        kernel,
        grid=(keys // NORM_ROWS,),
        out_shape=(
            shape_of(seg, width, F32),
            shape_of(keys - seg, width),
            shape_of(2, width, F32),
        ),
        in_specs=[row_blocks(width)] * (count + 1) + [row_blocks(width, last), kept(1, width)],
        out_specs=(row_blocks(width, last), kept(keys - seg, width), kept(2, width)),
        name="first_back",
        **kernel_params(500_000),
    )(*parts, joined, middle_grad, gain)


def beside_blocks(weights, members):
    rows, width = weights[0].shape
    cols = width // members
    count = len(weights)

    def kernel(*refs):
        out, sems = refs[count:]
        copies = []
        for member in range(members):
            for index in range(count):
                copies.append(
                    pltpu.make_async_copy(
                        refs[index].at[:, pl.ds(member * cols, cols)],
                        out.at[member, :, pl.ds(index * cols, cols)],
                        sems.at[member * count + index],
                    )
                )
        for copy in copies:
            copy.start()
        wait_all(copies)

    return pl.pallas_call(
        kernel,
        out_shape=jax.ShapeDtypeStruct((members, rows, count * cols), BF16),
        in_specs=[HBM] * count,
        out_specs=HBM,
        scratch_shapes=[pltpu.SemaphoreType.DMA((members * count,))],
        name="beside_blocks",
        **kernel_params(1),
    )(*weights)


def swap(value, rel):
    if rel == 0:
        return value
    count = lax.axis_size("fsdp")
    return lax.ppermute(value, "fsdp", [(i, i ^ rel) for i in range(count)])


def halves_of(value):
    rows = value.shape[0] // 2
    return [value[:rows], value[rows:]]


def spread_near(halves):
    near = range(1, min(lax.axis_size("fsdp"), 3))
    return [[swap(half, rel) for half in halves] for rel in near]


def spread_cut(near):
    return [halves_of(near[0][0])[0], halves_of(near[-1][0])[1]]


def spread_far(halves, near, *others, cut=None):
    members = lax.axis_size("fsdp")
    near, cut = lax.optimization_barrier((near, cut, others))[:2]
    pieces = [halves, *near]
    if members > 3:
        top, bottom = near[0][0], near[1][-1]
        if len(halves) == 1:
            top, bottom = cut or spread_cut(near)
        pieces.append([swap(top, 2), swap(bottom, 1)])
    return pieces + [[swap(half, rel) for half in halves] for rel in range(4, members)]


def after(value, *others):
    return lax.optimization_barrier((value, *others))[0]


def add_low(left, right):
    return (left.astype(F32) + right.astype(F32)).astype(BF16)


def output_halves(rel, halves, over, early):
    if over and rel == 2:
        return [add_low(halves[0], over[0]), early[1]], [False, True]
    if over and rel == 1:
        return [early[0], add_low(halves[1], over[1])], [True, False]
    return halves, [False, False]


def trade_blocks(blocks):
    return lax.all_to_all(blocks, "fsdp", 0, 0, tiled=True)


def doubled(rows, axis):
    size = lax.axis_size(axis)
    place = lax.axis_index(axis)
    step = 1
    while step < size:
        came = lax.ppermute(rows, axis, [(i, i ^ step) for i in range(size)])
        high = (place & step) != 0
        rows = jnp.concatenate([jnp.where(high, came, rows), jnp.where(high, rows, came)], 0)
        step *= 2
    return rows


def scatter_small(rows):
    return jnp.sum(lax.all_to_all(rows, BOTH, 0, 0, tiled=True), axis=0)


def gather_dp(value):
    return lax.all_gather(value, "dp", axis=0, tiled=True)


def scatter_dp(value, axis):
    return lax.psum_scatter(value, "dp", scatter_dimension=axis, tiled=True)


def shards(
    tokens,
    summaries,
    presence,
    seg_counts,
    ln1_gain,
    ln1_bias,
    w_query,
    query_bias,
    w_key,
    w_value,
    value_bias,
    w_out,
    out_bias,
    ln2_gain,
    ln2_bias,
    w_up,
    up_bias,
    w_down,
    down_bias,
    cotangent,
):
    members = lax.axis_size("fsdp")
    columns = lax.axis_size("dp")
    total = members * columns
    me = lax.axis_index("fsdp")
    seg_len, width = tokens.shape
    n_summary = summaries.shape[1]
    my_cols = width // members
    my_ff = w_up.shape[1] // members
    row_share = w_query.shape[0]
    rels = list(range(members))
    own_last = rels[::-1]

    def blocks_of(weight):
        return weight.reshape(row_share, members, -1).swapaxes(0, 1)

    def gathered(blocks):
        rows = blocks.reshape(members * row_share, -1)
        return gather_dp(rows).reshape(columns, members, row_share, -1)

    small_parts = (
        ln1_gain, ln1_bias, query_bias, value_bias, out_bias, ln2_gain, ln2_bias, up_bias,
        down_bias, presence[0].astype(BF16),
    )
    packed = doubled(jnp.concatenate(small_parts)[None], "fsdp")
    prior = jnp.pad(summaries[0], ((0, PRIOR_ROWS - n_summary), (0, 0)))
    prior = lax.ppermute(prior, BOTH, [(i, i + 1) for i in range(total - 1)])
    joined = jnp.concatenate([tokens, prior], 0)

    qkv_blocks = beside_blocks([w_query, w_key, w_value], members)
    qkv_blocks = trade_blocks(qkv_blocks)
    up_blocks, packed = lax.optimization_barrier((blocks_of(w_up), packed, qkv_blocks, joined))[:2]
    up_blocks = trade_blocks(up_blocks)
    attn_w = gathered(jnp.concatenate([qkv_blocks, blocks_of(w_out)], 2))
    up_w = gathered(up_blocks)
    down_w = gather_dp(w_down)

    joined_rows = [joined]
    joined_near = spread_near(after(joined_rows, up_blocks))
    group_joined = spread_far(joined_rows, joined_near)
    cot_rows = [cotangent]
    cot_near = spread_near(after(cot_rows, group_joined))
    packed = doubled(packed, "dp").reshape(columns, members, -1).swapaxes(0, 1)
    packed = packed.reshape(total, -1)

    smalls = []
    at = 0
    for part in small_parts:
        smalls.append(packed[:, at : at + part.shape[0]].astype(F32))
        at += part.shape[0]
    gain_one, bias_one, query_off, value_off, out_off, gain_two, bias_two, up_off, down_off = [
        part.reshape(1, -1) for part in smalls[:-1]
    ]
    present_all = smalls[-1]
    query_off = lax.dynamic_slice_in_dim(query_off, me * my_cols, my_cols, 1)
    value_off = lax.dynamic_slice_in_dim(value_off, me * my_cols, my_cols, 1)
    up_off = lax.dynamic_slice_in_dim(up_off, me * my_ff, my_ff, 1)
    qkv_off = jnp.concatenate([query_off, jnp.zeros_like(query_off), value_off], 1)

    starts = jnp.cumsum(seg_counts) - seg_counts
    group_places = (me ^ jnp.arange(members)) * columns + lax.axis_index("dp")
    has_prev = jnp.all(group_places[:, None] != starts[None, :], axis=1)
    summary_ok = jnp.logical_and(present_all[group_places] == 1, has_prev[:, None]).astype(F32)
    ok_rows = jnp.pad(summary_ok, ((0, 0), (seg_len, PRIOR_ROWS - n_summary)))
    ok_cols = jnp.broadcast_to(ok_rows[:, :, None], (*ok_rows.shape, PAIR))


    def part_type(rel):
        return BF16

    attn = {}
    middle_parts = {}
    previous = []
    for some in ([[3], [1, 2], [0]] if members == 4 else [[rel] for rel in own_last]):
        xs = [group_joined[rel] for rel in some]
        if some == [0]:
            previous = previous + flat_list(cot_near)
        xs[0] = [after(xs[0][0], *previous), *xs[0][1:]]
        oks = jnp.concatenate([ok_rows[rel : rel + 1] for rel in some], 0)
        outs = attn_forward(
            xs, gain_one, bias_one, qkv_off, oks, attn_w, [part_type(rel) for rel in some]
        )
        for rel, (low, qkv, lse, mixed, *part) in zip(some, outs):
            attn[rel] = (low, qkv, lse, mixed)
            middle_parts[rel] = part
            previous = [lse]
        if members > 3 and some == [3]:
            over = middle_parts.pop(3)
            middle_over = [swap(over[0], 1), swap(over[1], 2)]
    if members > 3:
        two, one = middle_parts[2], middle_parts[1]
        middle_parts[2] = [add_low(two[0], middle_over[0]), two[1]]
        middle_parts[1] = [one[0], add_low(one[1], middle_over[1])]
    middle_parts = {rel: [swap(half, rel) for half in part] for rel, part in middle_parts.items()}
    cot_cut = spread_cut(cot_near)
    middle, *second_own = middle_norm(
        after(tokens, cot_cut), list(middle_parts.values()), out_off, gain_two, bias_two
    )
    def ordered(values):
        return [values[rel] for rel in own_last]

    second_near = spread_near(second_own)
    hidden_own, slope_own = ffn_hidden([second_own], up_off, up_w)
    group_second = spread_far(second_own, second_near, hidden_own)
    hidden, slope = {0: hidden_own[0]}, {0: slope_own[0]}
    previous = hidden_own
    cuts = [1, members - 1, members] if members > 2 else [1, members]
    for low_rel, high_rel in zip(cuts, cuts[1:]):
        some = rels[low_rel:high_rel]
        seconds = [group_second[rel] for rel in some]
        seconds[0] = [after(seconds[0][0], *previous), *seconds[0][1:]]
        hiddens, slopes = ffn_hidden(seconds, up_off, up_w)
        for rel, one, other in zip(some, hiddens, slopes):
            hidden[rel], slope[rel] = one, other
        previous = hiddens[:1]
        if low_rel == 1:
            group_cot = spread_far(cot_rows, cot_near, previous, cut=cot_cut)
    down_partial = weight_grad(ordered(hidden), flat_list(ordered(group_cot)))
    down_share = scatter_dp(down_partial, 0)
    pre, up_sums, second_parts = [], [], {}
    for some in (own_last[:-1], [0]):
        if not some:
            continue
        cots = [group_cot[rel] for rel in some]
        cots[0] = [after(cots[0][0], *(pre[-1:] or [down_partial])), *cots[0][1:]]
        pre_some, sums, *backs = ffn_back(
            cots, [slope[rel] for rel in some], up_w, down_w, [part_type(rel) for rel in some]
        )
        pre.append(pre_some)
        up_sums.append(sums)
        for rel, back in zip(some, backs):
            second_parts[rel] = swap(back, rel)
    up_partial = weight_grad(flat_list(ordered(group_second)), pre)
    def to_row_blocks(grad):
        return scatter_dp(grad.reshape(members, columns * row_share, -1), 1)

    hiddens = ordered(hidden)
    hiddens[0] = after(hiddens[0], up_partial)
    output_parts = ffn_out(hiddens, down_w, [part_type(rel) for rel in own_last])
    output_parts = dict(zip(own_last, output_parts))
    second_parts = after(second_parts, output_parts)
    up_share = to_row_blocks(after(up_partial, second_parts))
    middle_grad, *branch_low, middle_sums = middle_back(
        middle, cotangent, [second_parts[rel] for rel in rels], gain_two
    )

    branch_near = spread_near(branch_low)
    grads, qkv_sums, joined_parts = {}, {}, {}

    def back_of(some, branches, *others):
        first = [after(branches[0][0], *others), *branches[0][1:]]
        outs = attn_backward(
            [first, *branches[1:]],
            [attn[rel][1] for rel in some],
            [attn[rel][2] for rel in some],
            [ok_cols[rel] for rel in some],
            attn_w,
            [part_type(rel) for rel in some],
        )
        for rel, (grad, sums, part) in zip(some, outs):
            grads[rel], qkv_sums[rel] = grad, sums
            joined_parts[rel] = swap(part, rel)

    back_of([0], [branch_low], down_share)
    group_branch = spread_far(branch_low, branch_near, qkv_sums[0])
    output_over = []
    if members > 3:
        far = after(output_parts.pop(3), qkv_sums[0])
        output_over = [swap(far[0], 1), swap(far[1], 2)]
    last = 0
    for some in ([[1, 2], [3]] if members == 4 else [[rel] for rel in rels[1:]]):
        others = output_over if some == [3] else []
        back_of(some, [group_branch[rel] for rel in some], qkv_sums[last], *others)
        last = some[-1]
    output_early = []
    if members > 3:
        early = after([output_parts[1][0], output_parts[2][1]], qkv_sums[2])
        output_early = [swap(early[0], 1), swap(early[1], 2)]
    attn_partial = attn_weight_grad(
        [attn[rel][0] for rel in rels],
        [grads[rel] for rel in rels],
        [attn[rel][3] for rel in rels],
        flat_list(group_branch),
    )
    joined_parts = after(joined_parts, attn_partial, output_early)
    attn_share = to_row_blocks(after(attn_partial, up_share))
    out_grad = (
        attn_share[:, :, 3 * my_cols :].swapaxes(0, 1).reshape(row_share, width).astype(F32)
    )
    qkv_shares = trade_blocks(attn_share[:, :, : 3 * my_cols])
    query_mat_grad, key_mat_grad, value_mat_grad = [
        qkv_shares[:, :, part * my_cols : (part + 1) * my_cols]
        .swapaxes(0, 1)
        .reshape(row_share, width)
        .astype(F32)
        for part in range(3)
    ]
    tokens_grad, prior_part, first_sums = first_back(
        joined, [joined_parts[rel] for rel in rels], middle_grad, gain_one
    )
    summary_grad = lax.ppermute(
        prior_part[:n_summary], BOTH, [(i + 1, i) for i in range(total - 1)]
    ).astype(F32)
    def whole(value):
        return value.reshape(total, -1)

    def sliced(value):
        mine = value.reshape(columns, -1)
        full = jnp.zeros((total, mine.shape[1]), F32)
        return lax.dynamic_update_slice_in_dim(full, mine, me * columns, 0)

    qkv_sums, middle_sums, up_sums = after((qkv_sums, middle_sums, up_sums), first_sums)
    qkv_sum = sum(qkv_sums[rel] for rel in rels)
    pieces = [
        whole(first_sums[0]),
        whole(first_sums[1]),
        sliced(qkv_sum[:, :my_cols]),
        sliced(qkv_sum[:, 2 * my_cols :]),
        whole(middle_sums[2]),
        whole(middle_sums[0]),
        whole(middle_sums[1]),
        sliced(sum(up_sums)),
        whole(middle_sums[3]),
    ]
    share = scatter_small(jnp.concatenate(pieces, 1))
    up_blocks = trade_blocks(after(up_share, share))
    output_parts = after(output_parts, share)
    output_parts = {
        rel: [half if early else swap(half, rel) for half, early in zip(*halves)]
        for rel, halves in (
            (rel, (output_halves(rel, halves, output_over, output_early)))
            for rel, halves in output_parts.items()
        )
    }
    down_grad = after(down_share, share).astype(F32)
    up_grad = up_blocks.swapaxes(0, 1).reshape(row_share, members * my_ff).astype(F32)
    output_sum = jnp.concatenate(
        [sum(halves[half].astype(F32) for halves in output_parts.values()) for half in range(2)], 0
    )
    output = (middle + output_sum + down_off).astype(BF16)
    outs = []
    at = 0
    for piece in pieces:
        outs.append(share[at : at + piece.shape[1]])
        at += piece.shape[1]
    return (
        output,
        tokens_grad,
        summary_grad[None],
        outs[0],
        outs[1],
        query_mat_grad,
        outs[2],
        key_mat_grad,
        value_mat_grad,
        outs[3],
        out_grad,
        outs[4],
        outs[5],
        outs[6],
        up_grad,
        outs[7],
        down_grad,
        outs[8],
    )


def solution(mesh):
    rows, rows2, rows3 = P(BOTH), P(BOTH, None), P(BOTH, None, None)
    return jax.shard_map(
        shards,
        mesh=mesh,
        in_specs=(
            rows2, rows3, rows2, P(), rows, rows, rows2, rows, rows2, rows2, rows, rows2, rows,
            rows, rows, rows2, rows, rows2, rows, rows2,
        ),
        out_specs=(
            rows2, rows2, rows3, rows, rows, rows2, rows, rows2, rows2, rows, rows2, rows, rows,
            rows, rows2, rows, rows2, rows,
        ),
        check_vma=False,
    )
```

```python
import functools
import jax
import jax.numpy as jnp
from jax import lax
from jax.experimental import pallas as pl
from jax.experimental.pallas import tpu as pltpu
from jax.sharding import PartitionSpec as P

F32, BF16 = jnp.float32, jnp.bfloat16
HEADS = 32
BOTH = ("fsdp", "dp")
HEAD = 64
PAIR = 2 * HEAD
PRIOR_ROWS = 64
NORM_ROWS = 64
MASKED = -1e30
GELU_A, GELU_B = 0.7978845608028654, 0.044715
VMEM_LIMIT = 53 * 1024 * 1024
VMEM = pl.BlockSpec(memory_space=pltpu.VMEM)
HBM = pl.BlockSpec(memory_space=pl.ANY)


def dot(left, right):
    return jnp.dot(left, right, preferred_element_type=F32)


def dot_t(left, right):
    return lax.dot_general(left, right, (((1,), (1,)), ((), ())), preferred_element_type=F32)


def t_dot(left, right):
    return lax.dot_general(left, right, (((0,), (0,)), ((), ())), preferred_element_type=F32)


def norm_parts(values):
    centre = values - jnp.mean(values, axis=-1, keepdims=True)
    spread = jnp.mean(centre * centre, axis=-1, keepdims=True)
    return centre, lax.rsqrt(spread + 1e-05)


def norm_apply(values, norm_gain, norm_bias):
    centre, inverse = norm_parts(values)
    return centre * inverse * norm_gain + norm_bias


def in_pair(half, rows):
    lane = lax.broadcasted_iota(jnp.int32, (rows, PAIR), 1)
    return (lane >= HEAD) if half else (lane < HEAD)


def pair_at(base, pair):
    return pl.ds(pl.multiple_of(base + pair * PAIR, PAIR), PAIR)


def load_blocks(hbm, scratch, sems):
    copies = [
        pltpu.make_async_copy(hbm.at[:, block], scratch.at[block], sems.at[block])
        for block in range(scratch.shape[0])
    ]
    for copy in copies:
        copy.start()
    return copies


def load_rows(parts, scratch, sems):
    copies = []
    at = 0
    for index, part in enumerate(parts):
        rows = part.shape[0]
        copies.append(
            pltpu.make_async_copy(part, scratch.at[pl.ds(at, rows)], sems.at[index])
        )
        at += rows
    for copy in copies:
        copy.start()
    return copies


def flat_list(lists):
    return [piece for some in lists for piece in some]


def wait_all(copies):
    for copy in copies:
        copy.wait()


def rows_of(ref, columns):
    value = ref[:, :, :, columns]
    return value.reshape(-1, value.shape[-1])


def block_of(ref, block, columns):
    value = ref[block, :, :, columns]
    return value.reshape(-1, value.shape[-1])


COST = 1_000_000


def kernel_params(cost):
    return dict(
        compiler_params=pltpu.CompilerParams(vmem_limit_bytes=VMEM_LIMIT),
        cost_estimate=pl.CostEstimate(flops=cost * COST, bytes_accessed=1, transcendentals=0),
    )


def shape_of(rows, columns, dtype=BF16):
    return jax.ShapeDtypeStruct((rows, columns), dtype)


def attn_forward(xs, gain, bias, off, ok_rows, attn_w, types):
    count = len(xs)
    pieces = flat_list(xs)
    given = len(pieces)
    keys, width = sum(piece.shape[0] for piece in xs[0]), pieces[0].shape[1]
    seg = keys - PRIOR_ROWS
    columns, members, share, wide = attn_w.shape
    cols = wide // 4

    def kernel(*refs):
        gain_ref, bias_ref, off_ref, ok_ref, attn_hbm = refs[given : given + 5]
        outs = refs[given + 5 : given + 5 + 6 * count]
        x_all, weights, mask, sems = refs[given + 5 + 6 * count :]
        x_copies = load_rows(refs[:given], x_all, sems.at[pl.ds(members, given)])
        copies = load_blocks(attn_hbm, weights, sems)
        gain, bias = gain_ref[...], bias_ref[...]
        wait_all(x_copies)
        for index in range(count):
            low_ref = outs[6 * index]

            def norm_rows(block, _):
                start = pl.multiple_of(block * NORM_ROWS, NORM_ROWS)
                values = x_all[pl.ds(index * keys + start, NORM_ROWS), :].astype(F32)
                low_ref[pl.ds(start, NORM_ROWS), :] = norm_apply(values, gain, bias).astype(BF16)
                return _

            lax.fori_loop(0, keys // NORM_ROWS, norm_rows, 0)
        wait_all(copies)
        for index in range(count):
            attend_segment(ok_ref[index : index + 1, :], off_ref, weights, mask, outs[6 * index : 6 * index + 6])

    def attend_segment(ok_row, off_ref, weights, mask, refs):
        low_ref, qkv_ref, lse_ref, mixed_ref, *parts = refs
        row = lax.broadcasted_iota(jnp.int32, (seg, keys), 0)
        col = lax.broadcasted_iota(jnp.int32, (seg, keys), 1)
        mask[...] = jnp.where(jnp.logical_or(col <= row, ok_row > 0.5), 0.0, MASKED)

        value = dot(low_ref[...], rows_of(weights, pl.ds(0, 3 * cols))) + off_ref[...]
        qkv_ref[...] = value.astype(BF16)
        lane = lax.broadcasted_iota(jnp.int32, (seg, PAIR), 1)

        def attend(pair, _):
            query = qkv_ref[:seg, pair_at(0, pair)] * jnp.asarray(HEAD**-0.5, BF16)
            key = qkv_ref[:, pair_at(cols, pair)]
            value = qkv_ref[:, pair_at(2 * cols, pair)]
            merged = None
            for half in range(2):
                inside = in_pair(half, seg)
                scores = dot_t(jnp.where(inside, query, jnp.zeros_like(query)), key) + mask[...]
                row_max = jnp.max(scores, axis=-1, keepdims=True)
                expo = jnp.exp(scores - row_max)
                row_total = jnp.sum(expo, axis=-1, keepdims=True)
                log_total = row_max + jnp.log(row_total)
                lse_ref[...] = jnp.where(lane == 2 * pair + half, log_total, lse_ref[...])
                mixed = dot((expo * (1.0 / row_total)).astype(BF16), value)
                merged = mixed if merged is None else jnp.where(inside, mixed, merged)
            mixed_ref[:, pair_at(0, pair)] = merged.astype(BF16)
            return _

        lse_ref[...] = jnp.zeros_like(lse_ref)
        lax.fori_loop(0, cols // PAIR, attend, 0)

        def project_out(block, _):
            at = pl.ds(pl.multiple_of(block * cols, PAIR), cols)
            weight = block_of(weights, block, pl.ds(3 * cols, cols))
            value = dot(mixed_ref[...], weight)
            for half, part in enumerate(parts):
                part[:, at] = value[half * seg // 2 : (half + 1) * seg // 2].astype(part.dtype)
            return _

        lax.fori_loop(0, members, project_out, 0)

    shapes = []
    for dtype in types:
        shapes += [
            shape_of(keys, width),
            shape_of(keys, 3 * cols),
            shape_of(seg, PAIR, F32),
            shape_of(seg, cols),
            shape_of(seg // 2, width, dtype),
            shape_of(seg // 2, width, dtype),
        ]
    outs = pl.pallas_call(
        kernel,
        out_shape=shapes,
        in_specs=[HBM] * given + [VMEM] * 4 + [HBM],
        out_specs=[VMEM] * len(shapes),
        scratch_shapes=[
            pltpu.VMEM((count * keys, width), BF16),
            pltpu.VMEM((members, columns, share, wide), BF16),
            pltpu.VMEM((seg, keys), F32),
            pltpu.SemaphoreType.DMA((members + given,)),
        ],
        name="attn_forward",
        **kernel_params(12 * count),
    )(*pieces, gain, bias, off, ok_rows, attn_w)
    return [outs[6 * index : 6 * index + 6] for index in range(count)]


def attn_backward(branches, qkvs, lses, ok_cols, attn_w, types):
    count = len(branches)
    pieces = flat_list(branches)
    given = len(pieces)
    seg, width = sum(piece.shape[0] for piece in branches[0]), pieces[0].shape[1]
    keys = qkvs[0].shape[0]
    columns, members, share, wide = attn_w.shape
    cols = wide // 4

    def kernel(*refs):
        ins = refs[given : given + 3 * count]
        attn_hbm = refs[given + 3 * count]
        outs = refs[given + 3 * count + 1 : given + 6 * count + 1]
        branch_all, weights, mask, lse_t, mixed_grad, sems = refs[given + 6 * count + 1 :]
        branch_copies = load_rows(refs[:given], branch_all, sems.at[pl.ds(members, given)])
        copies = load_blocks(attn_hbm, weights, sems)
        wait_all(branch_copies)
        for index in range(count):
            branch = branch_all.at[pl.ds(index * seg, seg)]
            some_in = [ins[index], ins[count + index], ins[2 * count + index]]
            some_out = outs[3 * index : 3 * index + 3]
            waits = copies if index == 0 else []
            back_segment(branch, *some_in, *some_out, weights, mask, lse_t, mixed_grad, waits)

    def back_segment(
        branch_ref, qkv_ref, lse_ref, ok_ref, grads_ref, sums_ref, joined_ref,
        weights, mask, lse_t, mixed_grad, waits,
    ):
        row = lax.broadcasted_iota(jnp.int32, (keys, seg), 0)
        col = lax.broadcasted_iota(jnp.int32, (keys, seg), 1)
        mask[...] = jnp.where(jnp.logical_or(row <= col, ok_ref[:, :1] > 0.5), 0.0, MASKED)
        lse_t[...] = lse_ref[...].T
        grads_ref[seg:, :cols] = jnp.zeros((keys - seg, cols), BF16)
        total = 0.0
        for block in range(members):
            wait_all(waits[block : block + 1])
            weight = block_of(weights, block, pl.ds(3 * cols, cols))
            total = total + dot_t(branch_ref[:, block * cols : (block + 1) * cols], weight)
        mixed_grad[...] = total.astype(BF16)

        def attend(pair, _):
            query = qkv_ref[:seg, pair_at(0, pair)]
            scaled = query * jnp.asarray(HEAD**-0.5, BF16)
            key = qkv_ref[:, pair_at(cols, pair)]
            value = qkv_ref[:, pair_at(2 * cols, pair)]
            mixed = mixed_grad[:, pair_at(0, pair)]
            query_grad = key_grad = value_grad = 0.0
            for half in range(2):
                inside, inside_key = in_pair(half, seg), in_pair(half, keys)
                zero = jnp.zeros_like(query)
                scores = dot_t(key, jnp.where(inside, scaled, zero)) + mask[...]
                probs = jnp.exp(scores - lse_t[pl.ds(2 * pair + half, 1), :])
                mixed_half = jnp.where(inside, mixed, zero)
                prob_grad = dot_t(value, mixed_half)
                value_grad = value_grad + dot(probs.astype(BF16), mixed_half)
                delta = jnp.sum(prob_grad * probs, axis=0, keepdims=True)
                score_grad = (probs * (prob_grad - delta)).astype(BF16)
                key_grad = key_grad + dot(score_grad, jnp.where(inside, query, zero))
                key_half = jnp.where(inside_key, key, jnp.zeros_like(key))
                query_grad = query_grad + t_dot(score_grad, key_half)
            grads_ref[:seg, pair_at(0, pair)] = (query_grad * HEAD**-0.5).astype(BF16)
            grads_ref[:, pair_at(cols, pair)] = (key_grad * HEAD**-0.5).astype(BF16)
            grads_ref[:, pair_at(2 * cols, pair)] = value_grad.astype(BF16)
            return _

        lax.fori_loop(0, cols // PAIR, attend, 0)

        def back(block, _):
            weight = block_of(weights, block, pl.ds(0, 3 * cols))
            at = pl.ds(pl.multiple_of(block * cols, PAIR), cols)
            joined_ref[:, at] = dot_t(grads_ref[...], weight).astype(joined_ref.dtype)
            return _

        lax.fori_loop(0, members, back, 0)
        sums_ref[...] = jnp.sum(grads_ref[...].astype(F32), axis=0, keepdims=True)

    shapes = []
    for dtype in types:
        shapes += [
            shape_of(keys, 3 * cols),
            shape_of(1, 3 * cols, F32),
            shape_of(keys, width, dtype),
        ]
    outs = pl.pallas_call(
        kernel,
        out_shape=shapes,
        in_specs=[HBM] * given + [VMEM] * (3 * count) + [HBM],
        out_specs=[VMEM] * len(shapes),
        scratch_shapes=[
            pltpu.VMEM((count * seg, width), BF16),
            pltpu.VMEM((members, columns, share, wide), BF16),
            pltpu.VMEM((keys, seg), F32),
            pltpu.VMEM((PAIR, seg), F32),
            pltpu.VMEM((seg, cols), BF16),
            pltpu.SemaphoreType.DMA((members + given,)),
        ],
        name="attn_backward",
        **kernel_params(12 * count),
    )(*pieces, *qkvs, *lses, *ok_cols, attn_w)
    return [outs[3 * index : 3 * index + 3] for index in range(count)]


def ffn_hidden(seconds, off, up_w):
    pieces = flat_list(seconds)
    given = len(pieces)
    width = pieces[0].shape[1]
    count = len(seconds)
    seg = sum(piece.shape[0] for piece in pieces) // count
    columns, members, share, wide = up_w.shape
    step = min(1024, wide)

    def kernel(*refs):
        off_ref, up_hbm = refs[given : given + 2]
        outs = refs[given + 2 : given + 2 + 2 * count]
        second, up, sems = refs[given + 2 + 2 * count :]
        copies = load_blocks(up_hbm, up, sems)
        wait_all(copies + load_rows(refs[:given], second, sems.at[pl.ds(members, given)]))

        def hidden(block, _):
            at = pl.ds(pl.multiple_of(block * step, step), step)
            weight = rows_of(up, at)
            for index in range(count):
                pre = dot(second[pl.ds(index * seg, seg), :], weight) + off_ref[:, at]
                square = pre * pre
                bent = jnp.tanh(GELU_A * pre * (1.0 + GELU_B * square))
                gate = 0.5 * (1.0 + bent)
                outs[index][:, at] = (pre * gate).astype(BF16)
                rise = 0.5 * pre * (1.0 - bent * bent) * (GELU_A * (1.0 + 3.0 * GELU_B * square))
                outs[count + index][:, at] = (gate + rise).astype(BF16)
            return _

        lax.fori_loop(0, wide // step, hidden, 0)

    outs = pl.pallas_call(
        kernel,
        out_shape=[shape_of(seg, wide)] * (2 * count),
        in_specs=[HBM] * given + [VMEM, HBM],
        out_specs=[VMEM] * (2 * count),
        scratch_shapes=[
            pltpu.VMEM((count * seg, width), BF16),
            pltpu.VMEM((members, columns, share, wide), BF16),
            pltpu.SemaphoreType.DMA((members + given,)),
        ],
        name="ffn_hidden",
        **kernel_params(6 * count),
    )(*pieces, off, up_w)
    return outs[:count], outs[count:]


def ffn_back(cots, slopes, up_w, down_w, types):
    pieces = flat_list(cots)
    given = len(pieces)
    count = len(slopes)
    seg, width = slopes[0].shape[0], pieces[0].shape[1]
    columns, members, share, wide = up_w.shape
    step = 512
    rows = count * seg
    loads = given + count

    def kernel(*refs):
        up_hbm, down_hbm, pre_ref, sums_ref = refs[loads : loads + 4]
        backs = refs[loads + 4 : loads + 4 + count]
        cot, slope, up, down, sems = refs[loads + 4 + count :]
        first = load_rows(refs[:given], cot, sems)
        first += load_rows([down_hbm], down, sems.at[pl.ds(loads, 1)])
        first += load_rows(refs[given:loads], slope, sems.at[pl.ds(given, count)])
        later = load_blocks(up_hbm, up, sems.at[pl.ds(loads + 1, members)])
        wait_all(first)

        def grad(block, _):
            at = pl.ds(pl.multiple_of(block * step, step), step)
            value = dot_t(cot[...], down[at, :]) * slope[:, at].astype(F32)
            value = value.astype(BF16)
            pre_ref[:, at] = value
            sums_ref[:, at] = jnp.sum(value.astype(F32), axis=0, keepdims=True)
            return _

        lax.fori_loop(0, wide // step, grad, 0)
        wait_all(later)
        deep = columns * share

        def back(block, _):
            at = pl.ds(pl.multiple_of(block * deep, PAIR), deep)
            value = dot_t(pre_ref[...], up[block].reshape(deep, wide))
            for index in range(count):
                backs[index][:, at] = value[index * seg : (index + 1) * seg].astype(types[index])
            return _

        lax.fori_loop(0, members, back, 0)

    return pl.pallas_call(
        kernel,
        out_shape=(
            shape_of(rows, wide),
            shape_of(1, wide, F32),
            *[shape_of(seg, width, dtype) for dtype in types],
        ),
        in_specs=[HBM] * (loads + 2),
        out_specs=(VMEM,) * (2 + count),
        scratch_shapes=[
            pltpu.VMEM((rows, width), BF16),
            pltpu.VMEM((rows, wide), BF16),
            pltpu.VMEM((members, columns, share, wide), BF16),
            pltpu.VMEM((wide, width), BF16),
            pltpu.SemaphoreType.DMA((loads + 1 + members,)),
        ],
        name="ffn_back",
        **kernel_params(10 * count),
    )(*pieces, *slopes, up_w, down_w)


def ffn_out(hiddens, down_w, types):
    count = len(types)
    seg, wide = hiddens[0].shape
    rows = seg // 2
    width = down_w.shape[1]
    step = min(1024, width)

    def kernel(*refs):
        down_ref = refs[count]
        outs = refs[count + 1 : 3 * count + 1]
        hidden, sems = refs[3 * count + 1 :]
        wait_all(load_rows(refs[:count], hidden, sems))

        def block(part, _):
            at = pl.ds(pl.multiple_of(part * step, step), step)
            value = dot(hidden[...], down_ref[:, at])
            for index in range(2 * count):
                half = value[index * rows : (index + 1) * rows]
                outs[index][:, at] = half.astype(types[index // 2])
            return _

        lax.fori_loop(0, width // step, block, 0)

    outs = pl.pallas_call(
        kernel,
        out_shape=[shape_of(rows, width, types[index // 2]) for index in range(2 * count)],
        in_specs=[HBM] * count + [VMEM],
        out_specs=[VMEM] * (2 * count),
        scratch_shapes=[
            pltpu.VMEM((count * seg, wide), BF16),
            pltpu.SemaphoreType.DMA((count,)),
        ],
        name="ffn_out",
        **kernel_params(18),
    )(*hiddens, down_w)
    return [outs[2 * index : 2 * index + 2] for index in range(count)]


def weight_grad(lefts, rights):
    tall, wide = lefts[0].shape[1], rights[0].shape[1]
    deep = sum(left.shape[0] for left in lefts)
    counts = len(lefts), len(rights)
    rows_each = min(512, tall)
    both = sum(counts)

    def kernel(*refs):
        out_ref, left, right, sems = refs[both:]
        step = pl.program_id(0)

        @pl.when(step == 0)
        def _():
            copies = load_rows(refs[: counts[0]], left, sems)
            wait_all(copies + load_rows(refs[counts[0] : both], right, sems.at[pl.ds(counts[0], counts[1])]))

        at = pl.ds(pl.multiple_of(step * rows_each, rows_each), rows_each)
        out_ref[...] = t_dot(left[:, at], right[...]).astype(BF16)

    return pl.pallas_call(
        kernel,
        grid=(tall // rows_each,),
        out_shape=shape_of(tall, wide),
        in_specs=[HBM] * both,
        out_specs=pl.BlockSpec((rows_each, wide), lambda i: (i, 0)),
        scratch_shapes=[
            pltpu.VMEM((deep, tall), BF16),
            pltpu.VMEM((deep, wide), BF16),
            pltpu.SemaphoreType.DMA((both,)),
        ],
        name="weight_grad",
        **kernel_params(17),
    )(*lefts, *rights)


def attn_weight_grad(lows, grads, mixeds, branches):
    lists = lows, grads, mixeds, branches
    width, cols = lows[0].shape[1], mixeds[0].shape[1]
    rows_each = min(512, cols)
    halves = cols // rows_each
    ends = [0]
    for some in lists:
        ends.append(ends[-1] + len(some))

    def kernel(*refs):
        out_ref, low, grad, mixed, branch, sems = refs[ends[-1] :]
        step = pl.program_id(0)

        @pl.when(step == 0)
        def _():
            copies = []
            for first, last, scratch in zip(ends, ends[1:], (low, grad, mixed, branch)):
                copies += load_rows(refs[first:last], scratch, sems.at[pl.ds(first, last - first)])
            wait_all(copies)

        at = pl.ds(pl.multiple_of(step * rows_each, rows_each), rows_each)
        out_ref[:, : 3 * cols] = t_dot(low[:, at], grad[...]).astype(BF16)
        half = pl.ds(pl.multiple_of((step % halves) * rows_each, rows_each), rows_each)
        block = pl.ds(pl.multiple_of((step // halves) * cols, PAIR), cols)
        out_ref[:, 3 * cols :] = t_dot(mixed[:, half], branch[:, block]).astype(BF16)

    return pl.pallas_call(
        kernel,
        grid=(width // rows_each,),
        out_shape=shape_of(width, 4 * cols),
        in_specs=[HBM] * ends[-1],
        out_specs=pl.BlockSpec((rows_each, 4 * cols), lambda i: (i, 0)),
        scratch_shapes=[
            pltpu.VMEM((sum(one.shape[0] for one in some), some[0].shape[1]), BF16)
            for some in lists
        ]
        + [pltpu.SemaphoreType.DMA((ends[-1],))],
        name="attn_weight_grad",
        **kernel_params(21),
    )(*lows, *grads, *mixeds, *branches)


def norm_values(values):
    centre, inverse = norm_parts(values)
    return centre * inverse, inverse


def norm_back(hat, inverse, grad, gain):
    hat_grad = grad * gain
    mean = jnp.mean(hat_grad, axis=-1, keepdims=True)
    along = jnp.mean(hat_grad * hat, axis=-1, keepdims=True)
    return inverse * (hat_grad - mean - hat * along)


def column_sum(value):
    return jnp.sum(value, axis=0, keepdims=True)


def row_blocks(width, last=None, rows=NORM_ROWS):
    if last is None:
        return pl.BlockSpec((rows, width), lambda i: (i, 0))
    return pl.BlockSpec((rows, width), lambda i: (jnp.minimum(i, last), 0))


def store_half(refs, value):
    for half, ref in enumerate(refs):

        @pl.when(pl.program_id(0) == half)
        def _(ref=ref):
            ref[...] = value


def kept(rows, width):
    return pl.BlockSpec((rows, width), lambda i: (0, 0))


def sum_parts(parts):
    total = parts[0][...].astype(F32)
    for part in parts[1:]:
        total = total + part[...].astype(F32)
    return total


def middle_norm(tokens, parts, off, gain, bias):
    seg, width = tokens.shape
    count = len(parts)
    rows = seg // 2
    step = 32

    def kernel(*refs):
        tokens_ref, off_ref, gain_ref, bias_ref, middle_ref, *seconds = refs[2 * count :]
        off, gain, bias = off_ref[...], gain_ref[...], bias_ref[...]
        for half in range(2):

            def body(block, _):
                start = pl.multiple_of(block * step, step)
                at, whole = pl.ds(start, step), pl.ds(half * rows + start, step)
                total = tokens_ref[whole, :].astype(F32)
                for index in range(count):
                    total = total + refs[2 * index + half][at, :].astype(F32)
                total = total + off
                middle_ref[whole, :] = total
                seconds[half][at, :] = norm_apply(total, gain, bias).astype(BF16)
                return _

            lax.fori_loop(0, rows // step, body, 0)

    return pl.pallas_call(
        kernel,
        out_shape=(shape_of(seg, width, F32), shape_of(rows, width), shape_of(rows, width)),
        in_specs=[VMEM] * (2 * count + 4),
        out_specs=(VMEM,) * 3,
        name="middle_norm",
        **kernel_params(5),
    )(*flat_list(parts), tokens, off, gain, bias)


def middle_back(middle, cot, parts, gain):
    seg, width = middle.shape
    count = len(parts)
    rows = seg // 2

    def kernel(*refs):
        middle_ref, cot_ref, gain_ref, grad_ref, top_ref, bottom_ref, sums_ref = refs[count:]

        @pl.when(pl.program_id(0) == 0)
        def _():
            sums_ref[...] = jnp.zeros_like(sums_ref)

        grad = sum_parts(refs[:count])
        hat, inverse = norm_values(middle_ref[...])
        cots = cot_ref[...].astype(F32)
        total = cots + norm_back(hat, inverse, grad, gain_ref[...])
        low = total.astype(BF16)
        grad_ref[...] = total
        store_half([top_ref, bottom_ref], low)
        sums_ref[0:1, :] += column_sum(grad * hat)
        sums_ref[1:2, :] += column_sum(grad)
        sums_ref[2:3, :] += column_sum(low.astype(F32))
        sums_ref[3:4, :] += column_sum(cots)

    return pl.pallas_call(
        kernel,
        grid=(2,),
        out_shape=(
            shape_of(seg, width, F32),
            shape_of(rows, width),
            shape_of(rows, width),
            shape_of(4, width, F32),
        ),
        in_specs=[row_blocks(width, rows=rows)] * (count + 2) + [kept(1, width)],
        out_specs=(
            row_blocks(width, rows=rows),
            kept(rows, width),
            kept(rows, width),
            kept(4, width),
        ),
        name="middle_back",
        **kernel_params(5),
    )(*parts, middle, cot, gain)


def first_back(joined, parts, middle_grad, gain):
    seg, width = middle_grad.shape
    keys = joined.shape[0]
    count = len(parts)
    last = seg // NORM_ROWS - 1

    def kernel(*refs):
        joined_ref, middle_ref, gain_ref, tokens_ref, prior_ref, sums_ref = refs[count:]
        step = pl.program_id(0)

        @pl.when(step == 0)
        def _():
            sums_ref[...] = jnp.zeros_like(sums_ref)

        grad = sum_parts(refs[:count])
        hat, inverse = norm_values(joined_ref[...].astype(F32))
        sums_ref[0:1, :] += column_sum(grad * hat)
        sums_ref[1:2, :] += column_sum(grad)
        back = norm_back(hat, inverse, grad, gain_ref[...])

        @pl.when(step <= last)
        def _():
            tokens_ref[...] = middle_ref[...] + back

        @pl.when(step > last)
        def _():
            prior_ref[...] = back.astype(BF16)

    return pl.pallas_call(
        kernel,
        grid=(keys // NORM_ROWS,),
        out_shape=(
            shape_of(seg, width, F32),
            shape_of(keys - seg, width),
            shape_of(2, width, F32),
        ),
        in_specs=[row_blocks(width)] * (count + 1) + [row_blocks(width, last), kept(1, width)],
        out_specs=(row_blocks(width, last), kept(keys - seg, width), kept(2, width)),
        name="first_back",
        **kernel_params(500_000),
    )(*parts, joined, middle_grad, gain)


def beside_blocks(weights, members):
    rows, width = weights[0].shape
    cols = width // members
    count = len(weights)

    def kernel(*refs):
        out, sems = refs[count:]
        copies = []
        for member in range(members):
            for index in range(count):
                copies.append(
                    pltpu.make_async_copy(
                        refs[index].at[:, pl.ds(member * cols, cols)],
                        out.at[member, :, pl.ds(index * cols, cols)],
                        sems.at[member * count + index],
                    )
                )
        for copy in copies:
            copy.start()
        wait_all(copies)

    return pl.pallas_call(
        kernel,
        out_shape=jax.ShapeDtypeStruct((members, rows, count * cols), BF16),
        in_specs=[HBM] * count,
        out_specs=HBM,
        scratch_shapes=[pltpu.SemaphoreType.DMA((members * count,))],
        name="beside_blocks",
        **kernel_params(1),
    )(*weights)


def swap(value, rel):
    if rel == 0:
        return value
    count = lax.axis_size("fsdp")
    return lax.ppermute(value, "fsdp", [(i, i ^ rel) for i in range(count)])


def halves_of(value):
    rows = value.shape[0] // 2
    return [value[:rows], value[rows:]]


def spread_near(halves):
    near = range(1, min(lax.axis_size("fsdp"), 3))
    return [[swap(half, rel) for half in halves] for rel in near]


def spread_cut(near):
    return [halves_of(near[0][0])[0], halves_of(near[-1][0])[1]]


def spread_far(halves, near, *others, cut=None):
    members = lax.axis_size("fsdp")
    near, cut = lax.optimization_barrier((near, cut, others))[:2]
    pieces = [halves, *near]
    if members > 3:
        top, bottom = near[0][0], near[1][-1]
        if len(halves) == 1:
            top, bottom = cut or spread_cut(near)
        pieces.append([swap(top, 2), swap(bottom, 1)])
    return pieces + [[swap(half, rel) for half in halves] for rel in range(4, members)]


def after(value, *others):
    return lax.optimization_barrier((value, *others))[0]


def add_low(left, right):
    return (left.astype(F32) + right.astype(F32)).astype(BF16)


def output_halves(rel, halves, over, early):
    if over and rel == 2:
        return [add_low(halves[0], over[0]), early[1]], [False, True]
    if over and rel == 1:
        return [early[0], add_low(halves[1], over[1])], [True, False]
    return halves, [False, False]


def trade_blocks(blocks):
    return lax.all_to_all(blocks, "fsdp", 0, 0, tiled=True)


def doubled(rows, axis):
    size = lax.axis_size(axis)
    place = lax.axis_index(axis)
    step = 1
    while step < size:
        came = lax.ppermute(rows, axis, [(i, i ^ step) for i in range(size)])
        high = (place & step) != 0
        rows = jnp.concatenate([jnp.where(high, came, rows), jnp.where(high, rows, came)], 0)
        step *= 2
    return rows


def scatter_small(rows):
    return jnp.sum(lax.all_to_all(rows, BOTH, 0, 0, tiled=True), axis=0)


def gather_dp(value):
    return lax.all_gather(value, "dp", axis=0, tiled=True)


def scatter_dp(value, axis):
    return lax.psum_scatter(value, "dp", scatter_dimension=axis, tiled=True)


def shards(
    tokens,
    summaries,
    presence,
    seg_counts,
    ln1_gain,
    ln1_bias,
    w_query,
    query_bias,
    w_key,
    w_value,
    value_bias,
    w_out,
    out_bias,
    ln2_gain,
    ln2_bias,
    w_up,
    up_bias,
    w_down,
    down_bias,
    cotangent,
):
    members = lax.axis_size("fsdp")
    columns = lax.axis_size("dp")
    total = members * columns
    me = lax.axis_index("fsdp")
    seg_len, width = tokens.shape
    n_summary = summaries.shape[1]
    my_cols = width // members
    my_ff = w_up.shape[1] // members
    row_share = w_query.shape[0]
    rels = list(range(members))
    own_last = rels[::-1]

    def blocks_of(weight):
        return weight.reshape(row_share, members, -1).swapaxes(0, 1)

    def gathered(blocks):
        rows = blocks.reshape(members * row_share, -1)
        return gather_dp(rows).reshape(columns, members, row_share, -1)

    small_parts = (
        ln1_gain, ln1_bias, query_bias, value_bias, out_bias, ln2_gain, ln2_bias, up_bias,
        down_bias, presence[0].astype(BF16),
    )
    packed = doubled(jnp.concatenate(small_parts)[None], "fsdp")
    prior = jnp.pad(summaries[0], ((0, PRIOR_ROWS - n_summary), (0, 0)))
    prior = lax.ppermute(prior, BOTH, [(i, i + 1) for i in range(total - 1)])
    joined = jnp.concatenate([tokens, prior], 0)

    qkv_blocks = beside_blocks([w_query, w_key, w_value], members)
    qkv_blocks = trade_blocks(qkv_blocks)
    up_blocks, packed = lax.optimization_barrier((blocks_of(w_up), packed, qkv_blocks, joined))[:2]
    up_blocks = trade_blocks(up_blocks)
    attn_w = gathered(jnp.concatenate([qkv_blocks, blocks_of(w_out)], 2))
    up_w = gathered(up_blocks)
    down_w = gather_dp(w_down)

    joined_rows = [joined]
    joined_near = spread_near(after(joined_rows, up_blocks))
    group_joined = spread_far(joined_rows, joined_near)
    cot_rows = [cotangent]
    cot_near = spread_near(after(cot_rows, group_joined))
    packed = doubled(packed, "dp").reshape(columns, members, -1).swapaxes(0, 1)
    packed = packed.reshape(total, -1)

    smalls = []
    at = 0
    for part in small_parts:
        smalls.append(packed[:, at : at + part.shape[0]].astype(F32))
        at += part.shape[0]
    gain_one, bias_one, query_off, value_off, out_off, gain_two, bias_two, up_off, down_off = [
        part.reshape(1, -1) for part in smalls[:-1]
    ]
    present_all = smalls[-1]
    query_off = lax.dynamic_slice_in_dim(query_off, me * my_cols, my_cols, 1)
    value_off = lax.dynamic_slice_in_dim(value_off, me * my_cols, my_cols, 1)
    up_off = lax.dynamic_slice_in_dim(up_off, me * my_ff, my_ff, 1)
    qkv_off = jnp.concatenate([query_off, jnp.zeros_like(query_off), value_off], 1)

    starts = jnp.cumsum(seg_counts) - seg_counts
    group_places = (me ^ jnp.arange(members)) * columns + lax.axis_index("dp")
    has_prev = jnp.all(group_places[:, None] != starts[None, :], axis=1)
    summary_ok = jnp.logical_and(present_all[group_places] == 1, has_prev[:, None]).astype(F32)
    ok_rows = jnp.pad(summary_ok, ((0, 0), (seg_len, PRIOR_ROWS - n_summary)))
    ok_cols = jnp.broadcast_to(ok_rows[:, :, None], (*ok_rows.shape, PAIR))


    def part_type(rel):
        return BF16

    attn = {}
    middle_parts = {}
    previous = []
    for some in ([[3], [1, 2], [0]] if members == 4 else [[rel] for rel in own_last]):
        xs = [group_joined[rel] for rel in some]
        if some == [0]:
            previous = previous + flat_list(cot_near)
        xs[0] = [after(xs[0][0], *previous), *xs[0][1:]]
        oks = jnp.concatenate([ok_rows[rel : rel + 1] for rel in some], 0)
        outs = attn_forward(
            xs, gain_one, bias_one, qkv_off, oks, attn_w, [part_type(rel) for rel in some]
        )
        for rel, (low, qkv, lse, mixed, *part) in zip(some, outs):
            attn[rel] = (low, qkv, lse, mixed)
            middle_parts[rel] = part
            previous = [lse]
        if members > 3 and some == [3]:
            over = middle_parts.pop(3)
            middle_over = [swap(over[0], 1), swap(over[1], 2)]
    if members > 3:
        two, one = middle_parts[2], middle_parts[1]
        middle_parts[2] = [add_low(two[0], middle_over[0]), two[1]]
        middle_parts[1] = [one[0], add_low(one[1], middle_over[1])]
    middle_parts = {rel: [swap(half, rel) for half in part] for rel, part in middle_parts.items()}
    cot_cut = spread_cut(cot_near)
    middle, *second_own = middle_norm(
        after(tokens, cot_cut), list(middle_parts.values()), out_off, gain_two, bias_two
    )
    def ordered(values):
        return [values[rel] for rel in own_last]

    second_near = spread_near(second_own)
    hidden_own, slope_own = ffn_hidden([second_own], up_off, up_w)
    group_second = spread_far(second_own, second_near, hidden_own)
    hidden, slope = {0: hidden_own[0]}, {0: slope_own[0]}
    previous = hidden_own
    cuts = [1, members - 1, members] if members > 2 else [1, members]
    for low_rel, high_rel in zip(cuts, cuts[1:]):
        some = rels[low_rel:high_rel]
        seconds = [group_second[rel] for rel in some]
        seconds[0] = [after(seconds[0][0], *previous), *seconds[0][1:]]
        hiddens, slopes = ffn_hidden(seconds, up_off, up_w)
        for rel, one, other in zip(some, hiddens, slopes):
            hidden[rel], slope[rel] = one, other
        previous = hiddens[:1]
        if low_rel == 1:
            group_cot = spread_far(cot_rows, cot_near, previous, cut=cot_cut)
    down_partial = weight_grad(ordered(hidden), flat_list(ordered(group_cot)))
    down_share = scatter_dp(down_partial, 0)
    pre, up_sums, second_parts = [], [], {}
    for some in (own_last[:-1], [0]):
        if not some:
            continue
        cots = [group_cot[rel] for rel in some]
        cots[0] = [after(cots[0][0], *(pre[-1:] or [down_partial])), *cots[0][1:]]
        pre_some, sums, *backs = ffn_back(
            cots, [slope[rel] for rel in some], up_w, down_w, [part_type(rel) for rel in some]
        )
        pre.append(pre_some)
        up_sums.append(sums)
        for rel, back in zip(some, backs):
            second_parts[rel] = swap(back, rel)
    up_partial = weight_grad(flat_list(ordered(group_second)), pre)
    def to_row_blocks(grad):
        return scatter_dp(grad.reshape(members, columns * row_share, -1), 1)

    hiddens = ordered(hidden)
    hiddens[0] = after(hiddens[0], up_partial)
    output_parts = ffn_out(hiddens, down_w, [part_type(rel) for rel in own_last])
    output_parts = dict(zip(own_last, output_parts))
    second_parts = after(second_parts, output_parts)
    up_share = to_row_blocks(after(up_partial, second_parts))
    middle_grad, *branch_low, middle_sums = middle_back(
        middle, cotangent, [second_parts[rel] for rel in rels], gain_two
    )

    branch_near = spread_near(branch_low)
    grads, qkv_sums, joined_parts = {}, {}, {}

    def back_of(some, branches, *others):
        first = [after(branches[0][0], *others), *branches[0][1:]]
        outs = attn_backward(
            [first, *branches[1:]],
            [attn[rel][1] for rel in some],
            [attn[rel][2] for rel in some],
            [ok_cols[rel] for rel in some],
            attn_w,
            [part_type(rel) for rel in some],
        )
        for rel, (grad, sums, part) in zip(some, outs):
            grads[rel], qkv_sums[rel] = grad, sums
            joined_parts[rel] = swap(part, rel)

    back_of([0], [branch_low], down_share)
    group_branch = spread_far(branch_low, branch_near, qkv_sums[0])
    output_over = []
    if members > 3:
        far = after(output_parts.pop(3), qkv_sums[0])
        output_over = [swap(far[0], 1), swap(far[1], 2)]
    last = 0
    for some in ([[1, 2], [3]] if members == 4 else [[rel] for rel in rels[1:]]):
        others = output_over if some == [3] else []
        back_of(some, [group_branch[rel] for rel in some], qkv_sums[last], *others)
        last = some[-1]
    output_early = []
    if members > 3:
        early = after([output_parts[1][0], output_parts[2][1]], qkv_sums[2])
        output_early = [swap(early[0], 1), swap(early[1], 2)]
    attn_partial = attn_weight_grad(
        [attn[rel][0] for rel in rels],
        [grads[rel] for rel in rels],
        [attn[rel][3] for rel in rels],
        flat_list(group_branch),
    )
    joined_parts = after(joined_parts, attn_partial, output_early)
    attn_share = to_row_blocks(after(attn_partial, up_share))
    out_grad = (
        attn_share[:, :, 3 * my_cols :].swapaxes(0, 1).reshape(row_share, width).astype(F32)
    )
    qkv_shares = trade_blocks(attn_share[:, :, : 3 * my_cols])
    query_mat_grad, key_mat_grad, value_mat_grad = [
        qkv_shares[:, :, part * my_cols : (part + 1) * my_cols]
        .swapaxes(0, 1)
        .reshape(row_share, width)
        .astype(F32)
        for part in range(3)
    ]
    tokens_grad, prior_part, first_sums = first_back(
        joined, [joined_parts[rel] for rel in rels], middle_grad, gain_one
    )
    summary_grad = lax.ppermute(
        prior_part[:n_summary], BOTH, [(i + 1, i) for i in range(total - 1)]
    ).astype(F32)
    def whole(value):
        return value.reshape(total, -1)

    def sliced(value):
        mine = value.reshape(columns, -1)
        full = jnp.zeros((total, mine.shape[1]), F32)
        return lax.dynamic_update_slice_in_dim(full, mine, me * columns, 0)

    qkv_sums, middle_sums, up_sums = after((qkv_sums, middle_sums, up_sums), first_sums)
    qkv_sum = sum(qkv_sums[rel] for rel in rels)
    pieces = [
        whole(first_sums[0]),
        whole(first_sums[1]),
        sliced(qkv_sum[:, :my_cols]),
        sliced(qkv_sum[:, 2 * my_cols :]),
        whole(middle_sums[2]),
        whole(middle_sums[0]),
        whole(middle_sums[1]),
        sliced(sum(up_sums)),
        whole(middle_sums[3]),
    ]
    share = scatter_small(jnp.concatenate(pieces, 1))
    up_blocks = trade_blocks(after(up_share, share))
    output_parts = after(output_parts, share)
    output_parts = {
        rel: [half if early else swap(half, rel) for half, early in zip(*halves)]
        for rel, halves in (
            (rel, (output_halves(rel, halves, output_over, output_early)))
            for rel, halves in output_parts.items()
        )
    }
    down_grad = after(down_share, share).astype(F32)
    up_grad = up_blocks.swapaxes(0, 1).reshape(row_share, members * my_ff).astype(F32)
    output_sum = jnp.concatenate(
        [sum(halves[half].astype(F32) for halves in output_parts.values()) for half in range(2)], 0
    )
    output = (middle + output_sum + down_off).astype(BF16)
    outs = []
    at = 0
    for piece in pieces:
        outs.append(share[at : at + piece.shape[1]])
        at += piece.shape[1]
    return (
        output,
        tokens_grad,
        summary_grad[None],
        outs[0],
        outs[1],
        query_mat_grad,
        outs[2],
        key_mat_grad,
        value_mat_grad,
        outs[3],
        out_grad,
        outs[4],
        outs[5],
        outs[6],
        up_grad,
        outs[7],
        down_grad,
        outs[8],
    )


def solution(mesh):
    rows, rows2, rows3 = P(BOTH), P(BOTH, None), P(BOTH, None, None)
    return jax.shard_map(
        shards,
        mesh=mesh,
        in_specs=(
            rows2, rows3, rows2, P(), rows, rows, rows2, rows, rows2, rows2, rows, rows2, rows,
            rows, rows, rows2, rows, rows2, rows, rows2,
        ),
        out_specs=(
            rows2, rows2, rows3, rows, rows, rows2, rows, rows2, rows2, rows, rows2, rows, rows,
            rows, rows2, rows, rows2, rows,
        ),
        check_vma=False,
    )
```

```python
import functools
import jax
import jax.numpy as jnp
from jax import lax
from jax.experimental import pallas as pl
from jax.experimental.pallas import tpu as pltpu
from jax.sharding import PartitionSpec as P

F32, BF16 = jnp.float32, jnp.bfloat16
HEADS = 32
BOTH = ("fsdp", "dp")
HEAD = 64
PAIR = 2 * HEAD
PRIOR_ROWS = 64
NORM_ROWS = 64
MASKED = -1e30
GELU_A, GELU_B = 0.7978845608028654, 0.044715
VMEM_LIMIT = 53 * 1024 * 1024
VMEM = pl.BlockSpec(memory_space=pltpu.VMEM)
HBM = pl.BlockSpec(memory_space=pl.ANY)


def dot(left, right):
    return jnp.dot(left, right, preferred_element_type=F32)


def dot_t(left, right):
    return lax.dot_general(left, right, (((1,), (1,)), ((), ())), preferred_element_type=F32)


def t_dot(left, right):
    return lax.dot_general(left, right, (((0,), (0,)), ((), ())), preferred_element_type=F32)


def norm_parts(values):
    centre = values - jnp.mean(values, axis=-1, keepdims=True)
    spread = jnp.mean(centre * centre, axis=-1, keepdims=True)
    return centre, lax.rsqrt(spread + 1e-05)


def norm_apply(values, norm_gain, norm_bias):
    centre, inverse = norm_parts(values)
    return centre * inverse * norm_gain + norm_bias


def in_pair(half, rows):
    lane = lax.broadcasted_iota(jnp.int32, (rows, PAIR), 1)
    return (lane >= HEAD) if half else (lane < HEAD)


def pair_at(base, pair):
    return pl.ds(pl.multiple_of(base + pair * PAIR, PAIR), PAIR)


def load_blocks(hbm, scratch, sems):
    copies = [
        pltpu.make_async_copy(hbm.at[:, block], scratch.at[block], sems.at[block])
        for block in range(scratch.shape[0])
    ]
    for copy in copies:
        copy.start()
    return copies


def load_rows(parts, scratch, sems):
    copies = []
    at = 0
    for index, part in enumerate(parts):
        rows = part.shape[0]
        copies.append(
            pltpu.make_async_copy(part, scratch.at[pl.ds(at, rows)], sems.at[index])
        )
        at += rows
    for copy in copies:
        copy.start()
    return copies


def flat_list(lists):
    return [piece for some in lists for piece in some]


def wait_all(copies):
    for copy in copies:
        copy.wait()


def rows_of(ref, columns):
    value = ref[:, :, :, columns]
    return value.reshape(-1, value.shape[-1])


def block_of(ref, block, columns):
    value = ref[block, :, :, columns]
    return value.reshape(-1, value.shape[-1])


COST = 1_000_000


def kernel_params(cost):
    return dict(
        compiler_params=pltpu.CompilerParams(vmem_limit_bytes=VMEM_LIMIT),
        cost_estimate=pl.CostEstimate(flops=cost * COST, bytes_accessed=1, transcendentals=0),
    )


def shape_of(rows, columns, dtype=BF16):
    return jax.ShapeDtypeStruct((rows, columns), dtype)


def attn_forward(xs, gain, bias, off, ok_rows, attn_w, types):
    count = len(xs)
    pieces = flat_list(xs)
    given = len(pieces)
    keys, width = sum(piece.shape[0] for piece in xs[0]), pieces[0].shape[1]
    seg = keys - PRIOR_ROWS
    columns, members, share, wide = attn_w.shape
    cols = wide // 4

    def kernel(*refs):
        gain_ref, bias_ref, off_ref, ok_ref, attn_hbm = refs[given : given + 5]
        outs = refs[given + 5 : given + 5 + 6 * count]
        x_all, weights, mask, sems = refs[given + 5 + 6 * count :]
        x_copies = load_rows(refs[:given], x_all, sems.at[pl.ds(members, given)])
        copies = load_blocks(attn_hbm, weights, sems)
        gain, bias = gain_ref[...], bias_ref[...]
        wait_all(x_copies)
        for index in range(count):
            low_ref = outs[6 * index]

            def norm_rows(block, _):
                start = pl.multiple_of(block * NORM_ROWS, NORM_ROWS)
                values = x_all[pl.ds(index * keys + start, NORM_ROWS), :].astype(F32)
                low_ref[pl.ds(start, NORM_ROWS), :] = norm_apply(values, gain, bias).astype(BF16)
                return _

            lax.fori_loop(0, keys // NORM_ROWS, norm_rows, 0)
        wait_all(copies)
        for index in range(count):
            attend_segment(ok_ref[index : index + 1, :], off_ref, weights, mask, outs[6 * index : 6 * index + 6])

    def attend_segment(ok_row, off_ref, weights, mask, refs):
        low_ref, qkv_ref, lse_ref, mixed_ref, *parts = refs
        row = lax.broadcasted_iota(jnp.int32, (seg, keys), 0)
        col = lax.broadcasted_iota(jnp.int32, (seg, keys), 1)
        mask[...] = jnp.where(jnp.logical_or(col <= row, ok_row > 0.5), 0.0, MASKED)

        value = dot(low_ref[...], rows_of(weights, pl.ds(0, 3 * cols))) + off_ref[...]
        qkv_ref[...] = value.astype(BF16)
        lane = lax.broadcasted_iota(jnp.int32, (seg, PAIR), 1)

        def attend(pair, _):
            query = qkv_ref[:seg, pair_at(0, pair)] * jnp.asarray(HEAD**-0.5, BF16)
            key = qkv_ref[:, pair_at(cols, pair)]
            value = qkv_ref[:, pair_at(2 * cols, pair)]
            merged = None
            for half in range(2):
                inside = in_pair(half, seg)
                scores = dot_t(jnp.where(inside, query, jnp.zeros_like(query)), key) + mask[...]
                row_max = jnp.max(scores, axis=-1, keepdims=True)
                expo = jnp.exp(scores - row_max)
                row_total = jnp.sum(expo, axis=-1, keepdims=True)
                log_total = row_max + jnp.log(row_total)
                lse_ref[...] = jnp.where(lane == 2 * pair + half, log_total, lse_ref[...])
                mixed = dot((expo * (1.0 / row_total)).astype(BF16), value)
                merged = mixed if merged is None else jnp.where(inside, mixed, merged)
            mixed_ref[:, pair_at(0, pair)] = merged.astype(BF16)
            return _

        lse_ref[...] = jnp.zeros_like(lse_ref)
        lax.fori_loop(0, cols // PAIR, attend, 0)

        def project_out(block, _):
            at = pl.ds(pl.multiple_of(block * cols, PAIR), cols)
            weight = block_of(weights, block, pl.ds(3 * cols, cols))
            value = dot(mixed_ref[...], weight)
            for half, part in enumerate(parts):
                part[:, at] = value[half * seg // 2 : (half + 1) * seg // 2].astype(part.dtype)
            return _

        lax.fori_loop(0, members, project_out, 0)

    shapes = []
    for dtype in types:
        shapes += [
            shape_of(keys, width),
            shape_of(keys, 3 * cols),
            shape_of(seg, PAIR, F32),
            shape_of(seg, cols),
            shape_of(seg // 2, width, dtype),
            shape_of(seg // 2, width, dtype),
        ]
    outs = pl.pallas_call(
        kernel,
        out_shape=shapes,
        in_specs=[HBM] * given + [VMEM] * 4 + [HBM],
        out_specs=[VMEM] * len(shapes),
        scratch_shapes=[
            pltpu.VMEM((count * keys, width), BF16),
            pltpu.VMEM((members, columns, share, wide), BF16),
            pltpu.VMEM((seg, keys), F32),
            pltpu.SemaphoreType.DMA((members + given,)),
        ],
        name="attn_forward",
        **kernel_params(12 * count),
    )(*pieces, gain, bias, off, ok_rows, attn_w)
    return [outs[6 * index : 6 * index + 6] for index in range(count)]


def attn_backward(branches, qkvs, lses, ok_cols, attn_w, types):
    count = len(branches)
    pieces = flat_list(branches)
    given = len(pieces)
    seg, width = sum(piece.shape[0] for piece in branches[0]), pieces[0].shape[1]
    keys = qkvs[0].shape[0]
    columns, members, share, wide = attn_w.shape
    cols = wide // 4

    def kernel(*refs):
        ins = refs[given : given + 3 * count]
        attn_hbm = refs[given + 3 * count]
        outs = refs[given + 3 * count + 1 : given + 6 * count + 1]
        branch_all, weights, mask, lse_t, mixed_grad, sems = refs[given + 6 * count + 1 :]
        branch_copies = load_rows(refs[:given], branch_all, sems.at[pl.ds(members, given)])
        copies = load_blocks(attn_hbm, weights, sems)
        wait_all(branch_copies)
        for index in range(count):
            branch = branch_all.at[pl.ds(index * seg, seg)]
            some_in = [ins[index], ins[count + index], ins[2 * count + index]]
            some_out = outs[3 * index : 3 * index + 3]
            waits = copies if index == 0 else []
            back_segment(branch, *some_in, *some_out, weights, mask, lse_t, mixed_grad, waits)

    def back_segment(
        branch_ref, qkv_ref, lse_ref, ok_ref, grads_ref, sums_ref, joined_ref,
        weights, mask, lse_t, mixed_grad, waits,
    ):
        row = lax.broadcasted_iota(jnp.int32, (keys, seg), 0)
        col = lax.broadcasted_iota(jnp.int32, (keys, seg), 1)
        mask[...] = jnp.where(jnp.logical_or(row <= col, ok_ref[:, :1] > 0.5), 0.0, MASKED)
        lse_t[...] = lse_ref[...].T
        grads_ref[seg:, :cols] = jnp.zeros((keys - seg, cols), BF16)
        total = 0.0
        for block in range(members):
            wait_all(waits[block : block + 1])
            weight = block_of(weights, block, pl.ds(3 * cols, cols))
            total = total + dot_t(branch_ref[:, block * cols : (block + 1) * cols], weight)
        mixed_grad[...] = total.astype(BF16)

        def attend(pair, _):
            query = qkv_ref[:seg, pair_at(0, pair)]
            scaled = query * jnp.asarray(HEAD**-0.5, BF16)
            key = qkv_ref[:, pair_at(cols, pair)]
            value = qkv_ref[:, pair_at(2 * cols, pair)]
            mixed = mixed_grad[:, pair_at(0, pair)]
            query_grad = key_grad = value_grad = 0.0
            for half in range(2):
                inside, inside_key = in_pair(half, seg), in_pair(half, keys)
                zero = jnp.zeros_like(query)
                scores = dot_t(key, jnp.where(inside, scaled, zero)) + mask[...]
                probs = jnp.exp(scores - lse_t[pl.ds(2 * pair + half, 1), :])
                mixed_half = jnp.where(inside, mixed, zero)
                prob_grad = dot_t(value, mixed_half)
                value_grad = value_grad + dot(probs.astype(BF16), mixed_half)
                delta = jnp.sum(prob_grad * probs, axis=0, keepdims=True)
                score_grad = (probs * (prob_grad - delta)).astype(BF16)
                key_grad = key_grad + dot(score_grad, jnp.where(inside, query, zero))
                key_half = jnp.where(inside_key, key, jnp.zeros_like(key))
                query_grad = query_grad + t_dot(score_grad, key_half)
            grads_ref[:seg, pair_at(0, pair)] = (query_grad * HEAD**-0.5).astype(BF16)
            grads_ref[:, pair_at(cols, pair)] = (key_grad * HEAD**-0.5).astype(BF16)
            grads_ref[:, pair_at(2 * cols, pair)] = value_grad.astype(BF16)
            return _

        lax.fori_loop(0, cols // PAIR, attend, 0)

        def back(block, _):
            weight = block_of(weights, block, pl.ds(0, 3 * cols))
            at = pl.ds(pl.multiple_of(block * cols, PAIR), cols)
            joined_ref[:, at] = dot_t(grads_ref[...], weight).astype(joined_ref.dtype)
            return _

        lax.fori_loop(0, members, back, 0)
        sums_ref[...] = jnp.sum(grads_ref[...].astype(F32), axis=0, keepdims=True)

    shapes = []
    for dtype in types:
        shapes += [
            shape_of(keys, 3 * cols),
            shape_of(1, 3 * cols, F32),
            shape_of(keys, width, dtype),
        ]
    outs = pl.pallas_call(
        kernel,
        out_shape=shapes,
        in_specs=[HBM] * given + [VMEM] * (3 * count) + [HBM],
        out_specs=[VMEM] * len(shapes),
        scratch_shapes=[
            pltpu.VMEM((count * seg, width), BF16),
            pltpu.VMEM((members, columns, share, wide), BF16),
            pltpu.VMEM((keys, seg), F32),
            pltpu.VMEM((PAIR, seg), F32),
            pltpu.VMEM((seg, cols), BF16),
            pltpu.SemaphoreType.DMA((members + given,)),
        ],
        name="attn_backward",
        **kernel_params(12 * count),
    )(*pieces, *qkvs, *lses, *ok_cols, attn_w)
    return [outs[3 * index : 3 * index + 3] for index in range(count)]


def ffn_hidden(seconds, off, up_w):
    pieces = flat_list(seconds)
    given = len(pieces)
    width = pieces[0].shape[1]
    count = len(seconds)
    seg = sum(piece.shape[0] for piece in pieces) // count
    columns, members, share, wide = up_w.shape
    step = min(1024, wide)

    def kernel(*refs):
        off_ref, up_hbm = refs[given : given + 2]
        outs = refs[given + 2 : given + 2 + 2 * count]
        second, up, sems = refs[given + 2 + 2 * count :]
        copies = load_blocks(up_hbm, up, sems)
        wait_all(copies + load_rows(refs[:given], second, sems.at[pl.ds(members, given)]))

        def hidden(block, _):
            at = pl.ds(pl.multiple_of(block * step, step), step)
            weight = rows_of(up, at)
            for index in range(count):
                pre = dot(second[pl.ds(index * seg, seg), :], weight) + off_ref[:, at]
                square = pre * pre
                bent = jnp.tanh(GELU_A * pre * (1.0 + GELU_B * square))
                gate = 0.5 * (1.0 + bent)
                outs[index][:, at] = (pre * gate).astype(BF16)
                rise = 0.5 * pre * (1.0 - bent * bent) * (GELU_A * (1.0 + 3.0 * GELU_B * square))
                outs[count + index][:, at] = (gate + rise).astype(BF16)
            return _

        lax.fori_loop(0, wide // step, hidden, 0)

    outs = pl.pallas_call(
        kernel,
        out_shape=[shape_of(seg, wide)] * (2 * count),
        in_specs=[HBM] * given + [VMEM, HBM],
        out_specs=[VMEM] * (2 * count),
        scratch_shapes=[
            pltpu.VMEM((count * seg, width), BF16),
            pltpu.VMEM((members, columns, share, wide), BF16),
            pltpu.SemaphoreType.DMA((members + given,)),
        ],
        name="ffn_hidden",
        **kernel_params(6 * count),
    )(*pieces, off, up_w)
    return outs[:count], outs[count:]


def ffn_back(cots, slopes, up_w, down_w, types):
    pieces = flat_list(cots)
    given = len(pieces)
    count = len(slopes)
    seg, width = slopes[0].shape[0], pieces[0].shape[1]
    columns, members, share, wide = up_w.shape
    step = 512
    rows = count * seg
    loads = given + count

    def kernel(*refs):
        up_hbm, down_hbm, pre_ref, sums_ref = refs[loads : loads + 4]
        backs = refs[loads + 4 : loads + 4 + count]
        cot, slope, up, down, sems = refs[loads + 4 + count :]
        first = load_rows(refs[:given], cot, sems)
        first += load_rows([down_hbm], down, sems.at[pl.ds(loads, 1)])
        first += load_rows(refs[given:loads], slope, sems.at[pl.ds(given, count)])
        later = load_blocks(up_hbm, up, sems.at[pl.ds(loads + 1, members)])
        wait_all(first)

        def grad(block, _):
            at = pl.ds(pl.multiple_of(block * step, step), step)
            value = dot_t(cot[...], down[at, :]) * slope[:, at].astype(F32)
            value = value.astype(BF16)
            pre_ref[:, at] = value
            sums_ref[:, at] = jnp.sum(value.astype(F32), axis=0, keepdims=True)
            return _

        lax.fori_loop(0, wide // step, grad, 0)
        wait_all(later)
        deep = columns * share

        def back(block, _):
            at = pl.ds(pl.multiple_of(block * deep, PAIR), deep)
            value = dot_t(pre_ref[...], up[block].reshape(deep, wide))
            for index in range(count):
                backs[index][:, at] = value[index * seg : (index + 1) * seg].astype(types[index])
            return _

        lax.fori_loop(0, members, back, 0)

    return pl.pallas_call(
        kernel,
        out_shape=(
            shape_of(rows, wide),
            shape_of(1, wide, F32),
            *[shape_of(seg, width, dtype) for dtype in types],
        ),
        in_specs=[HBM] * (loads + 2),
        out_specs=(VMEM,) * (2 + count),
        scratch_shapes=[
            pltpu.VMEM((rows, width), BF16),
            pltpu.VMEM((rows, wide), BF16),
            pltpu.VMEM((members, columns, share, wide), BF16),
            pltpu.VMEM((wide, width), BF16),
            pltpu.SemaphoreType.DMA((loads + 1 + members,)),
        ],
        name="ffn_back",
        **kernel_params(10 * count),
    )(*pieces, *slopes, up_w, down_w)


def ffn_out(hiddens, down_w, types):
    count = len(types)
    seg, wide = hiddens[0].shape
    rows = seg // 2
    width = down_w.shape[1]
    step = min(1024, width)

    def kernel(*refs):
        down_ref = refs[count]
        outs = refs[count + 1 : 3 * count + 1]
        hidden, sems = refs[3 * count + 1 :]
        wait_all(load_rows(refs[:count], hidden, sems))

        def block(part, _):
            at = pl.ds(pl.multiple_of(part * step, step), step)
            value = dot(hidden[...], down_ref[:, at])
            for index in range(2 * count):
                half = value[index * rows : (index + 1) * rows]
                outs[index][:, at] = half.astype(types[index // 2])
            return _

        lax.fori_loop(0, width // step, block, 0)

    outs = pl.pallas_call(
        kernel,
        out_shape=[shape_of(rows, width, types[index // 2]) for index in range(2 * count)],
        in_specs=[HBM] * count + [VMEM],
        out_specs=[VMEM] * (2 * count),
        scratch_shapes=[
            pltpu.VMEM((count * seg, wide), BF16),
            pltpu.SemaphoreType.DMA((count,)),
        ],
        name="ffn_out",
        **kernel_params(18),
    )(*hiddens, down_w)
    return [outs[2 * index : 2 * index + 2] for index in range(count)]


def weight_grad(lefts, rights):
    tall, wide = lefts[0].shape[1], rights[0].shape[1]
    deep = sum(left.shape[0] for left in lefts)
    counts = len(lefts), len(rights)
    rows_each = min(512, tall)
    both = sum(counts)

    def kernel(*refs):
        out_ref, left, right, sems = refs[both:]
        step = pl.program_id(0)

        @pl.when(step == 0)
        def _():
            copies = load_rows(refs[: counts[0]], left, sems)
            wait_all(copies + load_rows(refs[counts[0] : both], right, sems.at[pl.ds(counts[0], counts[1])]))

        at = pl.ds(pl.multiple_of(step * rows_each, rows_each), rows_each)
        out_ref[...] = t_dot(left[:, at], right[...]).astype(BF16)

    return pl.pallas_call(
        kernel,
        grid=(tall // rows_each,),
        out_shape=shape_of(tall, wide),
        in_specs=[HBM] * both,
        out_specs=pl.BlockSpec((rows_each, wide), lambda i: (i, 0)),
        scratch_shapes=[
            pltpu.VMEM((deep, tall), BF16),
            pltpu.VMEM((deep, wide), BF16),
            pltpu.SemaphoreType.DMA((both,)),
        ],
        name="weight_grad",
        **kernel_params(17),
    )(*lefts, *rights)


def attn_weight_grad(lows, grads, mixeds, branches):
    lists = lows, grads, mixeds, branches
    width, cols = lows[0].shape[1], mixeds[0].shape[1]
    rows_each = min(512, cols)
    halves = cols // rows_each
    ends = [0]
    for some in lists:
        ends.append(ends[-1] + len(some))

    def kernel(*refs):
        out_ref, low, grad, mixed, branch, sems = refs[ends[-1] :]
        step = pl.program_id(0)

        @pl.when(step == 0)
        def _():
            copies = []
            for first, last, scratch in zip(ends, ends[1:], (low, grad, mixed, branch)):
                copies += load_rows(refs[first:last], scratch, sems.at[pl.ds(first, last - first)])
            wait_all(copies)

        at = pl.ds(pl.multiple_of(step * rows_each, rows_each), rows_each)
        out_ref[:, : 3 * cols] = t_dot(low[:, at], grad[...]).astype(BF16)
        half = pl.ds(pl.multiple_of((step % halves) * rows_each, rows_each), rows_each)
        block = pl.ds(pl.multiple_of((step // halves) * cols, PAIR), cols)
        out_ref[:, 3 * cols :] = t_dot(mixed[:, half], branch[:, block]).astype(BF16)

    return pl.pallas_call(
        kernel,
        grid=(width // rows_each,),
        out_shape=shape_of(width, 4 * cols),
        in_specs=[HBM] * ends[-1],
        out_specs=pl.BlockSpec((rows_each, 4 * cols), lambda i: (i, 0)),
        scratch_shapes=[
            pltpu.VMEM((sum(one.shape[0] for one in some), some[0].shape[1]), BF16)
            for some in lists
        ]
        + [pltpu.SemaphoreType.DMA((ends[-1],))],
        name="attn_weight_grad",
        **kernel_params(21),
    )(*lows, *grads, *mixeds, *branches)


def norm_values(values):
    centre, inverse = norm_parts(values)
    return centre * inverse, inverse


def norm_back(hat, inverse, grad, gain):
    hat_grad = grad * gain
    mean = jnp.mean(hat_grad, axis=-1, keepdims=True)
    along = jnp.mean(hat_grad * hat, axis=-1, keepdims=True)
    return inverse * (hat_grad - mean - hat * along)


def column_sum(value):
    return jnp.sum(value, axis=0, keepdims=True)


def row_blocks(width, last=None, rows=NORM_ROWS):
    if last is None:
        return pl.BlockSpec((rows, width), lambda i: (i, 0))
    return pl.BlockSpec((rows, width), lambda i: (jnp.minimum(i, last), 0))


def store_half(refs, value):
    for half, ref in enumerate(refs):

        @pl.when(pl.program_id(0) == half)
        def _(ref=ref):
            ref[...] = value


def kept(rows, width):
    return pl.BlockSpec((rows, width), lambda i: (0, 0))


def sum_parts(parts):
    total = parts[0][...].astype(F32)
    for part in parts[1:]:
        total = total + part[...].astype(F32)
    return total


def middle_norm(tokens, parts, off, gain, bias):
    seg, width = tokens.shape
    count = len(parts)
    rows = seg // 2
    step = 80

    def kernel(*refs):
        tokens_ref, off_ref, gain_ref, bias_ref, middle_ref, *seconds = refs[2 * count :]
        off, gain, bias = off_ref[...], gain_ref[...], bias_ref[...]
        for half in range(2):

            def body(block, _):
                start = pl.multiple_of(block * step, step)
                at, whole = pl.ds(start, step), pl.ds(half * rows + start, step)
                total = tokens_ref[whole, :].astype(F32)
                for index in range(count):
                    total = total + refs[2 * index + half][at, :].astype(F32)
                total = total + off
                middle_ref[whole, :] = total
                seconds[half][at, :] = norm_apply(total, gain, bias).astype(BF16)
                return _

            lax.fori_loop(0, rows // step, body, 0)

    return pl.pallas_call(
        kernel,
        out_shape=(shape_of(seg, width, F32), shape_of(rows, width), shape_of(rows, width)),
        in_specs=[VMEM] * (2 * count + 4),
        out_specs=(VMEM,) * 3,
        name="middle_norm",
        **kernel_params(5),
    )(*flat_list(parts), tokens, off, gain, bias)


def middle_back(middle, cot, parts, gain):
    seg, width = middle.shape
    count = len(parts)
    rows = seg // 2

    def kernel(*refs):
        middle_ref, cot_ref, gain_ref, grad_ref, top_ref, bottom_ref, sums_ref = refs[count:]

        @pl.when(pl.program_id(0) == 0)
        def _():
            sums_ref[...] = jnp.zeros_like(sums_ref)

        grad = sum_parts(refs[:count])
        hat, inverse = norm_values(middle_ref[...])
        cots = cot_ref[...].astype(F32)
        total = cots + norm_back(hat, inverse, grad, gain_ref[...])
        low = total.astype(BF16)
        grad_ref[...] = total
        store_half([top_ref, bottom_ref], low)
        sums_ref[0:1, :] += column_sum(grad * hat)
        sums_ref[1:2, :] += column_sum(grad)
        sums_ref[2:3, :] += column_sum(low.astype(F32))
        sums_ref[3:4, :] += column_sum(cots)

    return pl.pallas_call(
        kernel,
        grid=(2,),
        out_shape=(
            shape_of(seg, width, F32),
            shape_of(rows, width),
            shape_of(rows, width),
            shape_of(4, width, F32),
        ),
        in_specs=[row_blocks(width, rows=rows)] * (count + 2) + [kept(1, width)],
        out_specs=(
            row_blocks(width, rows=rows),
            kept(rows, width),
            kept(rows, width),
            kept(4, width),
        ),
        name="middle_back",
        **kernel_params(5),
    )(*parts, middle, cot, gain)


def first_back(joined, parts, middle_grad, gain):
    seg, width = middle_grad.shape
    keys = joined.shape[0]
    count = len(parts)
    last = seg // NORM_ROWS - 1

    def kernel(*refs):
        joined_ref, middle_ref, gain_ref, tokens_ref, prior_ref, sums_ref = refs[count:]
        step = pl.program_id(0)

        @pl.when(step == 0)
        def _():
            sums_ref[...] = jnp.zeros_like(sums_ref)

        grad = sum_parts(refs[:count])
        hat, inverse = norm_values(joined_ref[...].astype(F32))
        sums_ref[0:1, :] += column_sum(grad * hat)
        sums_ref[1:2, :] += column_sum(grad)
        back = norm_back(hat, inverse, grad, gain_ref[...])

        @pl.when(step <= last)
        def _():
            tokens_ref[...] = middle_ref[...] + back

        @pl.when(step > last)
        def _():
            prior_ref[...] = back.astype(BF16)

    return pl.pallas_call(
        kernel,
        grid=(keys // NORM_ROWS,),
        out_shape=(
            shape_of(seg, width, F32),
            shape_of(keys - seg, width),
            shape_of(2, width, F32),
        ),
        in_specs=[row_blocks(width)] * (count + 1) + [row_blocks(width, last), kept(1, width)],
        out_specs=(row_blocks(width, last), kept(keys - seg, width), kept(2, width)),
        name="first_back",
        **kernel_params(500_000),
    )(*parts, joined, middle_grad, gain)


def beside_blocks(weights, members):
    rows, width = weights[0].shape
    cols = width // members
    count = len(weights)

    def kernel(*refs):
        out, sems = refs[count:]
        copies = []
        for member in range(members):
            for index in range(count):
                copies.append(
                    pltpu.make_async_copy(
                        refs[index].at[:, pl.ds(member * cols, cols)],
                        out.at[member, :, pl.ds(index * cols, cols)],
                        sems.at[member * count + index],
                    )
                )
        for copy in copies:
            copy.start()
        wait_all(copies)

    return pl.pallas_call(
        kernel,
        out_shape=jax.ShapeDtypeStruct((members, rows, count * cols), BF16),
        in_specs=[HBM] * count,
        out_specs=HBM,
        scratch_shapes=[pltpu.SemaphoreType.DMA((members * count,))],
        name="beside_blocks",
        **kernel_params(1),
    )(*weights)


def swap(value, rel):
    if rel == 0:
        return value
    count = lax.axis_size("fsdp")
    return lax.ppermute(value, "fsdp", [(i, i ^ rel) for i in range(count)])


def halves_of(value):
    rows = value.shape[0] // 2
    return [value[:rows], value[rows:]]


def spread_near(halves):
    near = range(1, min(lax.axis_size("fsdp"), 3))
    return [[swap(half, rel) for half in halves] for rel in near]


def spread_cut(near):
    return [halves_of(near[0][0])[0], halves_of(near[-1][0])[1]]


def spread_far(halves, near, *others, cut=None):
    members = lax.axis_size("fsdp")
    near, cut = lax.optimization_barrier((near, cut, others))[:2]
    pieces = [halves, *near]
    if members > 3:
        top, bottom = near[0][0], near[1][-1]
        if len(halves) == 1:
            top, bottom = cut or spread_cut(near)
        pieces.append([swap(top, 2), swap(bottom, 1)])
    return pieces + [[swap(half, rel) for half in halves] for rel in range(4, members)]


def after(value, *others):
    return lax.optimization_barrier((value, *others))[0]


def add_low(left, right):
    return (left.astype(F32) + right.astype(F32)).astype(BF16)


def output_halves(rel, halves, over, early):
    if over and rel == 2:
        return [add_low(halves[0], over[0]), early[1]], [False, True]
    if over and rel == 1:
        return [early[0], add_low(halves[1], over[1])], [True, False]
    return halves, [False, False]


def trade_blocks(blocks):
    return lax.all_to_all(blocks, "fsdp", 0, 0, tiled=True)


def doubled(rows, axis):
    size = lax.axis_size(axis)
    place = lax.axis_index(axis)
    step = 1
    while step < size:
        came = lax.ppermute(rows, axis, [(i, i ^ step) for i in range(size)])
        high = (place & step) != 0
        rows = jnp.concatenate([jnp.where(high, came, rows), jnp.where(high, rows, came)], 0)
        step *= 2
    return rows


def scatter_small(rows):
    return jnp.sum(lax.all_to_all(rows, BOTH, 0, 0, tiled=True), axis=0)


def gather_dp(value):
    return lax.all_gather(value, "dp", axis=0, tiled=True)


def scatter_dp(value, axis):
    return lax.psum_scatter(value, "dp", scatter_dimension=axis, tiled=True)


def shards(
    tokens,
    summaries,
    presence,
    seg_counts,
    ln1_gain,
    ln1_bias,
    w_query,
    query_bias,
    w_key,
    w_value,
    value_bias,
    w_out,
    out_bias,
    ln2_gain,
    ln2_bias,
    w_up,
    up_bias,
    w_down,
    down_bias,
    cotangent,
):
    members = lax.axis_size("fsdp")
    columns = lax.axis_size("dp")
    total = members * columns
    me = lax.axis_index("fsdp")
    seg_len, width = tokens.shape
    n_summary = summaries.shape[1]
    my_cols = width // members
    my_ff = w_up.shape[1] // members
    row_share = w_query.shape[0]
    rels = list(range(members))
    own_last = rels[::-1]

    def blocks_of(weight):
        return weight.reshape(row_share, members, -1).swapaxes(0, 1)

    def gathered(blocks):
        rows = blocks.reshape(members * row_share, -1)
        return gather_dp(rows).reshape(columns, members, row_share, -1)

    small_parts = (
        ln1_gain, ln1_bias, query_bias, value_bias, out_bias, ln2_gain, ln2_bias, up_bias,
        down_bias, presence[0].astype(BF16),
    )
    packed = doubled(jnp.concatenate(small_parts)[None], "fsdp")
    prior = jnp.pad(summaries[0], ((0, PRIOR_ROWS - n_summary), (0, 0)))
    prior = lax.ppermute(prior, BOTH, [(i, i + 1) for i in range(total - 1)])
    joined = jnp.concatenate([tokens, prior], 0)

    qkv_blocks = beside_blocks([w_query, w_key, w_value], members)
    qkv_blocks = trade_blocks(qkv_blocks)
    up_blocks, packed = lax.optimization_barrier((blocks_of(w_up), packed, qkv_blocks, joined))[:2]
    up_blocks = trade_blocks(up_blocks)
    attn_w = gathered(jnp.concatenate([qkv_blocks, blocks_of(w_out)], 2))
    up_w = gathered(up_blocks)
    down_w = gather_dp(w_down)

    joined_rows = [joined]
    joined_near = spread_near(after(joined_rows, up_blocks))
    group_joined = spread_far(joined_rows, joined_near)
    cot_rows = [cotangent]
    cot_near = spread_near(after(cot_rows, group_joined))
    packed = doubled(packed, "dp").reshape(columns, members, -1).swapaxes(0, 1)
    packed = packed.reshape(total, -1)

    smalls = []
    at = 0
    for part in small_parts:
        smalls.append(packed[:, at : at + part.shape[0]].astype(F32))
        at += part.shape[0]
    gain_one, bias_one, query_off, value_off, out_off, gain_two, bias_two, up_off, down_off = [
        part.reshape(1, -1) for part in smalls[:-1]
    ]
    present_all = smalls[-1]
    query_off = lax.dynamic_slice_in_dim(query_off, me * my_cols, my_cols, 1)
    value_off = lax.dynamic_slice_in_dim(value_off, me * my_cols, my_cols, 1)
    up_off = lax.dynamic_slice_in_dim(up_off, me * my_ff, my_ff, 1)
    qkv_off = jnp.concatenate([query_off, jnp.zeros_like(query_off), value_off], 1)

    starts = jnp.cumsum(seg_counts) - seg_counts
    group_places = (me ^ jnp.arange(members)) * columns + lax.axis_index("dp")
    has_prev = jnp.all(group_places[:, None] != starts[None, :], axis=1)
    summary_ok = jnp.logical_and(present_all[group_places] == 1, has_prev[:, None]).astype(F32)
    ok_rows = jnp.pad(summary_ok, ((0, 0), (seg_len, PRIOR_ROWS - n_summary)))
    ok_cols = jnp.broadcast_to(ok_rows[:, :, None], (*ok_rows.shape, PAIR))


    def part_type(rel):
        return BF16

    attn = {}
    middle_parts = {}
    previous = []
    for some in ([[3], [1, 2], [0]] if members == 4 else [[rel] for rel in own_last]):
        xs = [group_joined[rel] for rel in some]
        xs[0] = [after(xs[0][0], *previous), *xs[0][1:]]
        oks = jnp.concatenate([ok_rows[rel : rel + 1] for rel in some], 0)
        outs = attn_forward(
            xs, gain_one, bias_one, qkv_off, oks, attn_w, [part_type(rel) for rel in some]
        )
        for rel, (low, qkv, lse, mixed, *part) in zip(some, outs):
            attn[rel] = (low, qkv, lse, mixed)
            middle_parts[rel] = part
            previous = [lse]
        if members > 3 and some == [3]:
            over = middle_parts.pop(3)
            middle_over = [swap(over[0], 1), swap(over[1], 2)]
    if members > 3:
        two, one = middle_parts[2], middle_parts[1]
        middle_parts[2] = [add_low(two[0], middle_over[0]), two[1]]
        middle_parts[1] = [one[0], add_low(one[1], middle_over[1])]
    middle_parts = {rel: [swap(half, rel) for half in part] for rel, part in middle_parts.items()}
    cot_cut = spread_cut(cot_near)
    middle, *second_own = middle_norm(
        after(tokens, cot_cut), list(middle_parts.values()), out_off, gain_two, bias_two
    )
    def ordered(values):
        return [values[rel] for rel in own_last]

    second_near = spread_near(second_own)
    hidden_own, slope_own = ffn_hidden([second_own], up_off, up_w)
    group_second = spread_far(second_own, second_near, hidden_own)
    hidden, slope = {0: hidden_own[0]}, {0: slope_own[0]}
    previous = hidden_own
    cuts = [1, members - 1, members] if members > 2 else [1, members]
    for low_rel, high_rel in zip(cuts, cuts[1:]):
        some = rels[low_rel:high_rel]
        seconds = [group_second[rel] for rel in some]
        seconds[0] = [after(seconds[0][0], *previous), *seconds[0][1:]]
        hiddens, slopes = ffn_hidden(seconds, up_off, up_w)
        for rel, one, other in zip(some, hiddens, slopes):
            hidden[rel], slope[rel] = one, other
        previous = hiddens[:1]
        if low_rel == 1:
            group_cot = spread_far(cot_rows, cot_near, previous, cut=cot_cut)
    down_partial = weight_grad(ordered(hidden), flat_list(ordered(group_cot)))
    down_share = scatter_dp(down_partial, 0)
    pre, up_sums, second_parts = [], [], {}
    for some in (own_last[:-1], [0]):
        if not some:
            continue
        cots = [group_cot[rel] for rel in some]
        cots[0] = [after(cots[0][0], *(pre[-1:] or [down_partial])), *cots[0][1:]]
        pre_some, sums, *backs = ffn_back(
            cots, [slope[rel] for rel in some], up_w, down_w, [part_type(rel) for rel in some]
        )
        pre.append(pre_some)
        up_sums.append(sums)
        for rel, back in zip(some, backs):
            second_parts[rel] = swap(back, rel)
    up_partial = weight_grad(flat_list(ordered(group_second)), pre)
    def to_row_blocks(grad):
        return scatter_dp(grad.reshape(members, columns * row_share, -1), 1)

    hiddens = ordered(hidden)
    hiddens[0] = after(hiddens[0], up_partial)
    output_parts = ffn_out(hiddens, down_w, [part_type(rel) for rel in own_last])
    output_parts = dict(zip(own_last, output_parts))
    second_parts = after(second_parts, output_parts)
    up_share = to_row_blocks(after(up_partial, second_parts))
    middle_grad, *branch_low, middle_sums = middle_back(
        middle, cotangent, [second_parts[rel] for rel in rels], gain_two
    )

    branch_near = spread_near(branch_low)
    grads, qkv_sums, joined_parts = {}, {}, {}

    def back_of(some, branches, *others):
        first = [after(branches[0][0], *others), *branches[0][1:]]
        outs = attn_backward(
            [first, *branches[1:]],
            [attn[rel][1] for rel in some],
            [attn[rel][2] for rel in some],
            [ok_cols[rel] for rel in some],
            attn_w,
            [part_type(rel) for rel in some],
        )
        for rel, (grad, sums, part) in zip(some, outs):
            grads[rel], qkv_sums[rel] = grad, sums
            joined_parts[rel] = swap(part, rel)

    back_of([0], [branch_low], down_share)
    group_branch = spread_far(branch_low, branch_near, qkv_sums[0])
    output_over = []
    if members > 3:
        far = after(output_parts.pop(3), qkv_sums[0])
        output_over = [swap(far[0], 1), swap(far[1], 2)]
    last = 0
    for some in ([[1, 2], [3]] if members == 4 else [[rel] for rel in rels[1:]]):
        others = output_over if some == [3] else []
        back_of(some, [group_branch[rel] for rel in some], qkv_sums[last], *others)
        last = some[-1]
    output_early = []
    if members > 3:
        early = after([output_parts[1][0], output_parts[2][1]], qkv_sums[2])
        output_early = [swap(early[0], 1), swap(early[1], 2)]
    attn_partial = attn_weight_grad(
        [attn[rel][0] for rel in rels],
        [grads[rel] for rel in rels],
        [attn[rel][3] for rel in rels],
        flat_list(group_branch),
    )
    joined_parts = after(joined_parts, attn_partial, output_early)
    attn_share = to_row_blocks(after(attn_partial, up_share))
    out_grad = (
        attn_share[:, :, 3 * my_cols :].swapaxes(0, 1).reshape(row_share, width).astype(F32)
    )
    qkv_shares = trade_blocks(attn_share[:, :, : 3 * my_cols])
    query_mat_grad, key_mat_grad, value_mat_grad = [
        qkv_shares[:, :, part * my_cols : (part + 1) * my_cols]
        .swapaxes(0, 1)
        .reshape(row_share, width)
        .astype(F32)
        for part in range(3)
    ]
    tokens_grad, prior_part, first_sums = first_back(
        joined, [joined_parts[rel] for rel in rels], middle_grad, gain_one
    )
    summary_grad = lax.ppermute(
        prior_part[:n_summary], BOTH, [(i + 1, i) for i in range(total - 1)]
    ).astype(F32)
    def whole(value):
        return value.reshape(total, -1)

    def sliced(value):
        mine = value.reshape(columns, -1)
        full = jnp.zeros((total, mine.shape[1]), F32)
        return lax.dynamic_update_slice_in_dim(full, mine, me * columns, 0)

    qkv_sums, middle_sums, up_sums = after((qkv_sums, middle_sums, up_sums), first_sums)
    qkv_sum = sum(qkv_sums[rel] for rel in rels)
    pieces = [
        whole(first_sums[0]),
        whole(first_sums[1]),
        sliced(qkv_sum[:, :my_cols]),
        sliced(qkv_sum[:, 2 * my_cols :]),
        whole(middle_sums[2]),
        whole(middle_sums[0]),
        whole(middle_sums[1]),
        sliced(sum(up_sums)),
        whole(middle_sums[3]),
    ]
    share = scatter_small(jnp.concatenate(pieces, 1))
    up_blocks = trade_blocks(after(up_share, share))
    output_parts = after(output_parts, share)
    output_parts = {
        rel: [half if early else swap(half, rel) for half, early in zip(*halves)]
        for rel, halves in (
            (rel, (output_halves(rel, halves, output_over, output_early)))
            for rel, halves in output_parts.items()
        )
    }
    down_grad = after(down_share, share).astype(F32)
    up_grad = up_blocks.swapaxes(0, 1).reshape(row_share, members * my_ff).astype(F32)
    output_sum = jnp.concatenate(
        [sum(halves[half].astype(F32) for halves in output_parts.values()) for half in range(2)], 0
    )
    output = (middle + output_sum + down_off).astype(BF16)
    outs = []
    at = 0
    for piece in pieces:
        outs.append(share[at : at + piece.shape[1]])
        at += piece.shape[1]
    return (
        output,
        tokens_grad,
        summary_grad[None],
        outs[0],
        outs[1],
        query_mat_grad,
        outs[2],
        key_mat_grad,
        value_mat_grad,
        outs[3],
        out_grad,
        outs[4],
        outs[5],
        outs[6],
        up_grad,
        outs[7],
        down_grad,
        outs[8],
    )


def solution(mesh):
    rows, rows2, rows3 = P(BOTH), P(BOTH, None), P(BOTH, None, None)
    return jax.shard_map(
        shards,
        mesh=mesh,
        in_specs=(
            rows2, rows3, rows2, P(), rows, rows, rows2, rows, rows2, rows2, rows, rows2, rows,
            rows, rows, rows2, rows, rows2, rows, rows2,
        ),
        out_specs=(
            rows2, rows2, rows3, rows, rows, rows2, rows, rows2, rows2, rows, rows2, rows, rows,
            rows, rows2, rows, rows2, rows,
        ),
        check_vma=False,
    )
```

```python
import functools
import jax
import jax.numpy as jnp
from jax import lax
from jax.experimental import pallas as pl
from jax.experimental.pallas import tpu as pltpu
from jax.sharding import PartitionSpec as P

F32, BF16 = jnp.float32, jnp.bfloat16
HEADS = 32
BOTH = ("fsdp", "dp")
HEAD = 64
PAIR = 2 * HEAD
PRIOR_ROWS = 64
NORM_ROWS = 64
MASKED = -1e30
GELU_A, GELU_B = 0.7978845608028654, 0.044715
VMEM_LIMIT = 53 * 1024 * 1024
VMEM = pl.BlockSpec(memory_space=pltpu.VMEM)
HBM = pl.BlockSpec(memory_space=pl.ANY)


def dot(left, right):
    return jnp.dot(left, right, preferred_element_type=F32)


def dot_t(left, right):
    return lax.dot_general(left, right, (((1,), (1,)), ((), ())), preferred_element_type=F32)


def t_dot(left, right):
    return lax.dot_general(left, right, (((0,), (0,)), ((), ())), preferred_element_type=F32)


def norm_parts(values):
    centre = values - jnp.mean(values, axis=-1, keepdims=True)
    spread = jnp.mean(centre * centre, axis=-1, keepdims=True)
    return centre, lax.rsqrt(spread + 1e-05)


def norm_apply(values, norm_gain, norm_bias):
    centre, inverse = norm_parts(values)
    return centre * inverse * norm_gain + norm_bias


def in_pair(half, rows):
    lane = lax.broadcasted_iota(jnp.int32, (rows, PAIR), 1)
    return (lane >= HEAD) if half else (lane < HEAD)


def pair_at(base, pair):
    return pl.ds(pl.multiple_of(base + pair * PAIR, PAIR), PAIR)


def load_blocks(hbm, scratch, sems):
    copies = [
        pltpu.make_async_copy(hbm.at[:, block], scratch.at[block], sems.at[block])
        for block in range(scratch.shape[0])
    ]
    for copy in copies:
        copy.start()
    return copies


def load_rows(parts, scratch, sems):
    copies = []
    at = 0
    for index, part in enumerate(parts):
        rows = part.shape[0]
        copies.append(
            pltpu.make_async_copy(part, scratch.at[pl.ds(at, rows)], sems.at[index])
        )
        at += rows
    for copy in copies:
        copy.start()
    return copies


def flat_list(lists):
    return [piece for some in lists for piece in some]


def wait_all(copies):
    for copy in copies:
        copy.wait()


def rows_of(ref, columns):
    value = ref[:, :, :, columns]
    return value.reshape(-1, value.shape[-1])


def block_of(ref, block, columns):
    value = ref[block, :, :, columns]
    return value.reshape(-1, value.shape[-1])


COST = 1_000_000


def kernel_params(cost):
    return dict(
        compiler_params=pltpu.CompilerParams(vmem_limit_bytes=VMEM_LIMIT),
        cost_estimate=pl.CostEstimate(flops=cost * COST, bytes_accessed=1, transcendentals=0),
    )


def shape_of(rows, columns, dtype=BF16):
    return jax.ShapeDtypeStruct((rows, columns), dtype)


def attn_forward(xs, gain, bias, off, ok_rows, attn_w, types):
    count = len(xs)
    pieces = flat_list(xs)
    given = len(pieces)
    keys, width = sum(piece.shape[0] for piece in xs[0]), pieces[0].shape[1]
    seg = keys - PRIOR_ROWS
    columns, members, share, wide = attn_w.shape
    cols = wide // 4

    def kernel(*refs):
        gain_ref, bias_ref, off_ref, ok_ref, attn_hbm = refs[given : given + 5]
        outs = refs[given + 5 : given + 5 + 6 * count]
        x_all, weights, mask, sems = refs[given + 5 + 6 * count :]
        x_copies = load_rows(refs[:given], x_all, sems.at[pl.ds(members, given)])
        copies = load_blocks(attn_hbm, weights, sems)
        gain, bias = gain_ref[...], bias_ref[...]
        wait_all(x_copies)
        for index in range(count):
            low_ref = outs[6 * index]

            def norm_rows(block, _):
                start = pl.multiple_of(block * NORM_ROWS, NORM_ROWS)
                values = x_all[pl.ds(index * keys + start, NORM_ROWS), :].astype(F32)
                low_ref[pl.ds(start, NORM_ROWS), :] = norm_apply(values, gain, bias).astype(BF16)
                return _

            lax.fori_loop(0, keys // NORM_ROWS, norm_rows, 0)
        wait_all(copies)
        for index in range(count):
            attend_segment(ok_ref[index : index + 1, :], off_ref, weights, mask, outs[6 * index : 6 * index + 6])

    def attend_segment(ok_row, off_ref, weights, mask, refs):
        low_ref, qkv_ref, lse_ref, mixed_ref, *parts = refs
        row = lax.broadcasted_iota(jnp.int32, (seg, keys), 0)
        col = lax.broadcasted_iota(jnp.int32, (seg, keys), 1)
        mask[...] = jnp.where(jnp.logical_or(col <= row, ok_row > 0.5), 0.0, MASKED)

        value = dot(low_ref[...], rows_of(weights, pl.ds(0, 3 * cols))) + off_ref[...]
        qkv_ref[...] = value.astype(BF16)
        lane = lax.broadcasted_iota(jnp.int32, (seg, PAIR), 1)

        def attend(pair, _):
            query = qkv_ref[:seg, pair_at(0, pair)] * jnp.asarray(HEAD**-0.5, BF16)
            key = qkv_ref[:, pair_at(cols, pair)]
            value = qkv_ref[:, pair_at(2 * cols, pair)]
            merged = None
            for half in range(2):
                inside = in_pair(half, seg)
                scores = dot_t(jnp.where(inside, query, jnp.zeros_like(query)), key) + mask[...]
                row_max = jnp.max(scores, axis=-1, keepdims=True)
                expo = jnp.exp(scores - row_max)
                row_total = jnp.sum(expo, axis=-1, keepdims=True)
                log_total = row_max + jnp.log(row_total)
                lse_ref[...] = jnp.where(lane == 2 * pair + half, log_total, lse_ref[...])
                mixed = dot((expo * (1.0 / row_total)).astype(BF16), value)
                merged = mixed if merged is None else jnp.where(inside, mixed, merged)
            mixed_ref[:, pair_at(0, pair)] = merged.astype(BF16)
            return _

        lse_ref[...] = jnp.zeros_like(lse_ref)
        lax.fori_loop(0, cols // PAIR, attend, 0)

        def project_out(block, _):
            at = pl.ds(pl.multiple_of(block * cols, PAIR), cols)
            weight = block_of(weights, block, pl.ds(3 * cols, cols))
            value = dot(mixed_ref[...], weight)
            for half, part in enumerate(parts):
                part[:, at] = value[half * seg // 2 : (half + 1) * seg // 2].astype(part.dtype)
            return _

        lax.fori_loop(0, members, project_out, 0)

    shapes = []
    for dtype in types:
        shapes += [
            shape_of(keys, width),
            shape_of(keys, 3 * cols),
            shape_of(seg, PAIR, F32),
            shape_of(seg, cols),
            shape_of(seg // 2, width, dtype),
            shape_of(seg // 2, width, dtype),
        ]
    outs = pl.pallas_call(
        kernel,
        out_shape=shapes,
        in_specs=[HBM] * given + [VMEM] * 4 + [HBM],
        out_specs=[VMEM] * len(shapes),
        scratch_shapes=[
            pltpu.VMEM((count * keys, width), BF16),
            pltpu.VMEM((members, columns, share, wide), BF16),
            pltpu.VMEM((seg, keys), F32),
            pltpu.SemaphoreType.DMA((members + given,)),
        ],
        name="attn_forward",
        **kernel_params(12 * count),
    )(*pieces, gain, bias, off, ok_rows, attn_w)
    return [outs[6 * index : 6 * index + 6] for index in range(count)]


def attn_backward(branches, qkvs, lses, ok_cols, attn_w, types):
    count = len(branches)
    pieces = flat_list(branches)
    given = len(pieces)
    seg, width = sum(piece.shape[0] for piece in branches[0]), pieces[0].shape[1]
    keys = qkvs[0].shape[0]
    columns, members, share, wide = attn_w.shape
    cols = wide // 4

    def kernel(*refs):
        ins = refs[given : given + 3 * count]
        attn_hbm = refs[given + 3 * count]
        outs = refs[given + 3 * count + 1 : given + 6 * count + 1]
        branch_all, weights, mask, lse_t, mixed_grad, sems = refs[given + 6 * count + 1 :]
        branch_copies = load_rows(refs[:given], branch_all, sems.at[pl.ds(members, given)])
        copies = load_blocks(attn_hbm, weights, sems)
        wait_all(branch_copies)
        for index in range(count):
            branch = branch_all.at[pl.ds(index * seg, seg)]
            some_in = [ins[index], ins[count + index], ins[2 * count + index]]
            some_out = outs[3 * index : 3 * index + 3]
            waits = copies if index == 0 else []
            back_segment(branch, *some_in, *some_out, weights, mask, lse_t, mixed_grad, waits)

    def back_segment(
        branch_ref, qkv_ref, lse_ref, ok_ref, grads_ref, sums_ref, joined_ref,
        weights, mask, lse_t, mixed_grad, waits,
    ):
        row = lax.broadcasted_iota(jnp.int32, (keys, seg), 0)
        col = lax.broadcasted_iota(jnp.int32, (keys, seg), 1)
        mask[...] = jnp.where(jnp.logical_or(row <= col, ok_ref[:, :1] > 0.5), 0.0, MASKED)
        lse_t[...] = lse_ref[...].T
        grads_ref[seg:, :cols] = jnp.zeros((keys - seg, cols), BF16)
        total = 0.0
        for block in range(members):
            wait_all(waits[block : block + 1])
            weight = block_of(weights, block, pl.ds(3 * cols, cols))
            total = total + dot_t(branch_ref[:, block * cols : (block + 1) * cols], weight)
        mixed_grad[...] = total.astype(BF16)

        def attend(pair, _):
            query = qkv_ref[:seg, pair_at(0, pair)]
            scaled = query * jnp.asarray(HEAD**-0.5, BF16)
            key = qkv_ref[:, pair_at(cols, pair)]
            value = qkv_ref[:, pair_at(2 * cols, pair)]
            mixed = mixed_grad[:, pair_at(0, pair)]
            query_grad = key_grad = value_grad = 0.0
            for half in range(2):
                inside, inside_key = in_pair(half, seg), in_pair(half, keys)
                zero = jnp.zeros_like(query)
                scores = dot_t(key, jnp.where(inside, scaled, zero)) + mask[...]
                probs = jnp.exp(scores - lse_t[pl.ds(2 * pair + half, 1), :])
                mixed_half = jnp.where(inside, mixed, zero)
                prob_grad = dot_t(value, mixed_half)
                value_grad = value_grad + dot(probs.astype(BF16), mixed_half)
                delta = jnp.sum(prob_grad * probs, axis=0, keepdims=True)
                score_grad = (probs * (prob_grad - delta)).astype(BF16)
                key_grad = key_grad + dot(score_grad, jnp.where(inside, query, zero))
                key_half = jnp.where(inside_key, key, jnp.zeros_like(key))
                query_grad = query_grad + t_dot(score_grad, key_half)
            grads_ref[:seg, pair_at(0, pair)] = (query_grad * HEAD**-0.5).astype(BF16)
            grads_ref[:, pair_at(cols, pair)] = (key_grad * HEAD**-0.5).astype(BF16)
            grads_ref[:, pair_at(2 * cols, pair)] = value_grad.astype(BF16)
            return _

        lax.fori_loop(0, cols // PAIR, attend, 0)

        def back(block, _):
            weight = block_of(weights, block, pl.ds(0, 3 * cols))
            at = pl.ds(pl.multiple_of(block * cols, PAIR), cols)
            joined_ref[:, at] = dot_t(grads_ref[...], weight).astype(joined_ref.dtype)
            return _

        lax.fori_loop(0, members, back, 0)
        sums_ref[...] = jnp.sum(grads_ref[...].astype(F32), axis=0, keepdims=True)

    shapes = []
    for dtype in types:
        shapes += [
            shape_of(keys, 3 * cols),
            shape_of(1, 3 * cols, F32),
            shape_of(keys, width, dtype),
        ]
    outs = pl.pallas_call(
        kernel,
        out_shape=shapes,
        in_specs=[HBM] * given + [VMEM] * (3 * count) + [HBM],
        out_specs=[VMEM] * len(shapes),
        scratch_shapes=[
            pltpu.VMEM((count * seg, width), BF16),
            pltpu.VMEM((members, columns, share, wide), BF16),
            pltpu.VMEM((keys, seg), F32),
            pltpu.VMEM((PAIR, seg), F32),
            pltpu.VMEM((seg, cols), BF16),
            pltpu.SemaphoreType.DMA((members + given,)),
        ],
        name="attn_backward",
        **kernel_params(12 * count),
    )(*pieces, *qkvs, *lses, *ok_cols, attn_w)
    return [outs[3 * index : 3 * index + 3] for index in range(count)]


def ffn_hidden(seconds, off, up_w):
    pieces = flat_list(seconds)
    given = len(pieces)
    width = pieces[0].shape[1]
    count = len(seconds)
    seg = sum(piece.shape[0] for piece in pieces) // count
    columns, members, share, wide = up_w.shape
    step = min(1024, wide)

    def kernel(*refs):
        off_ref, up_hbm = refs[given : given + 2]
        outs = refs[given + 2 : given + 2 + 2 * count]
        second, up, sems = refs[given + 2 + 2 * count :]
        copies = load_blocks(up_hbm, up, sems)
        wait_all(copies + load_rows(refs[:given], second, sems.at[pl.ds(members, given)]))

        def hidden(block, _):
            at = pl.ds(pl.multiple_of(block * step, step), step)
            weight = rows_of(up, at)
            for index in range(count):
                pre = dot(second[pl.ds(index * seg, seg), :], weight) + off_ref[:, at]
                square = pre * pre
                bent = jnp.tanh(GELU_A * pre * (1.0 + GELU_B * square))
                gate = 0.5 * (1.0 + bent)
                outs[index][:, at] = (pre * gate).astype(BF16)
                rise = 0.5 * pre * (1.0 - bent * bent) * (GELU_A * (1.0 + 3.0 * GELU_B * square))
                outs[count + index][:, at] = (gate + rise).astype(BF16)
            return _

        lax.fori_loop(0, wide // step, hidden, 0)

    outs = pl.pallas_call(
        kernel,
        out_shape=[shape_of(seg, wide)] * (2 * count),
        in_specs=[HBM] * given + [VMEM, HBM],
        out_specs=[VMEM] * (2 * count),
        scratch_shapes=[
            pltpu.VMEM((count * seg, width), BF16),
            pltpu.VMEM((members, columns, share, wide), BF16),
            pltpu.SemaphoreType.DMA((members + given,)),
        ],
        name="ffn_hidden",
        **kernel_params(6 * count),
    )(*pieces, off, up_w)
    return outs[:count], outs[count:]


def ffn_back(cots, slopes, up_w, down_w, types):
    pieces = flat_list(cots)
    given = len(pieces)
    count = len(slopes)
    seg, width = slopes[0].shape[0], pieces[0].shape[1]
    columns, members, share, wide = up_w.shape
    step = wide // 2
    rows = count * seg
    loads = given + count

    def kernel(*refs):
        up_hbm, down_hbm, pre_ref, sums_ref = refs[loads : loads + 4]
        backs = refs[loads + 4 : loads + 4 + count]
        cot, slope, up, down, sems = refs[loads + 4 + count :]
        first = load_rows(refs[:given], cot, sems)
        first += load_rows([down_hbm], down, sems.at[pl.ds(loads, 1)])
        first += load_rows(refs[given:loads], slope, sems.at[pl.ds(given, count)])
        later = load_blocks(up_hbm, up, sems.at[pl.ds(loads + 1, members)])
        wait_all(first)

        def grad(block, _):
            at = pl.ds(pl.multiple_of(block * step, step), step)
            value = dot_t(cot[...], down[at, :]) * slope[:, at].astype(F32)
            value = value.astype(BF16)
            pre_ref[:, at] = value
            sums_ref[:, at] = jnp.sum(value.astype(F32), axis=0, keepdims=True)
            return _

        lax.fori_loop(0, wide // step, grad, 0)
        wait_all(later)
        deep = columns * share

        def back(block, _):
            at = pl.ds(pl.multiple_of(block * deep, PAIR), deep)
            value = dot_t(pre_ref[...], up[block].reshape(deep, wide))
            for index in range(count):
                backs[index][:, at] = value[index * seg : (index + 1) * seg].astype(types[index])
            return _

        lax.fori_loop(0, members, back, 0)

    return pl.pallas_call(
        kernel,
        out_shape=(
            shape_of(rows, wide),
            shape_of(1, wide, F32),
            *[shape_of(seg, width, dtype) for dtype in types],
        ),
        in_specs=[HBM] * (loads + 2),
        out_specs=(VMEM,) * (2 + count),
        scratch_shapes=[
            pltpu.VMEM((rows, width), BF16),
            pltpu.VMEM((rows, wide), BF16),
            pltpu.VMEM((members, columns, share, wide), BF16),
            pltpu.VMEM((wide, width), BF16),
            pltpu.SemaphoreType.DMA((loads + 1 + members,)),
        ],
        name="ffn_back",
        **kernel_params(10 * count),
    )(*pieces, *slopes, up_w, down_w)


def ffn_out(hiddens, down_w, types):
    count = len(types)
    seg, wide = hiddens[0].shape
    rows = seg // 2
    width = down_w.shape[1]
    step = min(1024, width)

    def kernel(*refs):
        down_ref = refs[count]
        outs = refs[count + 1 : 3 * count + 1]
        hidden, sems = refs[3 * count + 1 :]
        wait_all(load_rows(refs[:count], hidden, sems))

        def block(part, _):
            at = pl.ds(pl.multiple_of(part * step, step), step)
            value = dot(hidden[...], down_ref[:, at])
            for index in range(2 * count):
                half = value[index * rows : (index + 1) * rows]
                outs[index][:, at] = half.astype(types[index // 2])
            return _

        lax.fori_loop(0, width // step, block, 0)

    outs = pl.pallas_call(
        kernel,
        out_shape=[shape_of(rows, width, types[index // 2]) for index in range(2 * count)],
        in_specs=[HBM] * count + [VMEM],
        out_specs=[VMEM] * (2 * count),
        scratch_shapes=[
            pltpu.VMEM((count * seg, wide), BF16),
            pltpu.SemaphoreType.DMA((count,)),
        ],
        name="ffn_out",
        **kernel_params(18),
    )(*hiddens, down_w)
    return [outs[2 * index : 2 * index + 2] for index in range(count)]


def weight_grad(lefts, rights):
    tall, wide = lefts[0].shape[1], rights[0].shape[1]
    deep = sum(left.shape[0] for left in lefts)
    counts = len(lefts), len(rights)
    rows_each = min(512, tall)
    both = sum(counts)

    def kernel(*refs):
        out_ref, left, right, sems = refs[both:]
        step = pl.program_id(0)

        @pl.when(step == 0)
        def _():
            copies = load_rows(refs[: counts[0]], left, sems)
            wait_all(copies + load_rows(refs[counts[0] : both], right, sems.at[pl.ds(counts[0], counts[1])]))

        at = pl.ds(pl.multiple_of(step * rows_each, rows_each), rows_each)
        out_ref[...] = t_dot(left[:, at], right[...]).astype(BF16)

    return pl.pallas_call(
        kernel,
        grid=(tall // rows_each,),
        out_shape=shape_of(tall, wide),
        in_specs=[HBM] * both,
        out_specs=pl.BlockSpec((rows_each, wide), lambda i: (i, 0)),
        scratch_shapes=[
            pltpu.VMEM((deep, tall), BF16),
            pltpu.VMEM((deep, wide), BF16),
            pltpu.SemaphoreType.DMA((both,)),
        ],
        name="weight_grad",
        **kernel_params(17),
    )(*lefts, *rights)


def attn_weight_grad(lows, grads, mixeds, branches):
    lists = lows, grads, mixeds, branches
    width, cols = lows[0].shape[1], mixeds[0].shape[1]
    rows_each = min(512, cols)
    halves = cols // rows_each
    ends = [0]
    for some in lists:
        ends.append(ends[-1] + len(some))

    def kernel(*refs):
        out_ref, low, grad, mixed, branch, sems = refs[ends[-1] :]
        step = pl.program_id(0)

        @pl.when(step == 0)
        def _():
            copies = []
            for first, last, scratch in zip(ends, ends[1:], (low, grad, mixed, branch)):
                copies += load_rows(refs[first:last], scratch, sems.at[pl.ds(first, last - first)])
            wait_all(copies)

        at = pl.ds(pl.multiple_of(step * rows_each, rows_each), rows_each)
        out_ref[:, : 3 * cols] = t_dot(low[:, at], grad[...]).astype(BF16)
        half = pl.ds(pl.multiple_of((step % halves) * rows_each, rows_each), rows_each)
        block = pl.ds(pl.multiple_of((step // halves) * cols, PAIR), cols)
        out_ref[:, 3 * cols :] = t_dot(mixed[:, half], branch[:, block]).astype(BF16)

    return pl.pallas_call(
        kernel,
        grid=(width // rows_each,),
        out_shape=shape_of(width, 4 * cols),
        in_specs=[HBM] * ends[-1],
        out_specs=pl.BlockSpec((rows_each, 4 * cols), lambda i: (i, 0)),
        scratch_shapes=[
            pltpu.VMEM((sum(one.shape[0] for one in some), some[0].shape[1]), BF16)
            for some in lists
        ]
        + [pltpu.SemaphoreType.DMA((ends[-1],))],
        name="attn_weight_grad",
        **kernel_params(21),
    )(*lows, *grads, *mixeds, *branches)


def norm_values(values):
    centre, inverse = norm_parts(values)
    return centre * inverse, inverse


def norm_back(hat, inverse, grad, gain):
    hat_grad = grad * gain
    mean = jnp.mean(hat_grad, axis=-1, keepdims=True)
    along = jnp.mean(hat_grad * hat, axis=-1, keepdims=True)
    return inverse * (hat_grad - mean - hat * along)


def column_sum(value):
    return jnp.sum(value, axis=0, keepdims=True)


def row_blocks(width, last=None, rows=NORM_ROWS):
    if last is None:
        return pl.BlockSpec((rows, width), lambda i: (i, 0))
    return pl.BlockSpec((rows, width), lambda i: (jnp.minimum(i, last), 0))


def store_half(refs, value):
    for half, ref in enumerate(refs):

        @pl.when(pl.program_id(0) == half)
        def _(ref=ref):
            ref[...] = value


def kept(rows, width):
    return pl.BlockSpec((rows, width), lambda i: (0, 0))


def sum_parts(parts):
    total = parts[0][...].astype(F32)
    for part in parts[1:]:
        total = total + part[...].astype(F32)
    return total


def middle_norm(tokens, parts, off, gain, bias):
    seg, width = tokens.shape
    count = len(parts)
    rows = seg // 2
    step = 80

    def kernel(*refs):
        tokens_ref, off_ref, gain_ref, bias_ref, middle_ref, *seconds = refs[2 * count :]
        off, gain, bias = off_ref[...], gain_ref[...], bias_ref[...]
        for half in range(2):

            def body(block, _):
                start = pl.multiple_of(block * step, step)
                at, whole = pl.ds(start, step), pl.ds(half * rows + start, step)
                total = tokens_ref[whole, :].astype(F32)
                for index in range(count):
                    total = total + refs[2 * index + half][at, :].astype(F32)
                total = total + off
                middle_ref[whole, :] = total
                seconds[half][at, :] = norm_apply(total, gain, bias).astype(BF16)
                return _

            lax.fori_loop(0, rows // step, body, 0)

    return pl.pallas_call(
        kernel,
        out_shape=(shape_of(seg, width, F32), shape_of(rows, width), shape_of(rows, width)),
        in_specs=[VMEM] * (2 * count + 4),
        out_specs=(VMEM,) * 3,
        name="middle_norm",
        **kernel_params(5),
    )(*flat_list(parts), tokens, off, gain, bias)


def middle_back(middle, cot, parts, gain):
    seg, width = middle.shape
    count = len(parts)
    rows = seg // 2

    def kernel(*refs):
        middle_ref, cot_ref, gain_ref, grad_ref, top_ref, bottom_ref, sums_ref = refs[count:]

        @pl.when(pl.program_id(0) == 0)
        def _():
            sums_ref[...] = jnp.zeros_like(sums_ref)

        grad = sum_parts(refs[:count])
        hat, inverse = norm_values(middle_ref[...])
        cots = cot_ref[...].astype(F32)
        total = cots + norm_back(hat, inverse, grad, gain_ref[...])
        low = total.astype(BF16)
        grad_ref[...] = total
        store_half([top_ref, bottom_ref], low)
        sums_ref[0:1, :] += column_sum(grad * hat)
        sums_ref[1:2, :] += column_sum(grad)
        sums_ref[2:3, :] += column_sum(low.astype(F32))
        sums_ref[3:4, :] += column_sum(cots)

    return pl.pallas_call(
        kernel,
        grid=(2,),
        out_shape=(
            shape_of(seg, width, F32),
            shape_of(rows, width),
            shape_of(rows, width),
            shape_of(4, width, F32),
        ),
        in_specs=[row_blocks(width, rows=rows)] * (count + 2) + [kept(1, width)],
        out_specs=(
            row_blocks(width, rows=rows),
            kept(rows, width),
            kept(rows, width),
            kept(4, width),
        ),
        name="middle_back",
        **kernel_params(5),
    )(*parts, middle, cot, gain)


def first_back(joined, parts, middle_grad, gain):
    seg, width = middle_grad.shape
    keys = joined.shape[0]
    count = len(parts)
    last = seg // NORM_ROWS - 1

    def kernel(*refs):
        joined_ref, middle_ref, gain_ref, tokens_ref, prior_ref, sums_ref = refs[count:]
        step = pl.program_id(0)

        @pl.when(step == 0)
        def _():
            sums_ref[...] = jnp.zeros_like(sums_ref)

        grad = sum_parts(refs[:count])
        hat, inverse = norm_values(joined_ref[...].astype(F32))
        sums_ref[0:1, :] += column_sum(grad * hat)
        sums_ref[1:2, :] += column_sum(grad)
        back = norm_back(hat, inverse, grad, gain_ref[...])

        @pl.when(step <= last)
        def _():
            tokens_ref[...] = middle_ref[...] + back

        @pl.when(step > last)
        def _():
            prior_ref[...] = back.astype(BF16)

    return pl.pallas_call(
        kernel,
        grid=(keys // NORM_ROWS,),
        out_shape=(
            shape_of(seg, width, F32),
            shape_of(keys - seg, width),
            shape_of(2, width, F32),
        ),
        in_specs=[row_blocks(width)] * (count + 1) + [row_blocks(width, last), kept(1, width)],
        out_specs=(row_blocks(width, last), kept(keys - seg, width), kept(2, width)),
        name="first_back",
        **kernel_params(500_000),
    )(*parts, joined, middle_grad, gain)


def beside_blocks(weights, members):
    rows, width = weights[0].shape
    cols = width // members
    count = len(weights)

    def kernel(*refs):
        out, sems = refs[count:]
        copies = []
        for member in range(members):
            for index in range(count):
                copies.append(
                    pltpu.make_async_copy(
                        refs[index].at[:, pl.ds(member * cols, cols)],
                        out.at[member, :, pl.ds(index * cols, cols)],
                        sems.at[member * count + index],
                    )
                )
        for copy in copies:
            copy.start()
        wait_all(copies)

    return pl.pallas_call(
        kernel,
        out_shape=jax.ShapeDtypeStruct((members, rows, count * cols), BF16),
        in_specs=[HBM] * count,
        out_specs=HBM,
        scratch_shapes=[pltpu.SemaphoreType.DMA((members * count,))],
        name="beside_blocks",
        **kernel_params(1),
    )(*weights)


def swap(value, rel):
    if rel == 0:
        return value
    count = lax.axis_size("fsdp")
    return lax.ppermute(value, "fsdp", [(i, i ^ rel) for i in range(count)])


def halves_of(value):
    rows = value.shape[0] // 2
    return [value[:rows], value[rows:]]


def spread_near(halves):
    near = range(1, min(lax.axis_size("fsdp"), 3))
    return [[swap(half, rel) for half in halves] for rel in near]


def spread_cut(near):
    return [halves_of(near[0][0])[0], halves_of(near[-1][0])[1]]


def spread_far(halves, near, *others, cut=None):
    members = lax.axis_size("fsdp")
    near, cut = lax.optimization_barrier((near, cut, others))[:2]
    pieces = [halves, *near]
    if members > 3:
        top, bottom = near[0][0], near[1][-1]
        if len(halves) == 1:
            top, bottom = cut or spread_cut(near)
        pieces.append([swap(top, 2), swap(bottom, 1)])
    return pieces + [[swap(half, rel) for half in halves] for rel in range(4, members)]


def after(value, *others):
    return lax.optimization_barrier((value, *others))[0]


def add_low(left, right):
    return (left.astype(F32) + right.astype(F32)).astype(BF16)


def output_halves(rel, halves, over, early):
    if over and rel == 2:
        return [add_low(halves[0], over[0]), early[1]], [False, True]
    if over and rel == 1:
        return [early[0], add_low(halves[1], over[1])], [True, False]
    return halves, [False, False]


def trade_blocks(blocks):
    return lax.all_to_all(blocks, "fsdp", 0, 0, tiled=True)


def doubled(rows, axis):
    size = lax.axis_size(axis)
    place = lax.axis_index(axis)
    step = 1
    while step < size:
        came = lax.ppermute(rows, axis, [(i, i ^ step) for i in range(size)])
        high = (place & step) != 0
        rows = jnp.concatenate([jnp.where(high, came, rows), jnp.where(high, rows, came)], 0)
        step *= 2
    return rows


def scatter_small(rows):
    return jnp.sum(lax.all_to_all(rows, BOTH, 0, 0, tiled=True), axis=0)


def gather_dp(value):
    return lax.all_gather(value, "dp", axis=0, tiled=True)


def scatter_dp(value, axis):
    return lax.psum_scatter(value, "dp", scatter_dimension=axis, tiled=True)


def shards(
    tokens,
    summaries,
    presence,
    seg_counts,
    ln1_gain,
    ln1_bias,
    w_query,
    query_bias,
    w_key,
    w_value,
    value_bias,
    w_out,
    out_bias,
    ln2_gain,
    ln2_bias,
    w_up,
    up_bias,
    w_down,
    down_bias,
    cotangent,
):
    members = lax.axis_size("fsdp")
    columns = lax.axis_size("dp")
    total = members * columns
    me = lax.axis_index("fsdp")
    seg_len, width = tokens.shape
    n_summary = summaries.shape[1]
    my_cols = width // members
    my_ff = w_up.shape[1] // members
    row_share = w_query.shape[0]
    rels = list(range(members))
    own_last = rels[::-1]

    def blocks_of(weight):
        return weight.reshape(row_share, members, -1).swapaxes(0, 1)

    def gathered(blocks):
        rows = blocks.reshape(members * row_share, -1)
        return gather_dp(rows).reshape(columns, members, row_share, -1)

    small_parts = (
        ln1_gain, ln1_bias, query_bias, value_bias, out_bias, ln2_gain, ln2_bias, up_bias,
        down_bias, presence[0].astype(BF16),
    )
    packed = doubled(jnp.concatenate(small_parts)[None], "fsdp")
    prior = jnp.pad(summaries[0], ((0, PRIOR_ROWS - n_summary), (0, 0)))
    prior = lax.ppermute(prior, BOTH, [(i, i + 1) for i in range(total - 1)])
    joined = jnp.concatenate([tokens, prior], 0)

    qkv_blocks = beside_blocks([w_query, w_key, w_value], members)
    qkv_blocks = trade_blocks(qkv_blocks)
    up_blocks, packed = lax.optimization_barrier((blocks_of(w_up), packed, qkv_blocks, joined))[:2]
    up_blocks = trade_blocks(up_blocks)
    attn_w = gathered(jnp.concatenate([qkv_blocks, blocks_of(w_out)], 2))
    up_w = gathered(up_blocks)
    down_w = gather_dp(w_down)

    joined_rows = [joined]
    joined_near = spread_near(after(joined_rows, up_blocks))
    group_joined = spread_far(joined_rows, joined_near)
    cot_rows = [cotangent]
    cot_near = spread_near(after(cot_rows, group_joined))
    packed = doubled(packed, "dp").reshape(columns, members, -1).swapaxes(0, 1)
    packed = packed.reshape(total, -1)

    smalls = []
    at = 0
    for part in small_parts:
        smalls.append(packed[:, at : at + part.shape[0]].astype(F32))
        at += part.shape[0]
    gain_one, bias_one, query_off, value_off, out_off, gain_two, bias_two, up_off, down_off = [
        part.reshape(1, -1) for part in smalls[:-1]
    ]
    present_all = smalls[-1]
    query_off = lax.dynamic_slice_in_dim(query_off, me * my_cols, my_cols, 1)
    value_off = lax.dynamic_slice_in_dim(value_off, me * my_cols, my_cols, 1)
    up_off = lax.dynamic_slice_in_dim(up_off, me * my_ff, my_ff, 1)
    qkv_off = jnp.concatenate([query_off, jnp.zeros_like(query_off), value_off], 1)

    starts = jnp.cumsum(seg_counts) - seg_counts
    group_places = (me ^ jnp.arange(members)) * columns + lax.axis_index("dp")
    has_prev = jnp.all(group_places[:, None] != starts[None, :], axis=1)
    summary_ok = jnp.logical_and(present_all[group_places] == 1, has_prev[:, None]).astype(F32)
    ok_rows = jnp.pad(summary_ok, ((0, 0), (seg_len, PRIOR_ROWS - n_summary)))
    ok_cols = jnp.broadcast_to(ok_rows[:, :, None], (*ok_rows.shape, PAIR))


    def part_type(rel):
        return BF16

    attn = {}
    middle_parts = {}
    previous = []
    for some in ([[3], [1, 2], [0]] if members == 4 else [[rel] for rel in own_last]):
        xs = [group_joined[rel] for rel in some]
        xs[0] = [after(xs[0][0], *previous), *xs[0][1:]]
        oks = jnp.concatenate([ok_rows[rel : rel + 1] for rel in some], 0)
        outs = attn_forward(
            xs, gain_one, bias_one, qkv_off, oks, attn_w, [part_type(rel) for rel in some]
        )
        for rel, (low, qkv, lse, mixed, *part) in zip(some, outs):
            attn[rel] = (low, qkv, lse, mixed)
            middle_parts[rel] = part
            previous = [lse]
        if members > 3 and some == [3]:
            over = middle_parts.pop(3)
            middle_over = [swap(over[0], 1), swap(over[1], 2)]
    if members > 3:
        two, one = middle_parts[2], middle_parts[1]
        middle_parts[2] = [add_low(two[0], middle_over[0]), two[1]]
        middle_parts[1] = [one[0], add_low(one[1], middle_over[1])]
    middle_parts = {rel: [swap(half, rel) for half in part] for rel, part in middle_parts.items()}
    cot_cut = spread_cut(cot_near)
    middle, *second_own = middle_norm(
        after(tokens, cot_cut), list(middle_parts.values()), out_off, gain_two, bias_two
    )
    def ordered(values):
        return [values[rel] for rel in own_last]

    second_near = spread_near(second_own)
    hidden_own, slope_own = ffn_hidden([second_own], up_off, up_w)
    group_second = spread_far(second_own, second_near, hidden_own)
    hidden, slope = {0: hidden_own[0]}, {0: slope_own[0]}
    previous = hidden_own
    cuts = [1, members - 1, members] if members > 2 else [1, members]
    for low_rel, high_rel in zip(cuts, cuts[1:]):
        some = rels[low_rel:high_rel]
        seconds = [group_second[rel] for rel in some]
        seconds[0] = [after(seconds[0][0], *previous), *seconds[0][1:]]
        hiddens, slopes = ffn_hidden(seconds, up_off, up_w)
        for rel, one, other in zip(some, hiddens, slopes):
            hidden[rel], slope[rel] = one, other
        previous = hiddens[:1]
        if low_rel == 1:
            group_cot = spread_far(cot_rows, cot_near, previous, cut=cot_cut)
    down_partial = weight_grad(ordered(hidden), flat_list(ordered(group_cot)))
    down_share = scatter_dp(down_partial, 0)
    pre, up_sums, second_parts = [], [], {}
    for some in (own_last[:-1], [0]):
        if not some:
            continue
        cots = [group_cot[rel] for rel in some]
        cots[0] = [after(cots[0][0], *(pre[-1:] or [down_partial])), *cots[0][1:]]
        pre_some, sums, *backs = ffn_back(
            cots, [slope[rel] for rel in some], up_w, down_w, [part_type(rel) for rel in some]
        )
        pre.append(pre_some)
        up_sums.append(sums)
        for rel, back in zip(some, backs):
            second_parts[rel] = swap(back, rel)
    up_partial = weight_grad(flat_list(ordered(group_second)), pre)
    def to_row_blocks(grad):
        return scatter_dp(grad.reshape(members, columns * row_share, -1), 1)

    hiddens = ordered(hidden)
    hiddens[0] = after(hiddens[0], up_partial)
    output_parts = ffn_out(hiddens, down_w, [part_type(rel) for rel in own_last])
    output_parts = dict(zip(own_last, output_parts))
    second_parts = after(second_parts, output_parts)
    up_share = to_row_blocks(after(up_partial, second_parts))
    middle_grad, *branch_low, middle_sums = middle_back(
        middle, cotangent, [second_parts[rel] for rel in rels], gain_two
    )

    branch_near = spread_near(branch_low)
    grads, qkv_sums, joined_parts = {}, {}, {}

    def back_of(some, branches, *others):
        first = [after(branches[0][0], *others), *branches[0][1:]]
        outs = attn_backward(
            [first, *branches[1:]],
            [attn[rel][1] for rel in some],
            [attn[rel][2] for rel in some],
            [ok_cols[rel] for rel in some],
            attn_w,
            [part_type(rel) for rel in some],
        )
        for rel, (grad, sums, part) in zip(some, outs):
            grads[rel], qkv_sums[rel] = grad, sums
            joined_parts[rel] = swap(part, rel)

    back_of([0], [branch_low], down_share)
    group_branch = spread_far(branch_low, branch_near, qkv_sums[0])
    output_over = []
    if members > 3:
        far = after(output_parts.pop(3), qkv_sums[0])
        output_over = [swap(far[0], 1), swap(far[1], 2)]
    last = 0
    for some in ([[1, 2], [3]] if members == 4 else [[rel] for rel in rels[1:]]):
        others = output_over if some == [3] else []
        back_of(some, [group_branch[rel] for rel in some], qkv_sums[last], *others)
        last = some[-1]
    output_early = []
    if members > 3:
        early = after([output_parts[1][0], output_parts[2][1]], qkv_sums[2])
        output_early = [swap(early[0], 1), swap(early[1], 2)]
    attn_partial = attn_weight_grad(
        [attn[rel][0] for rel in rels],
        [grads[rel] for rel in rels],
        [attn[rel][3] for rel in rels],
        flat_list(group_branch),
    )
    joined_parts = after(joined_parts, attn_partial, output_early)
    attn_share = to_row_blocks(after(attn_partial, up_share))
    out_grad = (
        attn_share[:, :, 3 * my_cols :].swapaxes(0, 1).reshape(row_share, width).astype(F32)
    )
    qkv_shares = trade_blocks(attn_share[:, :, : 3 * my_cols])
    query_mat_grad, key_mat_grad, value_mat_grad = [
        qkv_shares[:, :, part * my_cols : (part + 1) * my_cols]
        .swapaxes(0, 1)
        .reshape(row_share, width)
        .astype(F32)
        for part in range(3)
    ]
    tokens_grad, prior_part, first_sums = first_back(
        joined, [joined_parts[rel] for rel in rels], middle_grad, gain_one
    )
    summary_grad = lax.ppermute(
        prior_part[:n_summary], BOTH, [(i + 1, i) for i in range(total - 1)]
    ).astype(F32)
    def whole(value):
        return value.reshape(total, -1)

    def sliced(value):
        mine = value.reshape(columns, -1)
        full = jnp.zeros((total, mine.shape[1]), F32)
        return lax.dynamic_update_slice_in_dim(full, mine, me * columns, 0)

    qkv_sums, middle_sums, up_sums = after((qkv_sums, middle_sums, up_sums), first_sums)
    qkv_sum = sum(qkv_sums[rel] for rel in rels)
    pieces = [
        whole(first_sums[0]),
        whole(first_sums[1]),
        sliced(qkv_sum[:, :my_cols]),
        sliced(qkv_sum[:, 2 * my_cols :]),
        whole(middle_sums[2]),
        whole(middle_sums[0]),
        whole(middle_sums[1]),
        sliced(sum(up_sums)),
        whole(middle_sums[3]),
    ]
    share = scatter_small(jnp.concatenate(pieces, 1))
    up_blocks = trade_blocks(after(up_share, share))
    output_parts = after(output_parts, share)
    output_parts = {
        rel: [half if early else swap(half, rel) for half, early in zip(*halves)]
        for rel, halves in (
            (rel, (output_halves(rel, halves, output_over, output_early)))
            for rel, halves in output_parts.items()
        )
    }
    down_grad = after(down_share, share).astype(F32)
    up_grad = up_blocks.swapaxes(0, 1).reshape(row_share, members * my_ff).astype(F32)
    output_sum = jnp.concatenate(
        [sum(halves[half].astype(F32) for halves in output_parts.values()) for half in range(2)], 0
    )
    output = (middle + output_sum + down_off).astype(BF16)
    outs = []
    at = 0
    for piece in pieces:
        outs.append(share[at : at + piece.shape[1]])
        at += piece.shape[1]
    return (
        output,
        tokens_grad,
        summary_grad[None],
        outs[0],
        outs[1],
        query_mat_grad,
        outs[2],
        key_mat_grad,
        value_mat_grad,
        outs[3],
        out_grad,
        outs[4],
        outs[5],
        outs[6],
        up_grad,
        outs[7],
        down_grad,
        outs[8],
    )


def solution(mesh):
    rows, rows2, rows3 = P(BOTH), P(BOTH, None), P(BOTH, None, None)
    return jax.shard_map(
        shards,
        mesh=mesh,
        in_specs=(
            rows2, rows3, rows2, P(), rows, rows, rows2, rows, rows2, rows2, rows, rows2, rows,
            rows, rows, rows2, rows, rows2, rows, rows2,
        ),
        out_specs=(
            rows2, rows2, rows3, rows, rows, rows2, rows, rows2, rows2, rows, rows2, rows, rows,
            rows, rows2, rows, rows2, rows,
        ),
        check_vma=False,
    )
```
